32 devices in a mesh: az: 4 (over x, core), curve: 8 (over z, y).
Axes of the slice: x: 2, y: 2, z: 4, core: 2. Of those that a mesh axis runs over, the one named last changes fastest.
Arguments:
- fields: float32 [2, 256, 16, 1024], P(None, 'az', None, 'curve'), may hold values from -6 to 6
- impedance: float32 [2, 256, 1024], P(None, 'az', 'curve'), may hold values from 0.25 to 1.5
- tile_data: bfloat16 [256, 8, 3, 2, 128, 128], P('az', 'curve'), may hold values from -0.21875 to 0.21875
- tile_cols: int32 [256, 8, 3], P('az', 'curve'), may hold values from 0 to 7, as said below
- tile_count: int32 [256, 8], P('az', 'curve'), may hold values from 1 to 3
Outputs:
- applied: float32 [2, 256, 16, 1024], P(None, 'az', None, 'curve')
The draws below stay inside these ranges and needn't reach their ends.
Inputs may be any that keep to these rules, and one draw needn't show every extreme that they name: `tile_cols`: for every mode and block row the 3 entries are distinct blocks lying within one block of the row's own block along the closed curve, indices taken modulo 8; only the first tile_count entries are used.
All inputs are finite; a program needn't handle non-finite values.
Results may differ from the reference program's by a relative error of at most 0.0021.
Values may be sent and summed in bfloat16 or wider, within the bound.
No kernel may reach another device: no remote copies, remote signals or barrier semaphores. Data moves between devices by JAX's collectives and lax.ppermute only.
A program may use at most 64 MiB of HBM per device.

```python
import jax
import jax.numpy as jnp
from jax import lax

NPHI = 256
RHS = 16
BLK = 128
TILES = 3
MODES = 256
NBLK = 8
NODES = 1024


def pattern_draw(key):
    base_key = jax.random.fold_in(key, 7)
    key_cols, key_count = jax.random.split(base_key)
    scores = jax.random.randint(key_cols, (MODES, NBLK, TILES), 0, 1 << 20) * TILES + jnp.arange(TILES, dtype=jnp.int32)
    ranking = jnp.argsort(scores, axis=-1, stable=True).astype(jnp.int32)
    block_rows = jnp.arange(NBLK, dtype=jnp.int32)[None, :, None]
    columns = jnp.mod(block_rows + ranking - 1, NBLK).astype(jnp.int32)
    counts = jax.random.randint(key_count, (MODES, NBLK), 1, TILES + 1).astype(jnp.int32)
    counts = counts.at[0, 0].set(TILES).at[0, 1].set(1)
    return (columns, counts)


def draw_tile_cols(key, part):
    return pattern_draw(key)[0]


def draw_tile_count(key, part):
    return pattern_draw(key)[1]


def block_levels(rng, shape, shards, least, high):
    factor_of, own = 1.0, jax.random.fold_in(rng, 6)
    for dim, blocks in shards:
        draws = jnp.exp(jax.random.uniform(jax.random.fold_in(own, dim), (blocks,), jnp.float32, least / len(shards), high / len(shards)))
        factor_of = factor_of * jnp.repeat(draws, shape[dim] // blocks).reshape([-1 if axis == dim else 1 for axis in range(len(shape))])
    return factor_of


def centred(stream_key, extent, scale, most, cuts=(), held_as=jnp.bfloat16):
    values = scale * jax.random.normal(stream_key, extent, jnp.float32)
    if cuts:
        values = values * block_levels(stream_key, extent, cuts, -0.22, 0.18)
    return jnp.clip(values, -most, most).astype(held_as)


def setup_inputs(seed: int = 0) -> dict:
    splits = jax.random.split(jax.random.key(seed), 6)
    fields = centred(splits[0], (2, NPHI, RHS, NODES), 1.0, 6.0, ((1, 4), (3, 8)), jnp.float32)
    impedance = jnp.clip(0.25 + 1.25 * jax.random.uniform(splits[1], (2, NPHI, NODES), jnp.float32) ** block_levels(splits[1], (2, NPHI, NODES), ((1, 4), (2, 8)), -0.2, 0.2), 0.25, 1.5)
    tile_data = centred(splits[2], (MODES, NBLK, TILES, 2, BLK, BLK), (6 * BLK) ** -0.5, 0.21875, ((0, 4), (1, 8)))
    tile_cols = draw_tile_cols(jax.random.fold_in(splits[5], 71), 0)
    tile_count = draw_tile_count(jax.random.fold_in(splits[5], 71), 0)
    return dict(fields=fields, impedance=impedance, tile_data=tile_data, tile_cols=tile_cols, tile_count=tile_count)


def reference(fields, impedance, tile_data, tile_cols, tile_count):
    period = fields.shape[1]
    rhs_count = fields.shape[2]
    node_count = fields.shape[3]
    block_size = tile_data.shape[-1]
    block_total = node_count // block_size
    slot_count = tile_data.shape[2]
    signal = fields[0] + 1j * fields[1]
    spectrum = jnp.fft.fft(signal, axis=0) / period
    mode_values = jnp.stack([jnp.real(spectrum), jnp.imag(spectrum)]).astype(jnp.bfloat16)
    blocked = jnp.transpose(mode_values.reshape(2, period, rhs_count, block_total, block_size), (1, 0, 2, 3, 4))

    def one_mode(inputs):
        vectors, matrices, columns, counts = inputs
        picked = vectors[:, :, columns, :].astype(jnp.float32)
        live_slots = (jnp.arange(slot_count, dtype=jnp.int32)[None, :] < counts[:, None]).astype(jnp.float32)
        picked = picked * live_slots[None, None, :, :, None]
        matrices = matrices.astype(jnp.float32)
        tile_real = matrices[:, :, 0]
        tile_imag = matrices[:, :, 1]

        def tile_apply(mat, vals):
            return jnp.einsum("btpq,rbtq->rbp", mat, vals)

        near_real = tile_apply(tile_real, picked[0]) - tile_apply(tile_imag, picked[1])
        near_imag = tile_apply(tile_real, picked[1]) + tile_apply(tile_imag, picked[0])
        return jnp.stack([near_real, near_imag])

    near = lax.map(one_mode, (blocked, tile_data, tile_cols, tile_count))
    near = near.reshape(period, 2, rhs_count, node_count)
    near_complex = near[:, 0] + 1j * near[:, 1]
    returned = jnp.fft.ifft(near_complex, axis=0) * period
    back_real = jnp.real(returned).astype(jnp.float32)
    back_imag = jnp.imag(returned).astype(jnp.float32)
    imped_real = impedance[0][:, None, :]
    imped_imag = impedance[1][:, None, :]
    out_real = fields[0] + imped_real * back_real - imped_imag * back_imag
    out_imag = fields[1] + imped_real * back_imag + imped_imag * back_real
    return jnp.stack([out_real, out_imag]).astype(jnp.float32)
```

```python
import functools

import jax
import jax.numpy as jnp
import numpy as np
from jax import lax
from jax.experimental import pallas as pl
from jax.experimental.pallas import tpu as pltpu
from jax.sharding import PartitionSpec as P

CHUNKS = 2
FIELD_BOUND = 6.0
CODE_TOP = 32767.0
VMEM_LIMIT = 40 * 1024 * 1024


def dft_tables(parts, local, order, inverse):
    period = parts * local
    own = np.arange(local)
    tables = np.zeros((parts, 2 * local, parts * 2 * local), np.float64)
    for a in range(parts):
        rows = a * local + own
        for j in range(parts):
            cols = order(a, j) * local + own
            angle = 2.0 * np.pi / period * ((rows[:, None] * cols[None, :]) % period)
            cosine, sine = np.cos(angle), np.sin(angle)
            if inverse:
                block = np.block([[cosine, -sine], [sine, cosine]])
            else:
                block = np.block([[cosine, sine], [-sine, cosine]]) / period
            tables[a, :, j * 2 * local : (j + 1) * 2 * local] = block
    tables = tables.astype(np.float32)
    high = tables.astype(jnp.bfloat16)
    low = (tables - high.astype(np.float32)).astype(jnp.bfloat16)
    return np.stack([high, low], axis=1)


def pack_kernel(rhs, fields_ref, *coded_refs):
    rows = fields_ref.shape[0] // rhs
    per = rhs // len(coded_refs)
    for r in range(rhs):
        x = fields_ref[pl.ds(r, rows, stride=rhs), :]
        root = jnp.sqrt(jnp.sqrt(jnp.abs(x) * (1.0 / FIELD_BOUND)))
        code = jnp.round(jnp.where(x < 0, -root, root) * CODE_TOP)
        coded_refs[r // per][r % per] = code.astype(jnp.int32).astype(jnp.int16)


def decoded(code):
    t = code.astype(jnp.int32).astype(jnp.float32) * (FIELD_BOUND**0.25 / CODE_TOP)
    return (t * jnp.abs(t)) * (t * t)


def forward_kernel(sources, az_ref, table_ref, *refs):
    coded_refs, modes_ref, held = refs[:sources], refs[sources], refs[sources + 1]
    rhs, rows, nodes = coded_refs[0].shape
    for r in range(0, rhs, 2):
        total = jnp.zeros((rows, 2 * nodes), jnp.float32)
        for j in range(sources):
            x = jnp.concatenate([decoded(coded_refs[j][r]), decoded(coded_refs[j][r + 1])], axis=1)
            high = x.astype(jnp.bfloat16)
            low = (x - high.astype(jnp.float32)).astype(jnp.bfloat16)
            cols = slice(j * rows, (j + 1) * rows)
            table_high, table_low = table_ref[0, 0, :, cols], table_ref[0, 1, :, cols]
            total += jnp.dot(table_high, high, preferred_element_type=jnp.float32)
            total += jnp.dot(table_low, high, preferred_element_type=jnp.float32)
            total += jnp.dot(table_high, low, preferred_element_type=jnp.float32)
        held[r * rows : (r + 1) * rows, :] = total[:, :nodes]
        held[(r + 1) * rows : (r + 2) * rows, :] = total[:, nodes:]
    local = rows // 2
    for k in range(local):
        real = held[pl.ds(k, rhs, stride=rows), :]
        imag = held[pl.ds(local + k, rhs, stride=rows), :]
        modes_ref[k] = jnp.concatenate([real, imag], axis=0).astype(jnp.bfloat16)


def near_kernel(pick_ref, tiles_ref, own_ref, side_ref, far_ref, near_ref, held):
    group, slots = tiles_ref.shape[0], tiles_ref.shape[2]
    block = tiles_ref.shape[-1]
    both = own_ref.shape[1]
    rhs = both // 2
    first = pl.program_id(0) * group
    for k in range(group):
        own, side, far = own_ref[k], side_ref[k], far_ref[k]
        values, tiles = [], []
        for t in range(slots):
            pick = pick_ref[(first + k) * slots + t]
            value = jnp.where(pick == 0, own, jnp.where(pick == 1, side, far))
            values.append(jnp.where(pick < 0, jnp.zeros_like(value), value))
            tiles.append(tiles_ref[k, 0, t].reshape(2 * block, block))
        product = lax.dot_general(
            jnp.concatenate(values, axis=1),
            jnp.concatenate(tiles, axis=1),
            (((1,), (1,)), ((), ())),
            preferred_element_type=jnp.float32,
        )
        held[k * both : k * both + rhs, :] = product[:rhs, :block] - product[rhs:, block:]
        held[k * both + rhs : (k + 1) * both, :] = product[rhs:, :block] + product[:rhs, block:]
    for r in range(rhs):
        for part in range(2):
            near_ref[r, part] = held[pl.ds(part * rhs + r, group, stride=both), :].astype(jnp.bfloat16)


def back_kernel(sources, rhs, az_ref, table_ref, fields_ref, impedance_ref, *refs):
    near_refs, out_ref = refs[:-1], refs[-1]
    per, _, local, nodes = near_refs[0].shape
    rows = 2 * local
    z_real, z_imag = impedance_ref[:local], impedance_ref[local:]
    for r in range(0, rhs, 2):
        total = jnp.zeros((rows, 2 * nodes), jnp.float32)
        for j in range(sources):
            source = near_refs[(r // per) * sources + j]
            x = jnp.concatenate(
                [source[r % per].reshape(rows, nodes), source[r % per + 1].reshape(rows, nodes)], axis=1
            )
            cols = slice(j * rows, (j + 1) * rows)
            total += jnp.dot(table_ref[0, 0, :, cols], x, preferred_element_type=jnp.float32)
            total += jnp.dot(table_ref[0, 1, :, cols], x, preferred_element_type=jnp.float32)
        for s in range(2):
            real, imag = total[:local, s * nodes : (s + 1) * nodes], total[local:, s * nodes : (s + 1) * nodes]
            at_real = pl.ds(r + s, local, stride=rhs)
            at_imag = pl.ds(local * rhs + r + s, local, stride=rhs)
            out_ref[at_real, :] = fields_ref[at_real, :] + z_real * real - z_imag * imag
            out_ref[at_imag, :] = fields_ref[at_imag, :] + z_real * imag + z_imag * real


def whole(x):
    return pl.BlockSpec(x.shape, lambda i, *s: (0,) * len(x.shape))


def table_spec(table):
    return pl.BlockSpec((1,) + table.shape[1:], lambda i, az: (az[0], 0, 0, 0))


def shared(x, parts):
    if parts == 4:
        peer = [(i, i ^ 1) for i in range(4)]
        across = [(i, i ^ 2) for i in range(4)]
        far = lax.ppermute(x, "az", across)
        near = lax.ppermute(x, "az", peer)
        return [x, near, far, lax.ppermute(far, "az", peer)]
    every = lax.all_gather(x, "az")
    return [every[j] for j in range(parts)]


def on_device(parts, ring, fields, impedance, tile_data, tile_cols, tile_count):
    _, local, rhs, nodes = fields.shape
    per = rhs // CHUNKS
    slots, block = tile_data.shape[2], tile_data.shape[-1]
    rows = 2 * local
    order = (lambda a, j: a ^ j) if parts == 4 else (lambda a, j: j)
    az = lax.axis_index("az").astype(jnp.int32)[None]
    place = lax.axis_index("curve")
    forward_table = jnp.asarray(dft_tables(parts, local, order, False))
    back_table = jnp.asarray(dft_tables(parts, local, order, True))
    flat_fields = fields.reshape(rows * rhs, nodes)
    params = pltpu.CompilerParams(vmem_limit_bytes=VMEM_LIMIT)

    even = jnp.mod(place, 2) == 0
    step = jnp.mod(tile_cols[:, 0, :] - place, ring)
    live = jnp.arange(slots, dtype=jnp.int32)[None, :] < tile_count
    pick = jnp.where(step == 0, 0, jnp.where((step == 1) == even, 1, 2))
    pick = jnp.where(live, pick, -1).astype(jnp.int32).reshape(-1)

    coded = pl.pallas_call(
        functools.partial(pack_kernel, rhs),
        out_shape=[jax.ShapeDtypeStruct((per, rows, nodes), jnp.int16)] * CHUNKS,
        compiler_params=params,
        name="pack",
    )(flat_fields)

    sides = [(i, i ^ 1) for i in range(ring)]
    onward = [(i, (i + 2 if i % 2 == 0 else i - 2) % ring) for i in range(ring)]
    group = min(16, local)
    near_all = []
    for chunk in coded:
        everyone = shared(chunk, parts)
        modes_shape = jax.ShapeDtypeStruct((local, 2 * per, nodes), jnp.bfloat16)
        own = pl.pallas_call(
            functools.partial(forward_kernel, parts),
            out_shape=modes_shape,
            grid_spec=pltpu.PrefetchScalarGridSpec(
                num_scalar_prefetch=1,
                grid=(1,),
                in_specs=[table_spec(forward_table)] + [whole(x) for x in everyone],
                out_specs=whole(modes_shape),
                scratch_shapes=[pltpu.VMEM((per * rows, nodes), jnp.float32)],
            ),
            compiler_params=params,
            name="forward",
        )(az, forward_table, *everyone)
        side = lax.ppermute(own, "curve", sides)
        far = lax.ppermute(side, "curve", onward)
        some_modes = pl.BlockSpec((group, 2 * per, nodes), lambda i, s: (i, 0, 0))
        near = pl.pallas_call(
            near_kernel,
            out_shape=jax.ShapeDtypeStruct((per, 2, local, nodes), jnp.bfloat16),
            grid_spec=pltpu.PrefetchScalarGridSpec(
                num_scalar_prefetch=1,
                grid=(local // group,),
                in_specs=[
                    pl.BlockSpec((group, 1, slots, 2, block, block), lambda i, s: (i, 0, 0, 0, 0, 0)),
                    some_modes,
                    some_modes,
                    some_modes,
                ],
                out_specs=pl.BlockSpec((per, 2, group, nodes), lambda i, s: (0, 0, i, 0)),
                scratch_shapes=[pltpu.VMEM((group * 2 * per, nodes), jnp.float32)],
            ),
            compiler_params=params,
            name="near",
        )(pick, tile_data, own, side, far)
        near_all += shared(near, parts)

    flat_impedance = impedance.reshape(rows, nodes)
    out_shape = jax.ShapeDtypeStruct(flat_fields.shape, jnp.float32)
    out = pl.pallas_call(
        functools.partial(back_kernel, parts, rhs),
        out_shape=out_shape,
        grid_spec=pltpu.PrefetchScalarGridSpec(
            num_scalar_prefetch=1,
            grid=(1,),
            in_specs=[table_spec(back_table), whole(flat_fields), whole(flat_impedance)]
            + [whole(x) for x in near_all],
            out_specs=whole(out_shape),
        ),
        compiler_params=params,
        name="back",
    )(az, back_table, flat_fields, flat_impedance, *near_all)
    return out.reshape(fields.shape)


def solution(mesh):
    placed = (
        P(None, "az", None, "curve"),
        P(None, "az", "curve"),
        P("az", "curve", None, None, None, None),
        P("az", "curve", None),
        P("az", "curve"),
    )
    return jax.shard_map(
        functools.partial(on_device, mesh.shape["az"], mesh.shape["curve"]),
        mesh=mesh,
        in_specs=placed,
        out_specs=P(None, "az", None, "curve"),
        check_vma=False,
    )
```

```python
import functools

import jax
import jax.numpy as jnp
import numpy as np
from jax import lax
from jax.experimental import pallas as pl
from jax.experimental.pallas import tpu as pltpu
from jax.sharding import PartitionSpec as P

CHUNKS = 2
FIELD_BOUND = 6.0
CODE_TOP = 32767.0
VMEM_LIMIT = 24 * 1024 * 1024


def dft_tables(parts, local, order, inverse):
    period = parts * local
    own = np.arange(local)
    tables = np.zeros((parts, 2 * local, parts * 2 * local), np.float64)
    for a in range(parts):
        rows = a * local + own
        for j in range(parts):
            cols = order(a, j) * local + own
            angle = 2.0 * np.pi / period * ((rows[:, None] * cols[None, :]) % period)
            cosine, sine = np.cos(angle), np.sin(angle)
            if inverse:
                block = np.block([[cosine, -sine], [sine, cosine]])
            else:
                block = np.block([[cosine, sine], [-sine, cosine]]) / period
            tables[a, :, j * 2 * local : (j + 1) * 2 * local] = block
    tables = tables.astype(np.float32)
    high = tables.astype(jnp.bfloat16)
    low = (tables - high.astype(np.float32)).astype(jnp.bfloat16)
    return np.stack([high, low], axis=1)


def pack_kernel(rhs, fields_ref, *coded_refs):
    rows = fields_ref.shape[0] // rhs
    per = rhs // len(coded_refs)
    for r in range(rhs):
        x = fields_ref[pl.ds(r, rows, stride=rhs), :]
        root = jnp.sqrt(jnp.sqrt(jnp.abs(x) * (1.0 / FIELD_BOUND)))
        code = jnp.round(jnp.where(x < 0, -root, root) * CODE_TOP)
        coded_refs[r // per][r % per] = code.astype(jnp.int32).astype(jnp.int16)


def decoded(code):
    t = code.astype(jnp.int32).astype(jnp.float32) * (FIELD_BOUND**0.25 / CODE_TOP)
    return (t * jnp.abs(t)) * (t * t)


def forward_kernel(sources, table_ref, *refs):
    coded_refs, modes_ref, held = refs[:sources], refs[sources], refs[sources + 1]
    rhs, rows, nodes = coded_refs[0].shape
    for r in range(0, rhs, 2):
        total = jnp.zeros((rows, 2 * nodes), jnp.float32)
        for j in range(sources):
            x = jnp.concatenate([decoded(coded_refs[j][r]), decoded(coded_refs[j][r + 1])], axis=1)
            high = x.astype(jnp.bfloat16)
            low = (x - high.astype(jnp.float32)).astype(jnp.bfloat16)
            cols = slice(j * rows, (j + 1) * rows)
            table_high, table_low = table_ref[0, :, cols], table_ref[1, :, cols]
            total += jnp.dot(table_high, high, preferred_element_type=jnp.float32)
            total += jnp.dot(table_low, high, preferred_element_type=jnp.float32)
            total += jnp.dot(table_high, low, preferred_element_type=jnp.float32)
        held[r * rows : (r + 1) * rows, :] = total[:, :nodes]
        held[(r + 1) * rows : (r + 2) * rows, :] = total[:, nodes:]
    local = rows // 2
    for k in range(local):
        real = held[pl.ds(k, rhs, stride=rows), :]
        imag = held[pl.ds(local + k, rhs, stride=rows), :]
        modes_ref[k] = jnp.concatenate([real, imag], axis=0).astype(jnp.bfloat16)


def stage_kernel(ring, place_ref, cols_ref, count_ref, tiles_ref, forward_ref, back_ref,
                 sorted_ref, forward_out, back_out, sems):
    az, place = place_ref[0], place_ref[1]
    modes, _, slots = tiles_ref.shape[:3]
    tables = [
        pltpu.make_async_copy(forward_ref.at[az], forward_out, sems.at[0]),
        pltpu.make_async_copy(back_ref.at[az], back_out, sems.at[1]),
    ]
    for copy in tables:
        copy.start()

    def tile_copy(k, t):
        step = lax.rem(cols_ref[t, k] - place + ring, ring)
        matched = jnp.where(lax.rem(place, 2) == 0, step == 1, step != 1)
        role = jnp.where(step == 0, 0, jnp.where(matched, 1, 2))
        copy = pltpu.make_async_copy(tiles_ref.at[k, 0, t], sorted_ref.at[role, k], sems.at[2])
        return role, copy

    def begin(k, carry):
        for t in range(slots):
            role, copy = tile_copy(k, t)
            used = t < count_ref[k]

            @pl.when(used)
            def _():
                copy.start()

            @pl.when(jnp.logical_not(used))
            def _():
                sorted_ref[role, k] = jnp.zeros(sorted_ref.shape[2:], sorted_ref.dtype)

        return carry

    def end(k, carry):
        for t in range(slots):

            @pl.when(t < count_ref[k])
            def _():
                tile_copy(k, t)[1].wait()

        return carry

    lax.fori_loop(0, modes, begin, 0)
    lax.fori_loop(0, modes, end, 0)
    for copy in tables:
        copy.wait()


def tile_product(sorted_ref, roles, k, values):
    block = sorted_ref.shape[-1]
    rhs = values[0].shape[0] // 2
    tiles = [sorted_ref[role, k].reshape(2 * block, block) for role in roles]
    product = lax.dot_general(
        jnp.concatenate(values, axis=1),
        jnp.concatenate(tiles, axis=1),
        (((1,), (1,)), ((), ())),
        preferred_element_type=jnp.float32,
    )
    real = product[:rhs, :block] - product[rhs:, block:]
    imag = product[rhs:, :block] + product[:rhs, block:]
    return real, imag


def inner_kernel(sorted_ref, own_ref, side_ref, part_ref):
    modes, both = own_ref.shape[:2]
    for k in range(modes):
        real, imag = tile_product(sorted_ref, (0, 1), k, [own_ref[k], side_ref[k]])
        part_ref[k * both : k * both + both // 2, :] = real
        part_ref[k * both + both // 2 : (k + 1) * both, :] = imag


def outer_kernel(sorted_ref, far_ref, part_ref, near_ref, held):
    modes, both = far_ref.shape[:2]
    rhs = both // 2
    for k in range(modes):
        real, imag = tile_product(sorted_ref, (2,), k, [far_ref[k]])
        at_real, at_imag = slice(k * both, k * both + rhs), slice(k * both + rhs, (k + 1) * both)
        held[at_real, :] = real + part_ref[at_real, :]
        held[at_imag, :] = imag + part_ref[at_imag, :]
    for r in range(rhs):
        for part in range(2):
            rows = slice(part * modes, (part + 1) * modes)
            near_ref[r, rows, :] = held[pl.ds(part * rhs + r, modes, stride=both), :].astype(jnp.bfloat16)


def back_kernel(sources, rhs, chunk, table_ref, fields_ref, impedance_ref, *refs):
    near_refs, out_ref, held, sem = refs[:sources], refs[-3], refs[-2], refs[-1]
    per, rows, nodes = near_refs[0].shape
    local = rows // 2
    z_real, z_imag = impedance_ref[:local], impedance_ref[local:]
    for r in range(0, per, 2):
        total = jnp.zeros((rows, 2 * nodes), jnp.float32)
        for j in range(sources):
            x = jnp.concatenate([near_refs[j][r], near_refs[j][r + 1]], axis=1)
            cols = slice(j * rows, (j + 1) * rows)
            total += jnp.dot(table_ref[0, :, cols], x, preferred_element_type=jnp.float32)
            total += jnp.dot(table_ref[1, :, cols], x, preferred_element_type=jnp.float32)
        for s in range(2):
            real, imag = total[:local, s * nodes : (s + 1) * nodes], total[local:, s * nodes : (s + 1) * nodes]
            from_row = chunk * per + r + s
            f_real = fields_ref[pl.ds(from_row, local, stride=rhs), :]
            f_imag = fields_ref[pl.ds(local * rhs + from_row, local, stride=rhs), :]
            held[pl.ds(r + s, local, stride=per), :] = f_real + z_real * real - z_imag * imag
            held[pl.ds(local * per + r + s, local, stride=per), :] = f_imag + z_real * imag + z_imag * real
    copy = pltpu.make_async_copy(
        held.reshape(rows, per, nodes), out_ref.at[:, pl.ds(chunk * per, per), :], sem
    )
    copy.start()
    copy.wait()


def shared(x, parts):
    if parts == 4:
        peer = [(i, i ^ 1) for i in range(4)]
        across = [(i, i ^ 2) for i in range(4)]
        far = lax.ppermute(x, "az", across)
        near = lax.ppermute(x, "az", peer)
        return [x, near, far, lax.ppermute(far, "az", peer)]
    every = lax.all_gather(x, "az")
    return [every[j] for j in range(parts)]


def after(x, *earlier):
    return lax.optimization_barrier((x,) + earlier)[0]


def on_device(parts, ring, fields, impedance, tile_data, tile_cols, tile_count):
    _, local, rhs, nodes = fields.shape
    per = rhs // CHUNKS
    slots, block = tile_data.shape[2], tile_data.shape[-1]
    rows = 2 * local
    order = (lambda a, j: a ^ j) if parts == 4 else (lambda a, j: j)
    forward_tables = jnp.asarray(dft_tables(parts, local, order, False))
    back_tables = jnp.asarray(dft_tables(parts, local, order, True))
    flat_fields = fields.reshape(rows * rhs, nodes)
    flat_impedance = impedance.reshape(rows, nodes)
    params = pltpu.CompilerParams(vmem_limit_bytes=VMEM_LIMIT)
    vmem, smem = pl.BlockSpec(memory_space=pltpu.VMEM), pl.BlockSpec(memory_space=pltpu.SMEM)
    hbm = pl.BlockSpec(memory_space=pltpu.HBM)

    coded = pl.pallas_call(
        functools.partial(pack_kernel, rhs),
        out_shape=[jax.ShapeDtypeStruct((per, rows, nodes), jnp.int16)] * CHUNKS,
        compiler_params=params,
        name="pack",
    )(flat_fields)

    everyone = []
    for chunk in coded:
        if everyone:
            chunk = after(chunk, everyone[-1][2])
        everyone.append(shared(chunk, parts))

    place = jnp.stack([lax.axis_index("az"), lax.axis_index("curve")]).astype(jnp.int32)
    place = after(place, coded[0])
    sorted_tiles, forward_table, back_table = pl.pallas_call(
        functools.partial(stage_kernel, ring),
        out_shape=[
            jax.ShapeDtypeStruct((slots, local, 2, block, block), tile_data.dtype),
            jax.ShapeDtypeStruct(forward_tables.shape[1:], jnp.bfloat16),
            jax.ShapeDtypeStruct(back_tables.shape[1:], jnp.bfloat16),
        ],
        in_specs=[smem, smem, smem, hbm, hbm, hbm],
        out_specs=[vmem, vmem, vmem],
        scratch_shapes=[pltpu.SemaphoreType.DMA((3,))],
        compiler_params=params,
        name="stage",
    )(place, tile_cols[:, 0, :].T, tile_count.reshape(local), tile_data, forward_tables, back_tables)

    sides = [(i, i ^ 1) for i in range(ring)]
    onward = [(i, (i + 2 if i % 2 == 0 else i - 2) % ring) for i in range(ring)]
    out_shape = jax.ShapeDtypeStruct((rows, rhs, nodes), jnp.float32)
    out = []
    for index, sources in enumerate(everyone):
        own = pl.pallas_call(
            functools.partial(forward_kernel, parts),
            out_shape=jax.ShapeDtypeStruct((local, 2 * per, nodes), jnp.bfloat16),
            in_specs=[vmem] * (1 + parts),
            out_specs=vmem,
            scratch_shapes=[pltpu.VMEM((per * rows, nodes), jnp.float32)],
            compiler_params=params,
            name="forward",
        )(forward_table, *sources)
        side = lax.ppermute(own, "curve", sides)
        far = lax.ppermute(side, "curve", onward)
        inner = pl.pallas_call(
            inner_kernel,
            out_shape=jax.ShapeDtypeStruct((local * 2 * per, nodes), jnp.float32),
            in_specs=[vmem] * 3,
            out_specs=vmem,
            compiler_params=params,
            name="inner",
        )(sorted_tiles, own, side)
        near = pl.pallas_call(
            outer_kernel,
            out_shape=jax.ShapeDtypeStruct((per, rows, nodes), jnp.bfloat16),
            in_specs=[vmem] * 3,
            out_specs=vmem,
            scratch_shapes=[pltpu.VMEM((local * 2 * per, nodes), jnp.float32)],
            compiler_params=params,
            name="outer",
        )(sorted_tiles, far, inner)
        operands = [back_table, flat_fields, flat_impedance] + shared(near, parts) + out
        out = [
            pl.pallas_call(
                functools.partial(back_kernel, parts, rhs, index),
                out_shape=out_shape,
                in_specs=[vmem] * (3 + parts) + [hbm] * len(out),
                out_specs=hbm,
                scratch_shapes=[pltpu.VMEM((rows * per, nodes), jnp.float32), pltpu.SemaphoreType.DMA],
                input_output_aliases={3 + parts: 0} if out else {},
                compiler_params=params,
                name="back",
            )(*operands)
        ]
    return out[0].reshape(fields.shape)


def solution(mesh):
    placed = (
        P(None, "az", None, "curve"),
        P(None, "az", "curve"),
        P("az", "curve", None, None, None, None),
        P("az", "curve", None),
        P("az", "curve"),
    )
    return jax.shard_map(
        functools.partial(on_device, mesh.shape["az"], mesh.shape["curve"]),
        mesh=mesh,
        in_specs=placed,
        out_specs=P(None, "az", None, "curve"),
        check_vma=False,
    )
```

```python
import functools

import jax
import jax.numpy as jnp
import numpy as np
from jax import lax
from jax.experimental import pallas as pl
from jax.experimental.pallas import tpu as pltpu
from jax.sharding import PartitionSpec as P

CHUNKS = 2
FIELD_BOUND = 6.0
CODE_TOP = 32767.0
VMEM_LIMIT = 24 * 1024 * 1024
STAGE_VMEM_LIMIT = 36 * 1024 * 1024


def dft_tables(parts, local, order, inverse):
    period = parts * local
    own = np.arange(local)
    tables = np.zeros((parts, 2 * local, parts * 2 * local), np.float64)
    for a in range(parts):
        rows = a * local + own
        for j in range(parts):
            cols = order(a, j) * local + own
            angle = 2.0 * np.pi / period * ((rows[:, None] * cols[None, :]) % period)
            cosine, sine = np.cos(angle), np.sin(angle)
            if inverse:
                block = np.block([[cosine, -sine], [sine, cosine]])
            else:
                block = np.block([[cosine, sine], [-sine, cosine]]) / period
            tables[a, :, j * 2 * local : (j + 1) * 2 * local] = block
    tables = tables.astype(np.float32)
    high = tables.astype(jnp.bfloat16)
    low = (tables - high.astype(np.float32)).astype(jnp.bfloat16)
    return np.stack([high, low], axis=1)


def pack_kernel(rhs, fields_ref, all_ref, *chunk_refs):
    rows = fields_ref.shape[0] // rhs
    per = rhs // len(chunk_refs)
    for r in range(rhs):
        x = fields_ref[pl.ds(r, rows, stride=rhs), :]
        root = jnp.sqrt(jnp.sqrt(jnp.abs(x) * (1.0 / FIELD_BOUND)))
        code = jnp.round(jnp.where(x < 0, -root, root) * CODE_TOP)
        code = code.astype(jnp.int32).astype(jnp.int16)
        all_ref[r] = code
        chunk_refs[r // per][r % per] = code


def decoded(code):
    t = code.astype(jnp.int32).astype(jnp.float32) * (FIELD_BOUND**0.25 / CODE_TOP)
    return (t * jnp.abs(t)) * (t * t)


def forward_kernel(firsts, table_ref, *refs):
    sources = len(firsts)
    coded_refs, modes_ref, held = refs[:sources], refs[sources], refs[sources + 1]
    rhs = modes_ref.shape[1] // 2
    rows, nodes = coded_refs[0].shape[1:]
    for r in range(0, rhs, 2):
        total = jnp.zeros((rows, 2 * nodes), jnp.float32)
        for j in range(sources):
            at = firsts[j] + r
            x = jnp.concatenate([decoded(coded_refs[j][at]), decoded(coded_refs[j][at + 1])], axis=1)
            high = x.astype(jnp.bfloat16)
            low = (x - high.astype(jnp.float32)).astype(jnp.bfloat16)
            cols = slice(j * rows, (j + 1) * rows)
            table_high, table_low = table_ref[0, :, cols], table_ref[1, :, cols]
            total += jnp.dot(table_high, high, preferred_element_type=jnp.float32)
            total += jnp.dot(table_low, high, preferred_element_type=jnp.float32)
            total += jnp.dot(table_high, low, preferred_element_type=jnp.float32)
        held[r * rows : (r + 1) * rows, :] = total[:, :nodes]
        held[(r + 1) * rows : (r + 2) * rows, :] = total[:, nodes:]
    local = rows // 2
    for k in range(local):
        real = held[pl.ds(k, rhs, stride=rows), :]
        imag = held[pl.ds(local + k, rhs, stride=rows), :]
        modes_ref[k] = jnp.concatenate([real, imag], axis=0).astype(jnp.bfloat16)


def stage_kernel(ring, place_ref, cols_ref, count_ref, tiles_ref, forward_ref, back_ref,
                 tiles_out, forward_out, back_out, slot_out, sems):
    az, place = place_ref[0], place_ref[1]
    modes = tiles_ref.shape[0]
    copies = [
        pltpu.make_async_copy(forward_ref.at[az], forward_out, sems.at[0]),
        pltpu.make_async_copy(back_ref.at[az], back_out, sems.at[1]),
        pltpu.make_async_copy(tiles_ref, tiles_out, sems.at[2]),
    ]
    for copy in copies:
        copy.start()
    even = lax.rem(place, 2) == 0
    side = jnp.where(even, place + 1, place - 1)
    far = lax.rem(jnp.where(even, place - 1, place + 1) + ring, ring)

    def find(k, carry):
        for role, wanted in enumerate((place, side, far)):
            slot = jnp.where(cols_ref[0, k] == wanted, 0, jnp.where(cols_ref[1, k] == wanted, 1, 2))
            slot_out[role * modes + k] = jnp.where(slot < count_ref[k], slot, -1)
        return carry

    lax.fori_loop(0, modes, find, 0)
    for copy in copies:
        copy.wait()


def tile_product(slot_ref, tiles_ref, k, roles, values):
    modes, block = tiles_ref.shape[0], tiles_ref.shape[-1]
    rhs = values[0].shape[0] // 2
    tiles, kept = [], []
    for role, value in zip(roles, values):
        slot = slot_ref[role * modes + k]
        tiles.append(tiles_ref[k, 0, jnp.maximum(slot, 0)].reshape(2 * block, block))
        kept.append(jnp.where(slot < 0, jnp.zeros_like(value), value))
    product = lax.dot_general(
        jnp.concatenate(kept, axis=1),
        jnp.concatenate(tiles, axis=1),
        (((1,), (1,)), ((), ())),
        preferred_element_type=jnp.float32,
    )
    real = product[:rhs, :block] - product[rhs:, block:]
    imag = product[rhs:, :block] + product[:rhs, block:]
    return real, imag


def inner_kernel(slot_ref, tiles_ref, own_ref, side_ref, part_ref):
    modes, both = own_ref.shape[:2]
    for k in range(modes):
        real, imag = tile_product(slot_ref, tiles_ref, k, (0, 1), [own_ref[k], side_ref[k]])
        part_ref[k * both : k * both + both // 2, :] = real
        part_ref[k * both + both // 2 : (k + 1) * both, :] = imag


def outer_kernel(slot_ref, tiles_ref, far_ref, part_ref, near_ref, held):
    modes, both = far_ref.shape[:2]
    rhs = both // 2
    for k in range(modes):
        real, imag = tile_product(slot_ref, tiles_ref, k, (2,), [far_ref[k]])
        at_real, at_imag = slice(k * both, k * both + rhs), slice(k * both + rhs, (k + 1) * both)
        held[at_real, :] = real + part_ref[at_real, :]
        held[at_imag, :] = imag + part_ref[at_imag, :]
    for r in range(rhs):
        for part in range(2):
            rows = slice(part * modes, (part + 1) * modes)
            near_ref[r, rows, :] = held[pl.ds(part * rhs + r, modes, stride=both), :].astype(jnp.bfloat16)


def back_kernel(sources, rhs, chunk, table_ref, fields_ref, impedance_ref, *refs):
    near_refs, out_ref, held, sem = refs[:sources], refs[-3], refs[-2], refs[-1]
    per, rows, nodes = near_refs[0].shape
    local = rows // 2
    z_real, z_imag = impedance_ref[:local], impedance_ref[local:]
    for r in range(0, per, 2):
        total = jnp.zeros((rows, 2 * nodes), jnp.float32)
        for j in range(sources):
            x = jnp.concatenate([near_refs[j][r], near_refs[j][r + 1]], axis=1)
            cols = slice(j * rows, (j + 1) * rows)
            total += jnp.dot(table_ref[0, :, cols], x, preferred_element_type=jnp.float32)
            total += jnp.dot(table_ref[1, :, cols], x, preferred_element_type=jnp.float32)
        for s in range(2):
            real, imag = total[:local, s * nodes : (s + 1) * nodes], total[local:, s * nodes : (s + 1) * nodes]
            from_row = chunk * per + r + s
            f_real = fields_ref[pl.ds(from_row, local, stride=rhs), :]
            f_imag = fields_ref[pl.ds(local * rhs + from_row, local, stride=rhs), :]
            held[pl.ds(r + s, local, stride=per), :] = f_real + z_real * real - z_imag * imag
            held[pl.ds(local * per + r + s, local, stride=per), :] = f_imag + z_real * imag + z_imag * real
    copy = pltpu.make_async_copy(
        held.reshape(rows, per, nodes), out_ref.at[:, pl.ds(chunk * per, per), :], sem
    )
    copy.start()
    copy.wait()


PEER = [(i, i ^ 1) for i in range(4)]
ACROSS = [(i, i ^ 2) for i in range(4)]


def after(x, *earlier):
    return lax.optimization_barrier((x,) + earlier)[0]


def cost(flops, moved):
    return pl.CostEstimate(flops=flops, bytes_accessed=moved, transcendentals=0)


def on_device(parts, ring, fields, impedance, tile_data, tile_cols, tile_count):
    _, local, rhs, nodes = fields.shape
    per = rhs // CHUNKS
    slots, block = tile_data.shape[2], tile_data.shape[-1]
    rows = 2 * local
    paired = parts == 4
    order = (lambda a, j: a ^ j) if paired else (lambda a, j: j)
    forward_tables = jnp.asarray(dft_tables(parts, local, order, False))
    back_tables = jnp.asarray(dft_tables(parts, local, order, True))
    flat_fields = fields.reshape(rows * rhs, nodes)
    flat_impedance = impedance.reshape(rows, nodes)
    params = pltpu.CompilerParams(vmem_limit_bytes=VMEM_LIMIT)
    vmem, smem = pl.BlockSpec(memory_space=pltpu.VMEM), pl.BlockSpec(memory_space=pltpu.SMEM)
    hbm = pl.BlockSpec(memory_space=pltpu.HBM)
    move = 16 * fields.size
    multiply = 4 * rows * rows * parts * per * nodes

    coded, *chunks = pl.pallas_call(
        functools.partial(pack_kernel, rhs),
        out_shape=[jax.ShapeDtypeStruct((rhs, rows, nodes), jnp.int16)]
        + [jax.ShapeDtypeStruct((per, rows, nodes), jnp.int16)] * CHUNKS,
        cost_estimate=cost(0, move),
        compiler_params=params,
        name="pack",
    )(flat_fields)

    place = jnp.stack([lax.axis_index("az"), lax.axis_index("curve")]).astype(jnp.int32)
    place = after(place, coded)
    tiles, forward_table, back_table, slot = pl.pallas_call(
        functools.partial(stage_kernel, ring),
        out_shape=[
            jax.ShapeDtypeStruct(tile_data.shape, tile_data.dtype),
            jax.ShapeDtypeStruct(forward_tables.shape[1:], jnp.bfloat16),
            jax.ShapeDtypeStruct(back_tables.shape[1:], jnp.bfloat16),
            jax.ShapeDtypeStruct((slots * local,), jnp.int32),
        ],
        in_specs=[smem, smem, smem, hbm, hbm, hbm],
        out_specs=[vmem, vmem, vmem, smem],
        scratch_shapes=[pltpu.SemaphoreType.DMA((3,))],
        cost_estimate=cost(0, 2 * tile_data.size),
        compiler_params=pltpu.CompilerParams(vmem_limit_bytes=STAGE_VMEM_LIMIT),
        name="stage",
    )(place, tile_cols[:, 0, :].T, tile_count.reshape(local), tile_data, forward_tables, back_tables)

    sides = [(i, i ^ 1) for i in range(ring)]
    onward = [(i, (i + 2 if i % 2 == 0 else i - 2) % ring) for i in range(ring)]
    peer = lax.ppermute(coded, "az", PEER) if paired else None
    owns, ready = [], (tiles,)
    for index, chunk in enumerate(chunks):
        if paired:
            across = lax.ppermute(after(chunk, *ready) if index else chunk, "az", ACROSS)
            across = after(across, *ready) if index == 0 else after(across, owns[-1])
            ready = (across,)
            sources = [coded, peer, across, lax.ppermute(across, "az", PEER)]
            firsts = (index * per, index * per, 0, 0)
        else:
            every = lax.all_gather(chunk, "az")
            sources, firsts = [every[j] for j in range(parts)], (0,) * parts
        owns.append(
            pl.pallas_call(
                functools.partial(forward_kernel, firsts),
                out_shape=jax.ShapeDtypeStruct((local, 2 * per, nodes), jnp.bfloat16),
                in_specs=[vmem] * (1 + parts),
                out_specs=vmem,
                scratch_shapes=[pltpu.VMEM((per * rows, nodes), jnp.float32)],
                cost_estimate=cost(3 * multiply, move),
                compiler_params=params,
                name="forward",
            )(forward_table, *sources)
        )

    nears = []
    for own in owns:
        side = lax.ppermute(own, "curve", sides)
        far = lax.ppermute(side, "curve", onward)
        inner = pl.pallas_call(
            inner_kernel,
            out_shape=jax.ShapeDtypeStruct((local * 2 * per, nodes), jnp.float32),
            in_specs=[smem] + [vmem] * 3,
            out_specs=vmem,
            cost_estimate=cost(0, tile_data.size),
            compiler_params=params,
            name="inner",
        )(slot, tiles, own, side)
        far = after(far, inner)
        nears.append(
            pl.pallas_call(
                outer_kernel,
                out_shape=jax.ShapeDtypeStruct((per, rows, nodes), jnp.bfloat16),
                in_specs=[smem] + [vmem] * 3,
                out_specs=vmem,
                scratch_shapes=[pltpu.VMEM((local * 2 * per, nodes), jnp.float32)],
                cost_estimate=cost(0, tile_data.size // 2),
                compiler_params=params,
                name="outer",
            )(slot, tiles, far, inner)
        )

    out = None
    for index, near in enumerate(nears):
        if paired:
            across = lax.ppermute(near, "az", ACROSS)
            if out is not None:
                across, out = lax.optimization_barrier((across, out))
            sources = [near, lax.ppermute(near, "az", PEER), across, lax.ppermute(across, "az", PEER)]
        else:
            every = lax.all_gather(near, "az")
            sources = [every[j] for j in range(parts)]
        earlier = [] if out is None else [out]
        out = pl.pallas_call(
            functools.partial(back_kernel, parts, rhs, index),
            out_shape=jax.ShapeDtypeStruct((rows, rhs, nodes), jnp.float32),
            in_specs=[vmem] * (3 + parts) + [hbm] * len(earlier),
            out_specs=hbm,
            scratch_shapes=[pltpu.VMEM((rows * per, nodes), jnp.float32), pltpu.SemaphoreType.DMA],
            input_output_aliases={3 + parts: 0} if earlier else {},
            cost_estimate=cost(2 * multiply, move),
            compiler_params=params,
            name="back",
        )(back_table, flat_fields, flat_impedance, *sources, *earlier)
    return out.reshape(fields.shape)


def solution(mesh):
    placed = (
        P(None, "az", None, "curve"),
        P(None, "az", "curve"),
        P("az", "curve", None, None, None, None),
        P("az", "curve", None),
        P("az", "curve"),
    )
    return jax.shard_map(
        functools.partial(on_device, mesh.shape["az"], mesh.shape["curve"]),
        mesh=mesh,
        in_specs=placed,
        out_specs=P(None, "az", None, "curve"),
        check_vma=False,
    )
```

```python
import functools

import jax
import jax.numpy as jnp
import numpy as np
from jax import lax
from jax.experimental import pallas as pl
from jax.experimental.pallas import tpu as pltpu
from jax.sharding import PartitionSpec as P

CHUNKS = 2
SHARES = 2
FIELD_BOUND = 6.0
CODE_TOP = 32767.0
VMEM_LIMIT = 24 * 1024 * 1024
STAGE_VMEM_LIMIT = 46 * 1024 * 1024
PACK_VMEM_LIMIT = 53 * 1024 * 1024
LATER_VMEM_LIMIT = 50 * 1024 * 1024


def dft_tables(parts, local, order, inverse):
    period = parts * local
    own = np.arange(local)
    tables = np.zeros((parts, 2 * local, parts * 2 * local), np.float64)
    for a in range(parts):
        rows = a * local + own
        for j in range(parts):
            cols = order(a, j) * local + own
            angle = 2.0 * np.pi / period * ((rows[:, None] * cols[None, :]) % period)
            cosine, sine = np.cos(angle), np.sin(angle)
            if inverse:
                block = np.block([[cosine, -sine], [sine, cosine]])
            else:
                block = np.block([[cosine, sine], [-sine, cosine]]) / period
            tables[a, :, j * 2 * local : (j + 1) * 2 * local] = block
    tables = tables.astype(np.float32)
    high = tables.astype(jnp.bfloat16)
    low = (tables - high.astype(np.float32)).astype(jnp.bfloat16)
    return np.stack([high, low], axis=1)


def code_rows(held, chunk_ref, all_ref, first):
    per, rows = chunk_ref.shape[:2]
    for r in range(per):
        x = held[pl.ds(r, rows, stride=per), :]
        root = jnp.sqrt(jnp.sqrt(jnp.abs(x) * (1.0 / FIELD_BOUND)))
        code = jnp.round(jnp.where(x < 0, -root, root) * CODE_TOP)
        code = code.astype(jnp.int32).astype(jnp.int16)
        chunk_ref[r] = code
        if all_ref is not None:
            all_ref[first + r] = code


def chunk_copy(fields_ref, held, per, chunk, sem):
    rows, _, nodes = fields_ref.shape
    return pltpu.make_async_copy(
        fields_ref.at[:, pl.ds(chunk * per, per), :], held.reshape(rows, per, nodes), sem
    )


def first_pack_kernel(fields_ref, chunk_ref, held, sem):
    copy = chunk_copy(fields_ref, held, chunk_ref.shape[0], 0, sem)
    copy.start()
    copy.wait()
    code_rows(held, chunk_ref, None, 0)


def later_pack_kernel(az_ref, fields_ref, tables_ref, first_ref, *refs):
    chunk_refs, (all_ref, forward_out, back_out, held, sems) = refs[:-5], refs[-5:]
    per = first_ref.shape[0]
    tables = [
        pltpu.make_async_copy(tables_ref.at[az_ref[0], 0], forward_out, sems.at[0]),
        pltpu.make_async_copy(tables_ref.at[az_ref[0], 1], back_out, sems.at[1]),
    ]
    for index, chunk_ref in enumerate(chunk_refs):
        copy = chunk_copy(fields_ref, held, per, index + 1, sems.at[2])
        copy.start()
        if index == 0:
            for table in tables:
                table.start()
            all_ref[:per] = first_ref[...]
        copy.wait()
        code_rows(held, chunk_ref, all_ref, (index + 1) * per)
    for table in tables:
        table.wait()


def decoded(code):
    t = code.astype(jnp.int32).astype(jnp.float32) * (FIELD_BOUND**0.25 / CODE_TOP)
    return (t * jnp.abs(t)) * (t * t)


def forward_kernel(firsts, table_ref, *refs):
    sources = len(firsts)
    coded_refs, modes_ref, held = refs[:sources], refs[sources], refs[sources + 1]
    rhs = modes_ref.shape[1] // 2
    rows, nodes = coded_refs[0].shape[1:]
    for r in range(0, rhs, 2):
        total = jnp.zeros((rows, 2 * nodes), jnp.float32)
        for j in range(sources):
            at = firsts[j] + r
            x = jnp.concatenate([decoded(coded_refs[j][at]), decoded(coded_refs[j][at + 1])], axis=1)
            high = x.astype(jnp.bfloat16)
            low = (x - high.astype(jnp.float32)).astype(jnp.bfloat16)
            cols = slice(j * rows, (j + 1) * rows)
            table_high, table_low = table_ref[0, :, cols], table_ref[1, :, cols]
            total += jnp.dot(table_high, high, preferred_element_type=jnp.float32)
            total += jnp.dot(table_low, high, preferred_element_type=jnp.float32)
            total += jnp.dot(table_high, low, preferred_element_type=jnp.float32)
        held[r * rows : (r + 1) * rows, :] = total[:, :nodes]
        held[(r + 1) * rows : (r + 2) * rows, :] = total[:, nodes:]
    local = rows // 2
    for k in range(local):
        real = held[pl.ds(k, rhs, stride=rows), :]
        imag = held[pl.ds(local + k, rhs, stride=rows), :]
        modes_ref[k] = jnp.concatenate([real, imag], axis=0).astype(jnp.bfloat16)


def stage_kernel(first, tiles_ref, out_ref, sem):
    share = out_ref.shape[0] - 1
    copy = pltpu.make_async_copy(tiles_ref.at[pl.ds(first, share)], out_ref.at[pl.ds(0, share)], sem)
    copy.start()
    out_ref[share] = jnp.zeros(out_ref.shape[1:], out_ref.dtype)
    copy.wait()


def find_kernel(ring, shares, place_ref, cols_ref, count_ref, tiles_ref, out_ref, slot_ref, sem):
    slots, modes = cols_ref.shape
    share = out_ref.shape[0] - 1
    copy = pltpu.make_async_copy(tiles_ref.at[pl.ds(0, share)], out_ref.at[pl.ds(0, share)], sem)
    copy.start()
    out_ref[share] = jnp.zeros(out_ref.shape[1:], out_ref.dtype)
    place = place_ref[0]
    even = lax.rem(place, 2) == 0
    side = jnp.where(even, place + 1, place - 1)
    far = lax.rem(jnp.where(even, place - 1, place + 1) + ring, ring)

    def find(k, carry):
        base = lax.rem(k, modes // shares) * slots
        for role, wanted in enumerate((place, side, far)):
            slot = jnp.where(cols_ref[0, k] == wanted, 0, jnp.where(cols_ref[1, k] == wanted, 1, 2))
            slot_ref[role * modes + k] = jnp.where(slot < count_ref[k], base + slot, share)
        return carry

    lax.fori_loop(0, modes, find, 0)
    copy.wait()


def tile_product(slot_ref, tile_refs, modes, k, roles, values):
    tiles_ref = tile_refs[k * len(tile_refs) // modes]
    block = tiles_ref.shape[-1]
    rhs = values[0].shape[0] // 2
    product = lax.dot_general(
        jnp.concatenate(values, axis=1),
        jnp.concatenate([tiles_ref[slot_ref[role * modes + k]] for role in roles], axis=1),
        (((1,), (1,)), ((), ())),
        preferred_element_type=jnp.float32,
    )
    real = product[:rhs, :block] - product[rhs:, block:]
    imag = product[rhs:, :block] + product[:rhs, block:]
    return real, imag


def inner_kernel(slot_ref, *refs):
    tile_refs, (own_ref, side_ref, part_ref) = refs[:-3], refs[-3:]
    modes, both = own_ref.shape[:2]
    for k in range(modes):
        real, imag = tile_product(slot_ref, tile_refs, modes, k, (0, 1), [own_ref[k], side_ref[k]])
        part_ref[k * both : k * both + both // 2, :] = real
        part_ref[k * both + both // 2 : (k + 1) * both, :] = imag


def outer_kernel(slot_ref, *refs):
    tile_refs, (far_ref, part_ref, near_ref, held) = refs[:-4], refs[-4:]
    modes, both = far_ref.shape[:2]
    rhs = both // 2
    for k in range(modes):
        real, imag = tile_product(slot_ref, tile_refs, modes, k, (2,), [far_ref[k]])
        at_real, at_imag = slice(k * both, k * both + rhs), slice(k * both + rhs, (k + 1) * both)
        held[at_real, :] = real + part_ref[at_real, :]
        held[at_imag, :] = imag + part_ref[at_imag, :]
    for r in range(rhs):
        for part in range(2):
            rows = slice(part * modes, (part + 1) * modes)
            near_ref[r, rows, :] = held[pl.ds(part * rhs + r, modes, stride=both), :].astype(jnp.bfloat16)


def back_kernel(sources, rhs, chunk, table_ref, fields_ref, impedance_ref, *refs):
    near_refs, out_ref, held, sem = refs[:sources], refs[-3], refs[-2], refs[-1]
    per, rows, nodes = near_refs[0].shape
    local = rows // 2
    z_real, z_imag = impedance_ref[:local], impedance_ref[local:]
    for r in range(0, per, 2):
        total = jnp.zeros((rows, 2 * nodes), jnp.float32)
        for j in range(sources):
            x = jnp.concatenate([near_refs[j][r], near_refs[j][r + 1]], axis=1)
            cols = slice(j * rows, (j + 1) * rows)
            total += jnp.dot(table_ref[0, :, cols], x, preferred_element_type=jnp.float32)
            total += jnp.dot(table_ref[1, :, cols], x, preferred_element_type=jnp.float32)
        for s in range(2):
            real, imag = total[:local, s * nodes : (s + 1) * nodes], total[local:, s * nodes : (s + 1) * nodes]
            from_row = chunk * per + r + s
            f_real = fields_ref[pl.ds(from_row, local, stride=rhs), :]
            f_imag = fields_ref[pl.ds(local * rhs + from_row, local, stride=rhs), :]
            held[pl.ds(r + s, local, stride=per), :] = f_real + z_real * real - z_imag * imag
            held[pl.ds(local * per + r + s, local, stride=per), :] = f_imag + z_real * imag + z_imag * real
    copy = pltpu.make_async_copy(
        held.reshape(rows, per, nodes), out_ref.at[:, pl.ds(chunk * per, per), :], sem
    )
    copy.start()
    copy.wait()


PEER = [(i, i ^ 1) for i in range(4)]
ACROSS = [(i, i ^ 2) for i in range(4)]


def after(x, *earlier):
    return lax.optimization_barrier((x,) + earlier)[0]


def cost(flops, moved):
    return pl.CostEstimate(flops=flops, bytes_accessed=moved, transcendentals=0)


def on_device(parts, ring, fields, impedance, tile_data, tile_cols, tile_count):
    _, local, rhs, nodes = fields.shape
    per = rhs // CHUNKS
    slots, block = tile_data.shape[2], tile_data.shape[-1]
    rows = 2 * local
    paired = parts == 4
    order = (lambda a, j: a ^ j) if paired else (lambda a, j: j)
    tables = jnp.asarray(
        np.stack([dft_tables(parts, local, order, False), dft_tables(parts, local, order, True)], axis=1)
    )
    table_shape = jax.ShapeDtypeStruct(tables.shape[2:], jnp.bfloat16)
    flat_fields = fields.reshape(rows * rhs, nodes)
    cut_fields = fields.reshape(rows, rhs, nodes)
    flat_impedance = impedance.reshape(rows, nodes)
    flat_tiles = tile_data.reshape(local * slots, 2 * block, block)
    share = local * slots // SHARES
    tiles_shape = jax.ShapeDtypeStruct((share + 1, 2 * block, block), tile_data.dtype)
    params = pltpu.CompilerParams(vmem_limit_bytes=VMEM_LIMIT)
    pack_params = pltpu.CompilerParams(vmem_limit_bytes=PACK_VMEM_LIMIT)
    later_params = pltpu.CompilerParams(vmem_limit_bytes=LATER_VMEM_LIMIT)
    stage_params = pltpu.CompilerParams(vmem_limit_bytes=STAGE_VMEM_LIMIT)
    vmem, smem = pl.BlockSpec(memory_space=pltpu.VMEM), pl.BlockSpec(memory_space=pltpu.SMEM)
    hbm = pl.BlockSpec(memory_space=pltpu.HBM)
    move = 16 * fields.size
    multiply = 4 * rows * rows * parts * per * nodes
    chunk_shape = jax.ShapeDtypeStruct((per, rows, nodes), jnp.int16)

    first = pl.pallas_call(
        first_pack_kernel,
        out_shape=chunk_shape,
        in_specs=[hbm],
        out_specs=vmem,
        scratch_shapes=[pltpu.VMEM((rows * per, nodes), jnp.float32), pltpu.SemaphoreType.DMA],
        cost_estimate=cost(0, move // 2),
        compiler_params=pack_params,
        name="pack",
    )(cut_fields)
    az = lax.axis_index("az").astype(jnp.int32)[None]
    place = lax.axis_index("curve").astype(jnp.int32)[None]
    *later, coded, forward_table, back_table = pl.pallas_call(
        later_pack_kernel,
        out_shape=[chunk_shape] * (CHUNKS - 1)
        + [jax.ShapeDtypeStruct((rhs, rows, nodes), jnp.int16), table_shape, table_shape],
        in_specs=[smem, hbm, hbm, vmem],
        out_specs=[vmem] * (CHUNKS + 2),
        scratch_shapes=[pltpu.VMEM((rows * per, nodes), jnp.float32), pltpu.SemaphoreType.DMA((3,))],
        cost_estimate=cost(0, move),
        compiler_params=later_params,
        name="later",
    )(az, cut_fields, tables, first)
    chunks = [first] + later

    peer = lax.ppermute(coded, "az", PEER) if paired else None
    tiles = []
    head, slot = pl.pallas_call(
        functools.partial(find_kernel, ring, SHARES),
        out_shape=[tiles_shape, jax.ShapeDtypeStruct((slots * local,), jnp.int32)],
        in_specs=[smem, smem, smem, hbm],
        out_specs=[vmem, smem],
        scratch_shapes=[pltpu.SemaphoreType.DMA],
        cost_estimate=cost(0, 2 * tile_data.size // SHARES),
        compiler_params=stage_params,
        name="find",
    )(after(place, coded), tile_cols[:, 0, :].T, tile_count.reshape(local), flat_tiles)
    tiles.append(head)

    sides = [(i, i ^ 1) for i in range(ring)]
    onward = [(i, (i + 2 if i % 2 == 0 else i - 2) % ring) for i in range(ring)]
    owns, ready = [], (head,)
    for index, chunk in enumerate(chunks):
        if paired:
            across = lax.ppermute(after(chunk, *ready) if index else chunk, "az", ACROSS)
            across = after(across, *ready, *tiles[1:])
            ready = (across,)
            sources = [coded, peer, across, lax.ppermute(across, "az", PEER)]
            firsts = (index * per, index * per, 0, 0)
        else:
            every = lax.all_gather(chunk, "az")
            sources, firsts = [every[j] for j in range(parts)], (0,) * parts
        own = pl.pallas_call(
            functools.partial(forward_kernel, firsts),
            out_shape=jax.ShapeDtypeStruct((local, 2 * per, nodes), jnp.bfloat16),
            in_specs=[vmem] * (1 + parts),
            out_specs=vmem,
            scratch_shapes=[pltpu.VMEM((per * rows, nodes), jnp.float32)],
            cost_estimate=cost(3 * multiply, move),
            compiler_params=params,
            name="forward",
        )(forward_table, *sources)
        owns.append(own)
        if index == 0:
            for place_of in range(1, SHARES):
                tail = pl.pallas_call(
                    functools.partial(stage_kernel, place_of * share),
                    out_shape=tiles_shape,
                    in_specs=[hbm],
                    out_specs=vmem,
                    scratch_shapes=[pltpu.SemaphoreType.DMA],
                    cost_estimate=cost(0, 2 * tile_data.size // SHARES),
                    compiler_params=stage_params,
                    name="stage",
                )(after(flat_tiles, own))
                tiles.append(tail)

    halo = []
    for own in owns:
        side = lax.ppermute(own, "curve", sides)
        far = lax.ppermute(side, "curve", onward)
        inner = pl.pallas_call(
            inner_kernel,
            out_shape=jax.ShapeDtypeStruct((local * 2 * per, nodes), jnp.float32),
            in_specs=[smem] + [vmem] * (2 + SHARES),
            out_specs=vmem,
            cost_estimate=cost(0, tile_data.size),
            compiler_params=params,
            name="inner",
        )(slot, *tiles, own, side)
        halo.append((inner, after(far, inner)))

    nears = []
    for inner, far in halo:
        nears.append(
            pl.pallas_call(
                outer_kernel,
                out_shape=jax.ShapeDtypeStruct((per, rows, nodes), jnp.bfloat16),
                in_specs=[smem] + [vmem] * (2 + SHARES),
                out_specs=vmem,
                scratch_shapes=[pltpu.VMEM((local * 2 * per, nodes), jnp.float32)],
                cost_estimate=cost(0, tile_data.size // 2),
                compiler_params=params,
                name="outer",
            )(slot, *tiles, far, inner)
        )

    out = None
    for index, near in enumerate(nears):
        if paired:
            across = lax.ppermute(near, "az", ACROSS)
            if out is not None:
                across, out = lax.optimization_barrier((across, out))
            elif CHUNKS > 1:
                across = after(across, halo[-1][0])
            sources = [near, lax.ppermute(near, "az", PEER), across, lax.ppermute(across, "az", PEER)]
        else:
            every = lax.all_gather(near, "az")
            sources = [every[j] for j in range(parts)]
        earlier = [] if out is None else [out]
        out = pl.pallas_call(
            functools.partial(back_kernel, parts, rhs, index),
            out_shape=jax.ShapeDtypeStruct((rows, rhs, nodes), jnp.float32),
            in_specs=[vmem] * (3 + parts) + [hbm] * len(earlier),
            out_specs=hbm,
            scratch_shapes=[pltpu.VMEM((rows * per, nodes), jnp.float32), pltpu.SemaphoreType.DMA],
            input_output_aliases={3 + parts: 0} if earlier else {},
            cost_estimate=cost(2 * multiply, move),
            compiler_params=params,
            name="back",
        )(back_table, flat_fields, flat_impedance, *sources, *earlier)
    return out.reshape(fields.shape)


def solution(mesh):
    placed = (
        P(None, "az", None, "curve"),
        P(None, "az", "curve"),
        P("az", "curve", None, None, None, None),
        P("az", "curve", None),
        P("az", "curve"),
    )
    return jax.shard_map(
        functools.partial(on_device, mesh.shape["az"], mesh.shape["curve"]),
        mesh=mesh,
        in_specs=placed,
        out_specs=P(None, "az", None, "curve"),
        check_vma=False,
    )
```

```python
import functools

import jax
import jax.numpy as jnp
import numpy as np
from jax import lax
from jax.experimental import pallas as pl
from jax.experimental.pallas import tpu as pltpu
from jax.sharding import PartitionSpec as P

CHUNKS = 2
SHARES = 2
FIELD_BOUND = 6.0
PARTIAL_BOUND = 4.25
CODE_TOP = 32767.0
VMEM_LIMIT = 24 * 1024 * 1024
STAGE_VMEM_LIMIT = 42 * 1024 * 1024
PACK_VMEM_LIMIT = 52 * 1024 * 1024


def dft_tables(parts, local, order, inverse):
    period = parts * local
    own = np.arange(local)
    tables = np.zeros((parts, 2 * local, parts * 2 * local), np.float64)
    for a in range(parts):
        rows = a * local + own
        for j in range(parts):
            cols = order(a, j) * local + own
            angle = 2.0 * np.pi / period * ((rows[:, None] * cols[None, :]) % period)
            cosine, sine = np.cos(angle), np.sin(angle)
            if inverse:
                block = np.block([[cosine, -sine], [sine, cosine]])
            else:
                block = np.block([[cosine, sine], [-sine, cosine]]) / period
            tables[a, :, j * 2 * local : (j + 1) * 2 * local] = block
    tables = tables.astype(np.float32)
    high = tables.astype(jnp.bfloat16)
    low = (tables - high.astype(np.float32)).astype(jnp.bfloat16)
    return np.stack([high, low], axis=1)


def encoded(x, bound):
    root = jnp.sqrt(jnp.sqrt(jnp.abs(x) * (1.0 / bound)))
    return jnp.round(jnp.where(x < 0, -root, root) * CODE_TOP).astype(jnp.int32).astype(jnp.int16)


def decoded(code, bound=FIELD_BOUND):
    t = code.astype(jnp.int32).astype(jnp.float32) * (bound**0.25 / CODE_TOP)
    return (t * jnp.abs(t)) * (t * t)


def pack_kernel(chunks, az_ref, fields_ref, tables_ref, first_ref, all_ref, forward_out, back_out, held, sems):
    rows, rhs, nodes = fields_ref.shape
    per = rhs // chunks
    copies = [
        pltpu.make_async_copy(
            fields_ref.at[:, pl.ds(index * per, per), :], held.at[index].reshape(rows, per, nodes), sems.at[index]
        )
        for index in range(chunks)
    ]
    tables = [
        pltpu.make_async_copy(tables_ref.at[az_ref[0], way], out, sems.at[chunks + way])
        for way, out in enumerate((forward_out, back_out))
    ]
    for copy in copies + tables:
        copy.start()
    for index in range(chunks):
        copies[index].wait()
        for r in range(per):
            code = encoded(held[index, pl.ds(r, rows, stride=per), :], FIELD_BOUND)
            all_ref[index * per + r] = code
            if index == 0:
                first_ref[r] = code
    for table in tables:
        table.wait()


def exact_product(table_ref, cols, x):
    high = x.astype(jnp.bfloat16)
    low = (x - high.astype(jnp.float32)).astype(jnp.bfloat16)
    table_high, table_low = table_ref[0, :, cols], table_ref[1, :, cols]
    total = jnp.dot(table_high, high, preferred_element_type=jnp.float32)
    total += jnp.dot(table_low, high, preferred_element_type=jnp.float32)
    return total + jnp.dot(table_high, low, preferred_element_type=jnp.float32)


def write_modes(held, modes_ref):
    local, both = modes_ref.shape[:2]
    rhs, rows = both // 2, 2 * local
    for k in range(local):
        real = held[pl.ds(k, rhs, stride=rows), :]
        imag = held[pl.ds(local + k, rhs, stride=rows), :]
        modes_ref[k] = jnp.concatenate([real, imag], axis=0).astype(jnp.bfloat16)


def split_kernel(first, find, table_ref, own_ref, peer_ref, place_ref, cols_ref, count_ref, tiles_ref,
                 near_ref, far_ref, out_ref, slot_ref, sem):
    copy = find(place_ref, cols_ref, count_ref, tiles_ref, out_ref, slot_ref, sem)
    per, rows, nodes = far_ref.shape
    odd = lax.rem(lax.broadcasted_iota(jnp.int32, (rows, 2 * nodes), 0), 2) == 1
    for r in range(0, per, 2):
        near = jnp.zeros((rows, 2 * nodes), jnp.float32)
        far = jnp.zeros((rows, 2 * nodes), jnp.float32)
        for j, ref in enumerate((own_ref, peer_ref)):
            x = jnp.concatenate([decoded(ref[first + r]), decoded(ref[first + r + 1])], axis=1)
            cols = slice(j * rows, (j + 1) * rows)
            near += exact_product(table_ref, cols, x)
            far += exact_product(table_ref, cols, jnp.where(odd, -x, x))
        code = encoded(far, PARTIAL_BOUND)
        for s in range(2):
            near_ref[r + s] = near[:, s * nodes : (s + 1) * nodes]
            far_ref[r + s] = code[:, s * nodes : (s + 1) * nodes]
    copy.wait()


def finish_kernel(near_ref, far_ref, modes_ref, held):
    per, rows = far_ref.shape[:2]
    for r in range(per):
        held[r * rows : (r + 1) * rows, :] = near_ref[r] + decoded(far_ref[r], PARTIAL_BOUND)
    write_modes(held, modes_ref)


def forward_kernel(firsts, table_ref, *refs):
    sources = len(firsts)
    coded_refs, modes_ref, held = refs[:sources], refs[sources], refs[sources + 1]
    rhs = modes_ref.shape[1] // 2
    rows, nodes = coded_refs[0].shape[1:]
    for r in range(0, rhs, 2):
        total = jnp.zeros((rows, 2 * nodes), jnp.float32)
        for j in range(sources):
            at = firsts[j] + r
            x = jnp.concatenate([decoded(coded_refs[j][at]), decoded(coded_refs[j][at + 1])], axis=1)
            total += exact_product(table_ref, slice(j * rows, (j + 1) * rows), x)
        held[r * rows : (r + 1) * rows, :] = total[:, :nodes]
        held[(r + 1) * rows : (r + 2) * rows, :] = total[:, nodes:]
    write_modes(held, modes_ref)


def stage_kernel(first, tiles_ref, out_ref, sem):
    share = out_ref.shape[0] - 1
    copy = pltpu.make_async_copy(tiles_ref.at[pl.ds(first, share)], out_ref.at[pl.ds(0, share)], sem)
    copy.start()
    out_ref[share] = jnp.zeros(out_ref.shape[1:], out_ref.dtype)
    copy.wait()


def begin_find(ring, place_ref, cols_ref, count_ref, tiles_ref, out_ref, slot_ref, sem):
    slots, modes = cols_ref.shape
    share = out_ref.shape[0] - 1
    copy = pltpu.make_async_copy(tiles_ref.at[pl.ds(0, share)], out_ref.at[pl.ds(0, share)], sem)
    copy.start()
    out_ref[share] = jnp.zeros(out_ref.shape[1:], out_ref.dtype)
    place = place_ref[0]
    even = lax.rem(place, 2) == 0
    side = jnp.where(even, place + 1, place - 1)
    far = lax.rem(jnp.where(even, place - 1, place + 1) + ring, ring)

    def find(k, carry):
        base = lax.rem(k, share // slots) * slots
        for role, wanted in enumerate((place, side, far)):
            slot = jnp.where(cols_ref[0, k] == wanted, 0, jnp.where(cols_ref[1, k] == wanted, 1, 2))
            slot_ref[role * modes + k] = jnp.where(slot < count_ref[k], base + slot, share)
        return carry

    lax.fori_loop(0, modes, find, 0)
    return copy


def find_kernel(find, *refs):
    find(*refs).wait()


def tile_product(slot_ref, tile_refs, modes, k, roles, values):
    tiles_ref = tile_refs[k * len(tile_refs) // modes]
    block = tiles_ref.shape[-1]
    rhs = values[0].shape[0] // 2
    product = lax.dot_general(
        jnp.concatenate(values, axis=1),
        jnp.concatenate([tiles_ref[slot_ref[role * modes + k]] for role in roles], axis=1),
        (((1,), (1,)), ((), ())),
        preferred_element_type=jnp.float32,
    )
    real = product[:rhs, :block] - product[rhs:, block:]
    imag = product[rhs:, :block] + product[:rhs, block:]
    return real, imag


def inner_kernel(slot_ref, *refs):
    tile_refs, (own_ref, side_ref, part_ref) = refs[:-3], refs[-3:]
    modes, both = own_ref.shape[:2]
    for k in range(modes):
        real, imag = tile_product(slot_ref, tile_refs, modes, k, (0, 1), [own_ref[k], side_ref[k]])
        part_ref[k * both : k * both + both // 2, :] = real
        part_ref[k * both + both // 2 : (k + 1) * both, :] = imag


def outer_kernel(slot_ref, *refs):
    tile_refs, (far_ref, part_ref, near_ref, held) = refs[:-4], refs[-4:]
    modes, both = far_ref.shape[:2]
    rhs = both // 2
    for k in range(modes):
        real, imag = tile_product(slot_ref, tile_refs, modes, k, (2,), [far_ref[k]])
        at_real, at_imag = slice(k * both, k * both + rhs), slice(k * both + rhs, (k + 1) * both)
        held[at_real, :] = real + part_ref[at_real, :]
        held[at_imag, :] = imag + part_ref[at_imag, :]
    for r in range(rhs):
        for part in range(2):
            rows = slice(part * modes, (part + 1) * modes)
            near_ref[r, rows, :] = held[pl.ds(part * rhs + r, modes, stride=both), :].astype(jnp.bfloat16)


def back_kernel(sources, rhs, chunk, table_ref, fields_ref, impedance_ref, *refs):
    near_refs, out_ref, held, sem = refs[:sources], refs[-3], refs[-2], refs[-1]
    per, rows, nodes = near_refs[0].shape
    local = rows // 2
    z_real, z_imag = impedance_ref[:local], impedance_ref[local:]
    for r in range(0, per, 2):
        total = jnp.zeros((rows, 2 * nodes), jnp.float32)
        for j in range(sources):
            x = jnp.concatenate([near_refs[j][r], near_refs[j][r + 1]], axis=1)
            cols = slice(j * rows, (j + 1) * rows)
            total += jnp.dot(table_ref[0, :, cols], x, preferred_element_type=jnp.float32)
            total += jnp.dot(table_ref[1, :, cols], x, preferred_element_type=jnp.float32)
        for s in range(2):
            real, imag = total[:local, s * nodes : (s + 1) * nodes], total[local:, s * nodes : (s + 1) * nodes]
            from_row = chunk * per + r + s
            f_real = fields_ref[pl.ds(from_row, local, stride=rhs), :]
            f_imag = fields_ref[pl.ds(local * rhs + from_row, local, stride=rhs), :]
            held[pl.ds(r + s, local, stride=per), :] = f_real + z_real * real - z_imag * imag
            held[pl.ds(local * per + r + s, local, stride=per), :] = f_imag + z_real * imag + z_imag * real
    copy = pltpu.make_async_copy(
        held.reshape(rows, per, nodes), out_ref.at[:, pl.ds(chunk * per, per), :], sem
    )
    copy.start()
    copy.wait()


PEER = [(i, i ^ 1) for i in range(4)]
ACROSS = [(i, i ^ 2) for i in range(4)]


def after(x, *earlier):
    return lax.optimization_barrier((x,) + earlier)[0]


def cost(flops, moved):
    return pl.CostEstimate(flops=flops, bytes_accessed=moved, transcendentals=0)


def on_device(parts, ring, fields, impedance, tile_data, tile_cols, tile_count):
    _, local, rhs, nodes = fields.shape
    per = rhs // CHUNKS
    slots, block = tile_data.shape[2], tile_data.shape[-1]
    rows = 2 * local
    paired = parts == 4
    order = (lambda a, j: a ^ j) if paired else (lambda a, j: j)
    tables = jnp.asarray(
        np.stack([dft_tables(parts, local, order, False), dft_tables(parts, local, order, True)], axis=1)
    )
    table_shape = jax.ShapeDtypeStruct(tables.shape[2:], jnp.bfloat16)
    flat_fields = fields.reshape(rows * rhs, nodes)
    cut_fields = fields.reshape(rows, rhs, nodes)
    flat_impedance = impedance.reshape(rows, nodes)
    flat_tiles = tile_data.reshape(local * slots, 2 * block, block)
    share = local * slots // SHARES
    tiles_shape = jax.ShapeDtypeStruct((share + 1, 2 * block, block), tile_data.dtype)
    params = pltpu.CompilerParams(vmem_limit_bytes=VMEM_LIMIT)
    pack_params = pltpu.CompilerParams(vmem_limit_bytes=PACK_VMEM_LIMIT)
    stage_params = pltpu.CompilerParams(vmem_limit_bytes=STAGE_VMEM_LIMIT)
    vmem, smem = pl.BlockSpec(memory_space=pltpu.VMEM), pl.BlockSpec(memory_space=pltpu.SMEM)
    hbm = pl.BlockSpec(memory_space=pltpu.HBM)
    move = 16 * fields.size
    multiply = 4 * rows * rows * parts * per * nodes
    chunk_shape = jax.ShapeDtypeStruct((per, rows, nodes), jnp.int16)

    az = lax.axis_index("az").astype(jnp.int32)[None]
    place = lax.axis_index("curve").astype(jnp.int32)[None]
    first, coded, forward_table, back_table = pl.pallas_call(
        functools.partial(pack_kernel, CHUNKS),
        out_shape=[chunk_shape, jax.ShapeDtypeStruct((rhs, rows, nodes), jnp.int16), table_shape, table_shape],
        in_specs=[smem, hbm, hbm],
        out_specs=[vmem] * 4,
        scratch_shapes=[
            pltpu.VMEM((CHUNKS, rows * per, nodes), jnp.float32),
            pltpu.SemaphoreType.DMA((CHUNKS + 2,)),
        ],
        cost_estimate=cost(0, move),
        compiler_params=pack_params,
        name="pack",
    )(az, cut_fields, tables)

    peer = lax.ppermute(coded, "az", PEER) if paired else None
    find = functools.partial(begin_find, ring)
    find_shapes = [tiles_shape, jax.ShapeDtypeStruct((slots * local,), jnp.int32)]
    find_operands = (after(place, coded), tile_cols[:, 0, :].T, tile_count.reshape(local), flat_tiles)
    if paired:
        near_part, far_part, head, slot = pl.pallas_call(
            functools.partial(split_kernel, per, find),
            out_shape=[jax.ShapeDtypeStruct((per, rows, nodes), jnp.float32), chunk_shape] + find_shapes,
            in_specs=[vmem] * 3 + [smem] * 3 + [hbm],
            out_specs=[vmem] * 3 + [smem],
            scratch_shapes=[pltpu.SemaphoreType.DMA],
            cost_estimate=cost(3 * multiply, move),
            compiler_params=stage_params,
            name="split",
        )(forward_table, coded, peer, *find_operands)
    else:
        head, slot = pl.pallas_call(
            functools.partial(find_kernel, find),
            out_shape=find_shapes,
            in_specs=[smem] * 3 + [hbm],
            out_specs=[vmem, smem],
            scratch_shapes=[pltpu.SemaphoreType.DMA],
            compiler_params=stage_params,
            name="find",
        )(*find_operands)
    tiles = [head]

    sides = [(i, i ^ 1) for i in range(ring)]
    onward = [(i, (i + 2 if i % 2 == 0 else i - 2) % ring) for i in range(ring)]
    modes_shape = jax.ShapeDtypeStruct((local, 2 * per, nodes), jnp.bfloat16)
    held_modes = pltpu.VMEM((per * rows, nodes), jnp.float32)
    owns, earlier = [], None
    for index in range(CHUNKS):
        if paired and index:
            across = after(lax.ppermute(after(far_part, earlier), "az", ACROSS), tiles[-1])
            own = pl.pallas_call(
                finish_kernel,
                out_shape=modes_shape,
                in_specs=[vmem] * 2,
                out_specs=vmem,
                scratch_shapes=[held_modes],
                cost_estimate=cost(0, move // 2),
                compiler_params=params,
                name="finish",
            )(near_part, across)
        else:
            if paired:
                across = after(lax.ppermute(first, "az", ACROSS), far_part)
                earlier = across
                sources = [coded, peer, across, lax.ppermute(across, "az", PEER)]
                firsts = (0,) * parts
            else:
                every = lax.all_gather(coded[index * per : (index + 1) * per], "az")
                sources, firsts = [every[j] for j in range(parts)], (0,) * parts
            own = pl.pallas_call(
                functools.partial(forward_kernel, firsts),
                out_shape=modes_shape,
                in_specs=[vmem] * (1 + parts),
                out_specs=vmem,
                scratch_shapes=[held_modes],
                cost_estimate=cost(3 * multiply, move),
                compiler_params=params,
                name="forward",
            )(forward_table, *sources)
        owns.append(own)
        if index == 0:
            for turn in range(1, SHARES):
                tail = pl.pallas_call(
                    functools.partial(stage_kernel, turn * share),
                    out_shape=tiles_shape,
                    in_specs=[hbm],
                    out_specs=vmem,
                    scratch_shapes=[pltpu.SemaphoreType.DMA],
                    cost_estimate=cost(0, 2 * tile_data.size // SHARES),
                    compiler_params=stage_params,
                    name="stage",
                )(after(flat_tiles, own))
                tiles.append(tail)

    sides_in = [lax.ppermute(own, "curve", sides) for own in owns]
    for index in range(CHUNKS - 1):
        sides_in[index] = after(sides_in[index], owns[index + 1])
    halo = []
    for own, side in zip(owns, sides_in):
        far = lax.ppermute(side, "curve", onward)
        inner = pl.pallas_call(
            inner_kernel,
            out_shape=jax.ShapeDtypeStruct((local * 2 * per, nodes), jnp.float32),
            in_specs=[smem] + [vmem] * (2 + SHARES),
            out_specs=vmem,
            cost_estimate=cost(0, tile_data.size),
            compiler_params=params,
            name="inner",
        )(slot, *tiles, own, side)
        halo.append((inner, after(far, inner)))
    for index in range(CHUNKS - 1):
        inner, far = halo[index]
        halo[index] = (inner, after(far, sides_in[index + 1]))

    nears = []
    for inner, far in halo:
        nears.append(
            pl.pallas_call(
                outer_kernel,
                out_shape=jax.ShapeDtypeStruct((per, rows, nodes), jnp.bfloat16),
                in_specs=[smem] + [vmem] * (2 + SHARES),
                out_specs=vmem,
                scratch_shapes=[pltpu.VMEM((local * 2 * per, nodes), jnp.float32)],
                cost_estimate=cost(0, tile_data.size // 2),
                compiler_params=params,
                name="outer",
            )(slot, *tiles, far, inner)
        )

    out = None
    for index, near in enumerate(nears):
        if paired:
            across = lax.ppermute(near, "az", ACROSS)
            if out is not None:
                across, out = lax.optimization_barrier((across, out))
            elif CHUNKS > 1:
                across = after(across, halo[-1][0])
            sources = [near, lax.ppermute(near, "az", PEER), across, lax.ppermute(across, "az", PEER)]
        else:
            every = lax.all_gather(near, "az")
            sources = [every[j] for j in range(parts)]
        earlier = [] if out is None else [out]
        out = pl.pallas_call(
            functools.partial(back_kernel, parts, rhs, index),
            out_shape=jax.ShapeDtypeStruct((rows, rhs, nodes), jnp.float32),
            in_specs=[vmem] * (3 + parts) + [hbm] * len(earlier),
            out_specs=hbm,
            scratch_shapes=[pltpu.VMEM((rows * per, nodes), jnp.float32), pltpu.SemaphoreType.DMA],
            input_output_aliases={3 + parts: 0} if earlier else {},
            cost_estimate=cost(2 * multiply, move),
            compiler_params=params,
            name="back",
        )(back_table, flat_fields, flat_impedance, *sources, *earlier)
    return out.reshape(fields.shape)


def solution(mesh):
    placed = (
        P(None, "az", None, "curve"),
        P(None, "az", "curve"),
        P("az", "curve", None, None, None, None),
        P("az", "curve", None),
        P("az", "curve"),
    )
    return jax.shard_map(
        functools.partial(on_device, mesh.shape["az"], mesh.shape["curve"]),
        mesh=mesh,
        in_specs=placed,
        out_specs=P(None, "az", None, "curve"),
        check_vma=False,
    )
```

```python
import functools

import jax
import jax.numpy as jnp
import numpy as np
from jax import lax
from jax.experimental import pallas as pl
from jax.experimental.pallas import tpu as pltpu
from jax.sharding import PartitionSpec as P

CHUNKS = 2
SHARES = 2
FIELD_BOUND = 6.0
PARTIAL_BOUND = 4.25
CODE_TOP = 32767.0
VMEM_LIMIT = 24 * 1024 * 1024
STAGE_VMEM_LIMIT = 42 * 1024 * 1024
PACK_VMEM_LIMIT = 52 * 1024 * 1024


def dft_tables(parts, local, order, inverse):
    period = parts * local
    own = np.arange(local)
    tables = np.zeros((parts, 2 * local, parts * 2 * local), np.float64)
    for a in range(parts):
        rows = a * local + own
        for j in range(parts):
            cols = order(a, j) * local + own
            angle = 2.0 * np.pi / period * ((rows[:, None] * cols[None, :]) % period)
            cosine, sine = np.cos(angle), np.sin(angle)
            if inverse:
                block = np.block([[cosine, -sine], [sine, cosine]])
            else:
                block = np.block([[cosine, sine], [-sine, cosine]]) / period
            tables[a, :, j * 2 * local : (j + 1) * 2 * local] = block
    tables = tables.astype(np.float32)
    high = tables.astype(jnp.bfloat16)
    low = (tables - high.astype(np.float32)).astype(jnp.bfloat16)
    return np.stack([high, low], axis=1)


def encoded(x, bound):
    root = jnp.sqrt(jnp.sqrt(jnp.abs(x) * (1.0 / bound)))
    return jnp.round(jnp.where(x < 0, -root, root) * CODE_TOP).astype(jnp.int32).astype(jnp.int16)


def decoded(code, bound=FIELD_BOUND):
    t = code.astype(jnp.int32).astype(jnp.float32) * (bound**0.25 / CODE_TOP)
    return (t * jnp.abs(t)) * (t * t)


def pack_kernel(chunks, az_ref, fields_ref, tables_ref, first_ref, all_ref, forward_out, back_out, held, sems):
    rows, rhs, nodes = fields_ref.shape
    per = rhs // chunks
    copies = [
        pltpu.make_async_copy(
            fields_ref.at[:, pl.ds(index * per, per), :], held.at[index].reshape(rows, per, nodes), sems.at[index]
        )
        for index in range(chunks)
    ]
    tables = [
        pltpu.make_async_copy(tables_ref.at[az_ref[0], way], out, sems.at[chunks + way])
        for way, out in enumerate((forward_out, back_out))
    ]
    for copy in copies + tables:
        copy.start()
    for index in range(chunks):
        copies[index].wait()
        for r in range(per):
            code = encoded(held[index, pl.ds(r, rows, stride=per), :], FIELD_BOUND)
            all_ref[index * per + r] = code
            if index == 0:
                first_ref[r] = code
    for table in tables:
        table.wait()


def exact_product(table_ref, cols, x):
    high = x.astype(jnp.bfloat16)
    low = (x - high.astype(jnp.float32)).astype(jnp.bfloat16)
    table_high, table_low = table_ref[0, :, cols], table_ref[1, :, cols]
    total = jnp.dot(table_high, high, preferred_element_type=jnp.float32)
    total += jnp.dot(table_low, high, preferred_element_type=jnp.float32)
    return total + jnp.dot(table_high, low, preferred_element_type=jnp.float32)


def write_modes(held, modes_ref):
    local, both = modes_ref.shape[:2]
    rhs, rows = both // 2, 2 * local
    for k in range(local):
        real = held[pl.ds(k, rhs, stride=rows), :]
        imag = held[pl.ds(local + k, rhs, stride=rows), :]
        modes_ref[k] = jnp.concatenate([real, imag], axis=0).astype(jnp.bfloat16)


def split_kernel(first, find, table_ref, own_ref, peer_ref, place_ref, cols_ref, count_ref, tiles_ref,
                 near_ref, far_ref, out_ref, slot_ref, sem):
    copy = find(place_ref, cols_ref, count_ref, tiles_ref, out_ref, slot_ref, sem)
    per, rows, nodes = far_ref.shape
    odd = lax.rem(lax.broadcasted_iota(jnp.int32, (rows, 2 * nodes), 0), 2) == 1
    for r in range(0, per, 2):
        near = jnp.zeros((rows, 2 * nodes), jnp.float32)
        far = jnp.zeros((rows, 2 * nodes), jnp.float32)
        for j, ref in enumerate((own_ref, peer_ref)):
            x = jnp.concatenate([decoded(ref[first + r]), decoded(ref[first + r + 1])], axis=1)
            cols = slice(j * rows, (j + 1) * rows)
            near += exact_product(table_ref, cols, x)
            far += exact_product(table_ref, cols, jnp.where(odd, -x, x))
        code = encoded(far, PARTIAL_BOUND)
        for s in range(2):
            near_ref[r + s] = near[:, s * nodes : (s + 1) * nodes]
            far_ref[r + s] = code[:, s * nodes : (s + 1) * nodes]
    copy.wait()


def finish_kernel(near_ref, far_ref, modes_ref, held):
    per, rows = far_ref.shape[:2]
    for r in range(per):
        held[r * rows : (r + 1) * rows, :] = near_ref[r] + decoded(far_ref[r], PARTIAL_BOUND)
    write_modes(held, modes_ref)


def forward_kernel(firsts, table_ref, *refs):
    sources = len(firsts)
    coded_refs, modes_ref, held = refs[:sources], refs[sources], refs[sources + 1]
    rhs = modes_ref.shape[1] // 2
    rows, nodes = coded_refs[0].shape[1:]
    for r in range(0, rhs, 2):
        total = jnp.zeros((rows, 2 * nodes), jnp.float32)
        for j in range(sources):
            at = firsts[j] + r
            x = jnp.concatenate([decoded(coded_refs[j][at]), decoded(coded_refs[j][at + 1])], axis=1)
            total += exact_product(table_ref, slice(j * rows, (j + 1) * rows), x)
        held[r * rows : (r + 1) * rows, :] = total[:, :nodes]
        held[(r + 1) * rows : (r + 2) * rows, :] = total[:, nodes:]
    write_modes(held, modes_ref)


def stage_kernel(first, tiles_ref, out_ref, sem):
    share = out_ref.shape[0] - 1
    copy = pltpu.make_async_copy(tiles_ref.at[pl.ds(first, share)], out_ref.at[pl.ds(0, share)], sem)
    copy.start()
    out_ref[share] = jnp.zeros(out_ref.shape[1:], out_ref.dtype)
    copy.wait()


def begin_find(ring, place_ref, cols_ref, count_ref, tiles_ref, out_ref, slot_ref, sem):
    slots, modes = cols_ref.shape
    share = out_ref.shape[0] - 1
    copy = pltpu.make_async_copy(tiles_ref.at[pl.ds(0, share)], out_ref.at[pl.ds(0, share)], sem)
    copy.start()
    out_ref[share] = jnp.zeros(out_ref.shape[1:], out_ref.dtype)
    place = place_ref[0]
    even = lax.rem(place, 2) == 0
    side = jnp.where(even, place + 1, place - 1)
    far = lax.rem(jnp.where(even, place - 1, place + 1) + ring, ring)

    def find(k, carry):
        base = lax.rem(k, share // slots) * slots
        for role, wanted in enumerate((place, side, far)):
            slot = jnp.where(cols_ref[0, k] == wanted, 0, jnp.where(cols_ref[1, k] == wanted, 1, 2))
            slot_ref[role * modes + k] = jnp.where(slot < count_ref[k], base + slot, share)
        return carry

    lax.fori_loop(0, modes, find, 0)
    return copy


def find_kernel(find, *refs):
    find(*refs).wait()


def tile_product(slot_ref, tile_refs, modes, k, roles, values):
    tiles_ref = tile_refs[k * len(tile_refs) // modes]
    return lax.dot_general(
        jnp.concatenate(values, axis=1),
        jnp.concatenate([tiles_ref[slot_ref[role * modes + k]] for role in roles], axis=1),
        (((1,), (1,)), ((), ())),
        preferred_element_type=jnp.float32,
    )


def combined(product):
    rhs, block = product.shape[0] // 2, product.shape[1] // 2
    real = product[:rhs, :block] - product[rhs:, block:]
    imag = product[rhs:, :block] + product[:rhs, block:]
    return real, imag


def put(out_ref, k, both, real, imag):
    out_ref[k * both : k * both + both // 2, :] = real
    out_ref[k * both + both // 2 : (k + 1) * both, :] = imag


def inner_kernel(chunks, slot_ref, *refs):
    own_refs, side_ref, part_refs = refs[-2 * chunks - 1 : -chunks - 1], refs[-chunks - 1], refs[-chunks:]
    tile_refs = refs[: -2 * chunks - 1]
    modes, both = side_ref.shape[:2]
    for k in range(modes):
        owns = jnp.concatenate([ref[k] for ref in own_refs], axis=0)
        product = tile_product(slot_ref, tile_refs, modes, k, (0,), [owns])
        side = tile_product(slot_ref, tile_refs, modes, k, (1,), [side_ref[k]])
        for index, part_ref in enumerate(part_refs):
            mine = product[index * both : (index + 1) * both]
            put(part_ref, k, both, *combined(mine + side if index == 0 else mine))


def outer_kernel(roles, slot_ref, *refs):
    count = len(roles)
    tile_refs, value_refs, (part_ref, near_ref, held) = refs[: -3 - count], refs[-3 - count : -3], refs[-3:]
    modes, both = value_refs[0].shape[:2]
    rhs = both // 2
    for k in range(modes):
        real, imag = combined(tile_product(slot_ref, tile_refs, modes, k, roles, [ref[k] for ref in value_refs]))
        at_real, at_imag = slice(k * both, k * both + rhs), slice(k * both + rhs, (k + 1) * both)
        held[at_real, :] = real + part_ref[at_real, :]
        held[at_imag, :] = imag + part_ref[at_imag, :]
    for r in range(rhs):
        for part in range(2):
            rows = slice(part * modes, (part + 1) * modes)
            near_ref[r, rows, :] = held[pl.ds(part * rhs + r, modes, stride=both), :].astype(jnp.bfloat16)


def back_kernel(sources, rhs, chunk, table_ref, fields_ref, impedance_ref, *refs):
    near_refs, out_ref, held, sem = refs[:sources], refs[-3], refs[-2], refs[-1]
    per, rows, nodes = near_refs[0].shape
    local = rows // 2
    z_real, z_imag = impedance_ref[:local], impedance_ref[local:]
    for r in range(0, per, 2):
        total = jnp.zeros((rows, 2 * nodes), jnp.float32)
        for j in range(sources):
            x = jnp.concatenate([near_refs[j][r], near_refs[j][r + 1]], axis=1)
            cols = slice(j * rows, (j + 1) * rows)
            total += jnp.dot(table_ref[0, :, cols], x, preferred_element_type=jnp.float32)
            total += jnp.dot(table_ref[1, :, cols], x, preferred_element_type=jnp.float32)
        for s in range(2):
            real, imag = total[:local, s * nodes : (s + 1) * nodes], total[local:, s * nodes : (s + 1) * nodes]
            from_row = chunk * per + r + s
            f_real = fields_ref[pl.ds(from_row, local, stride=rhs), :]
            f_imag = fields_ref[pl.ds(local * rhs + from_row, local, stride=rhs), :]
            held[pl.ds(r + s, local, stride=per), :] = f_real + z_real * real - z_imag * imag
            held[pl.ds(local * per + r + s, local, stride=per), :] = f_imag + z_real * imag + z_imag * real
    copy = pltpu.make_async_copy(
        held.reshape(rows, per, nodes), out_ref.at[:, pl.ds(chunk * per, per), :], sem
    )
    copy.start()
    copy.wait()


PEER = [(i, i ^ 1) for i in range(4)]
ACROSS = [(i, i ^ 2) for i in range(4)]


def after(x, *earlier):
    return lax.optimization_barrier((x,) + earlier)[0]


def cost(flops, moved):
    return pl.CostEstimate(flops=flops, bytes_accessed=moved, transcendentals=0)


def on_device(parts, ring, fields, impedance, tile_data, tile_cols, tile_count):
    _, local, rhs, nodes = fields.shape
    per = rhs // CHUNKS
    slots, block = tile_data.shape[2], tile_data.shape[-1]
    rows = 2 * local
    paired = parts == 4
    order = (lambda a, j: a ^ j) if paired else (lambda a, j: j)
    tables = jnp.asarray(
        np.stack([dft_tables(parts, local, order, False), dft_tables(parts, local, order, True)], axis=1)
    )
    table_shape = jax.ShapeDtypeStruct(tables.shape[2:], jnp.bfloat16)
    flat_fields = fields.reshape(rows * rhs, nodes)
    cut_fields = fields.reshape(rows, rhs, nodes)
    flat_impedance = impedance.reshape(rows, nodes)
    flat_tiles = tile_data.reshape(local * slots, 2 * block, block)
    share = local * slots // SHARES
    tiles_shape = jax.ShapeDtypeStruct((share + 1, 2 * block, block), tile_data.dtype)
    params = pltpu.CompilerParams(vmem_limit_bytes=VMEM_LIMIT)
    pack_params = pltpu.CompilerParams(vmem_limit_bytes=PACK_VMEM_LIMIT)
    stage_params = pltpu.CompilerParams(vmem_limit_bytes=STAGE_VMEM_LIMIT)
    vmem, smem = pl.BlockSpec(memory_space=pltpu.VMEM), pl.BlockSpec(memory_space=pltpu.SMEM)
    hbm = pl.BlockSpec(memory_space=pltpu.HBM)
    move = 16 * fields.size
    multiply = 4 * rows * rows * parts * per * nodes
    chunk_shape = jax.ShapeDtypeStruct((per, rows, nodes), jnp.int16)

    az = lax.axis_index("az").astype(jnp.int32)[None]
    place = lax.axis_index("curve").astype(jnp.int32)[None]
    first, coded, forward_table, back_table = pl.pallas_call(
        functools.partial(pack_kernel, CHUNKS),
        out_shape=[chunk_shape, jax.ShapeDtypeStruct((rhs, rows, nodes), jnp.int16), table_shape, table_shape],
        in_specs=[smem, hbm, hbm],
        out_specs=[vmem] * 4,
        scratch_shapes=[
            pltpu.VMEM((CHUNKS, rows * per, nodes), jnp.float32),
            pltpu.SemaphoreType.DMA((CHUNKS + 2,)),
        ],
        cost_estimate=cost(0, move),
        compiler_params=pack_params,
        name="pack",
    )(az, cut_fields, tables)

    peer = lax.ppermute(coded, "az", PEER) if paired else None
    find = functools.partial(begin_find, ring)
    find_shapes = [tiles_shape, jax.ShapeDtypeStruct((slots * local,), jnp.int32)]
    find_operands = (after(place, coded), tile_cols[:, 0, :].T, tile_count.reshape(local), flat_tiles)
    if paired:
        near_part, far_part, head, slot = pl.pallas_call(
            functools.partial(split_kernel, per, find),
            out_shape=[jax.ShapeDtypeStruct((per, rows, nodes), jnp.float32), chunk_shape] + find_shapes,
            in_specs=[vmem] * 3 + [smem] * 3 + [hbm],
            out_specs=[vmem] * 3 + [smem],
            scratch_shapes=[pltpu.SemaphoreType.DMA],
            cost_estimate=cost(3 * multiply, move),
            compiler_params=stage_params,
            name="split",
        )(forward_table, coded, peer, *find_operands)
    else:
        head, slot = pl.pallas_call(
            functools.partial(find_kernel, find),
            out_shape=find_shapes,
            in_specs=[smem] * 3 + [hbm],
            out_specs=[vmem, smem],
            scratch_shapes=[pltpu.SemaphoreType.DMA],
            compiler_params=stage_params,
            name="find",
        )(*find_operands)
    tiles = [head]

    sides = [(i, i ^ 1) for i in range(ring)]
    onward = [(i, (i + 2 if i % 2 == 0 else i - 2) % ring) for i in range(ring)]
    modes_shape = jax.ShapeDtypeStruct((local, 2 * per, nodes), jnp.bfloat16)
    held_modes = pltpu.VMEM((per * rows, nodes), jnp.float32)
    owns, earlier = [], None
    for index in range(CHUNKS):
        if paired and index:
            across = after(lax.ppermute(after(far_part, earlier), "az", ACROSS), tiles[-1])
            own = pl.pallas_call(
                finish_kernel,
                out_shape=modes_shape,
                in_specs=[vmem] * 2,
                out_specs=vmem,
                scratch_shapes=[held_modes],
                cost_estimate=cost(0, move // 2),
                compiler_params=params,
                name="finish",
            )(near_part, across)
        else:
            if paired:
                across = after(lax.ppermute(first, "az", ACROSS), far_part)
                earlier = across
                sources = [coded, peer, across, lax.ppermute(across, "az", PEER)]
                firsts = (0,) * parts
            else:
                every = lax.all_gather(coded[index * per : (index + 1) * per], "az")
                sources, firsts = [every[j] for j in range(parts)], (0,) * parts
            own = pl.pallas_call(
                functools.partial(forward_kernel, firsts),
                out_shape=modes_shape,
                in_specs=[vmem] * (1 + parts),
                out_specs=vmem,
                scratch_shapes=[held_modes],
                cost_estimate=cost(3 * multiply, move),
                compiler_params=params,
                name="forward",
            )(forward_table, *sources)
        owns.append(own)
        if index == 0:
            for turn in range(1, SHARES):
                tail = pl.pallas_call(
                    functools.partial(stage_kernel, turn * share),
                    out_shape=tiles_shape,
                    in_specs=[hbm],
                    out_specs=vmem,
                    scratch_shapes=[pltpu.SemaphoreType.DMA],
                    cost_estimate=cost(0, 2 * tile_data.size // SHARES),
                    compiler_params=stage_params,
                    name="stage",
                )(after(flat_tiles, own))
                tiles.append(tail)

    side_in = [lax.ppermute(own, "curve", sides) for own in owns]
    side_in[0] = after(side_in[0], *owns[1:])
    far_in = [lax.ppermute(side, "curve", onward) for side in side_in]
    part_shape = jax.ShapeDtypeStruct((local * 2 * per, nodes), jnp.float32)
    parts_of = pl.pallas_call(
        functools.partial(inner_kernel, CHUNKS),
        out_shape=[part_shape] * CHUNKS,
        in_specs=[smem] + [vmem] * (SHARES + CHUNKS + 1),
        out_specs=[vmem] * CHUNKS,
        cost_estimate=cost(0, tile_data.size),
        compiler_params=params,
        name="inner",
    )(slot, *tiles, *owns, side_in[0])

    nears = []
    for index in range(CHUNKS):
        if index == 0:
            roles, values = (2,), [after(far_in[0], parts_of[0], *side_in[1:])]
        else:
            roles, values = (1, 2), [side_in[index], after(far_in[index], nears[0])]
        nears.append(
            pl.pallas_call(
                functools.partial(outer_kernel, roles),
                out_shape=jax.ShapeDtypeStruct((per, rows, nodes), jnp.bfloat16),
                in_specs=[smem] + [vmem] * (SHARES + len(roles) + 1),
                out_specs=vmem,
                scratch_shapes=[pltpu.VMEM((local * 2 * per, nodes), jnp.float32)],
                cost_estimate=cost(0, tile_data.size // 2),
                compiler_params=params,
                name="outer",
            )(slot, *tiles, *values, parts_of[index])
        )

    out = None
    for index, near in enumerate(nears):
        if paired:
            across = lax.ppermute(near, "az", ACROSS)
            if out is not None:
                across, out = lax.optimization_barrier((across, out))
            elif CHUNKS > 1:
                across = after(across, nears[-1])
            sources = [near, lax.ppermute(near, "az", PEER), across, lax.ppermute(across, "az", PEER)]
        else:
            every = lax.all_gather(near, "az")
            sources = [every[j] for j in range(parts)]
        earlier = [] if out is None else [out]
        out = pl.pallas_call(
            functools.partial(back_kernel, parts, rhs, index),
            out_shape=jax.ShapeDtypeStruct((rows, rhs, nodes), jnp.float32),
            in_specs=[vmem] * (3 + parts) + [hbm] * len(earlier),
            out_specs=hbm,
            scratch_shapes=[pltpu.VMEM((rows * per, nodes), jnp.float32), pltpu.SemaphoreType.DMA],
            input_output_aliases={3 + parts: 0} if earlier else {},
            cost_estimate=cost(2 * multiply, move),
            compiler_params=params,
            name="back",
        )(back_table, flat_fields, flat_impedance, *sources, *earlier)
    return out.reshape(fields.shape)


def solution(mesh):
    placed = (
        P(None, "az", None, "curve"),
        P(None, "az", "curve"),
        P("az", "curve", None, None, None, None),
        P("az", "curve", None),
        P("az", "curve"),
    )
    return jax.shard_map(
        functools.partial(on_device, mesh.shape["az"], mesh.shape["curve"]),
        mesh=mesh,
        in_specs=placed,
        out_specs=P(None, "az", None, "curve"),
        check_vma=False,
    )
```

```python
import functools

import jax
import jax.numpy as jnp
import numpy as np
from jax import lax
from jax.experimental import pallas as pl
from jax.experimental.pallas import tpu as pltpu
from jax.sharding import PartitionSpec as P

CHUNKS = 2
SHARES = 2
FIELD_BOUND = 6.0
PARTIAL_BOUND = 4.25
CODE_TOP = 32767.0
VMEM_LIMIT = 24 * 1024 * 1024
STAGE_VMEM_LIMIT = 42 * 1024 * 1024
PACK_VMEM_LIMIT = 52 * 1024 * 1024


def dft_tables(parts, local, order, inverse):
    period = parts * local
    own = np.arange(local)
    tables = np.zeros((parts, 2 * local, parts * 2 * local), np.float64)
    for a in range(parts):
        rows = a * local + own
        for j in range(parts):
            cols = order(a, j) * local + own
            angle = 2.0 * np.pi / period * ((rows[:, None] * cols[None, :]) % period)
            cosine, sine = np.cos(angle), np.sin(angle)
            if inverse:
                block = np.block([[cosine, -sine], [sine, cosine]])
            else:
                block = np.block([[cosine, sine], [-sine, cosine]]) / period
            tables[a, :, j * 2 * local : (j + 1) * 2 * local] = block
    tables = tables.astype(np.float32)
    high = tables.astype(jnp.bfloat16)
    low = (tables - high.astype(np.float32)).astype(jnp.bfloat16)
    return np.stack([high, low], axis=1)


def encoded(x, bound):
    root = jnp.sqrt(jnp.sqrt(jnp.abs(x) * (1.0 / bound)))
    return jnp.round(jnp.where(x < 0, -root, root) * CODE_TOP).astype(jnp.int32).astype(jnp.int16)


def decoded(code, bound=FIELD_BOUND):
    t = code.astype(jnp.int32).astype(jnp.float32) * (bound**0.25 / CODE_TOP)
    return (t * jnp.abs(t)) * (t * t)


def pack_kernel(chunks, az_ref, fields_ref, tables_ref, first_ref, all_ref, forward_out, back_out, held, sems):
    rows, rhs, nodes = fields_ref.shape
    per = rhs // chunks
    copies = [
        pltpu.make_async_copy(
            fields_ref.at[:, pl.ds(index * per, per), :], held.at[index].reshape(rows, per, nodes), sems.at[index]
        )
        for index in range(chunks)
    ]
    tables = [
        pltpu.make_async_copy(tables_ref.at[az_ref[0], way], out, sems.at[chunks + way])
        for way, out in enumerate((forward_out, back_out))
    ]
    for copy in copies + tables:
        copy.start()
    for index in range(chunks):
        copies[index].wait()
        for r in range(per):
            code = encoded(held[index, pl.ds(r, rows, stride=per), :], FIELD_BOUND)
            all_ref[index * per + r] = code
            if index == 0:
                first_ref[r] = code
    for table in tables:
        table.wait()


def exact_product(table_ref, cols, x):
    high = x.astype(jnp.bfloat16)
    low = (x - high.astype(jnp.float32)).astype(jnp.bfloat16)
    table_high, table_low = table_ref[0, :, cols], table_ref[1, :, cols]
    total = jnp.dot(table_high, high, preferred_element_type=jnp.float32)
    total += jnp.dot(table_low, high, preferred_element_type=jnp.float32)
    return total + jnp.dot(table_high, low, preferred_element_type=jnp.float32)


def write_modes(held, modes_ref):
    local, both = modes_ref.shape[:2]
    rhs, rows = both // 2, 2 * local
    for k in range(local):
        real = held[pl.ds(k, rhs, stride=rows), :]
        imag = held[pl.ds(local + k, rhs, stride=rows), :]
        modes_ref[k] = jnp.concatenate([real, imag], axis=0).astype(jnp.bfloat16)


def split_kernel(first, find, table_ref, own_ref, peer_ref, place_ref, cols_ref, count_ref, tiles_ref,
                 near_ref, far_ref, out_ref, slot_ref, sem):
    copy = find(place_ref, cols_ref, count_ref, tiles_ref, out_ref, slot_ref, sem)
    per, rows, nodes = far_ref.shape
    odd = lax.rem(lax.broadcasted_iota(jnp.int32, (rows, 2 * nodes), 0), 2) == 1
    for r in range(0, per, 2):
        near = jnp.zeros((rows, 2 * nodes), jnp.float32)
        far = jnp.zeros((rows, 2 * nodes), jnp.float32)
        for j, ref in enumerate((own_ref, peer_ref)):
            x = jnp.concatenate([decoded(ref[first + r]), decoded(ref[first + r + 1])], axis=1)
            cols = slice(j * rows, (j + 1) * rows)
            near += exact_product(table_ref, cols, x)
            far += exact_product(table_ref, cols, jnp.where(odd, -x, x))
        code = encoded(far, PARTIAL_BOUND)
        for s in range(2):
            near_ref[r + s] = near[:, s * nodes : (s + 1) * nodes]
            far_ref[r + s] = code[:, s * nodes : (s + 1) * nodes]
    copy.wait()


def finish_kernel(near_ref, far_ref, modes_ref, held):
    per, rows = far_ref.shape[:2]
    for r in range(per):
        held[r * rows : (r + 1) * rows, :] = near_ref[r] + decoded(far_ref[r], PARTIAL_BOUND)
    write_modes(held, modes_ref)


def forward_kernel(firsts, table_ref, *refs):
    sources = len(firsts)
    coded_refs, modes_ref, held = refs[:sources], refs[sources], refs[sources + 1]
    rhs = modes_ref.shape[1] // 2
    rows, nodes = coded_refs[0].shape[1:]
    for r in range(0, rhs, 2):
        total = jnp.zeros((rows, 2 * nodes), jnp.float32)
        for j in range(sources):
            at = firsts[j] + r
            x = jnp.concatenate([decoded(coded_refs[j][at]), decoded(coded_refs[j][at + 1])], axis=1)
            total += exact_product(table_ref, slice(j * rows, (j + 1) * rows), x)
        held[r * rows : (r + 1) * rows, :] = total[:, :nodes]
        held[(r + 1) * rows : (r + 2) * rows, :] = total[:, nodes:]
    write_modes(held, modes_ref)


def stage_kernel(first, tiles_ref, out_ref, sem):
    share = out_ref.shape[0] - 1
    copy = pltpu.make_async_copy(tiles_ref.at[pl.ds(first, share)], out_ref.at[pl.ds(0, share)], sem)
    copy.start()
    out_ref[share] = jnp.zeros(out_ref.shape[1:], out_ref.dtype)
    copy.wait()


def begin_find(ring, place_ref, cols_ref, count_ref, tiles_ref, out_ref, slot_ref, sem):
    slots, modes = cols_ref.shape
    share = out_ref.shape[0] - 1
    copy = pltpu.make_async_copy(tiles_ref.at[pl.ds(0, share)], out_ref.at[pl.ds(0, share)], sem)
    copy.start()
    out_ref[share] = jnp.zeros(out_ref.shape[1:], out_ref.dtype)
    place = place_ref[0]
    even = lax.rem(place, 2) == 0
    side = jnp.where(even, place + 1, place - 1)
    far = lax.rem(jnp.where(even, place - 1, place + 1) + ring, ring)

    def find(k, carry):
        base = lax.rem(k, share // slots) * slots
        for role, wanted in enumerate((place, side, far)):
            slot = jnp.where(cols_ref[0, k] == wanted, 0, jnp.where(cols_ref[1, k] == wanted, 1, 2))
            slot_ref[role * modes + k] = jnp.where(slot < count_ref[k], base + slot, share)
        return carry

    lax.fori_loop(0, modes, find, 0)
    return copy


def find_kernel(find, *refs):
    find(*refs).wait()


def chosen(slot_ref, modes, roles):
    group = min(16, modes)
    for first in range(0, modes, group):
        places = [[slot_ref[role * modes + first + k] for role in roles] for k in range(group)]
        for k in range(group):
            yield first + k, places[k]


def tile_product(tiles_ref, places, values):
    return lax.dot_general(
        jnp.concatenate(values, axis=1),
        jnp.concatenate([tiles_ref[place] for place in places], axis=1),
        (((1,), (1,)), ((), ())),
        preferred_element_type=jnp.float32,
    )


def combined(product):
    rhs, block = product.shape[0] // 2, product.shape[1] // 2
    real = product[:rhs, :block] - product[rhs:, block:]
    imag = product[rhs:, :block] + product[:rhs, block:]
    return real, imag


def put(out_ref, k, both, real, imag):
    out_ref[k * both : k * both + both // 2, :] = real
    out_ref[k * both + both // 2 : (k + 1) * both, :] = imag


def inner_kernel(chunks, slot_ref, *refs):
    own_refs, side_ref, part_refs = refs[-2 * chunks - 1 : -chunks - 1], refs[-chunks - 1], refs[-chunks:]
    tile_refs = refs[: -2 * chunks - 1]
    modes, both = side_ref.shape[:2]
    for k, (own_place, side_place) in chosen(slot_ref, modes, (0, 1)):
        tiles_ref = tile_refs[k * len(tile_refs) // modes]
        owns = jnp.concatenate([ref[k] for ref in own_refs], axis=0)
        product = tile_product(tiles_ref, [own_place], [owns])
        side = tile_product(tiles_ref, [side_place], [side_ref[k]])
        for index, part_ref in enumerate(part_refs):
            mine = product[index * both : (index + 1) * both]
            put(part_ref, k, both, *combined(mine + side if index == 0 else mine))


def outer_kernel(roles, slot_ref, *refs):
    count = len(roles)
    tile_refs, value_refs, (part_ref, near_ref, held) = refs[: -3 - count], refs[-3 - count : -3], refs[-3:]
    modes, both = value_refs[0].shape[:2]
    rhs = both // 2
    for k, places in chosen(slot_ref, modes, roles):
        tiles_ref = tile_refs[k * len(tile_refs) // modes]
        real, imag = combined(tile_product(tiles_ref, places, [ref[k] for ref in value_refs]))
        at_real, at_imag = slice(k * both, k * both + rhs), slice(k * both + rhs, (k + 1) * both)
        held[at_real, :] = real + part_ref[at_real, :]
        held[at_imag, :] = imag + part_ref[at_imag, :]
    for r in range(rhs):
        for part in range(2):
            rows = slice(part * modes, (part + 1) * modes)
            near_ref[r, rows, :] = held[pl.ds(part * rhs + r, modes, stride=both), :].astype(jnp.bfloat16)


def back_product(table_ref, near_refs, terms, r):
    rows = near_refs[0].shape[1]
    total = None
    for j, ref in zip(terms, near_refs):
        x = jnp.concatenate([ref[r], ref[r + 1]], axis=1)
        for way in range(2):
            product = jnp.dot(
                table_ref[way, :, j * rows : (j + 1) * rows], x, preferred_element_type=jnp.float32
            )
            total = product if total is None else total + product
    return total


def back_kernel(sources, ahead, chunk, starts, table_ref, fields_ref, impedance_ref, *refs):
    given, next_refs, refs = refs[:sources], refs[sources : sources + ahead], refs[sources + ahead :]
    if starts:
        ready_ref, refs = refs[0], refs[1:]
    if ahead:
        out_ref, next_out, held, sem = refs[-4:]
    else:
        out_ref, held, sem = refs[-3:]
    per, rows, nodes = given[0].shape
    rhs = fields_ref.shape[0] // rows
    local = rows // 2
    z_real, z_imag = impedance_ref[:local], impedance_ref[local:]
    for r in range(0, per, 2):
        total = back_product(table_ref, given, range(starts, starts + sources), r)
        if starts:
            total += ready_ref[r // 2]
        for s in range(2):
            real, imag = total[:local, s * nodes : (s + 1) * nodes], total[local:, s * nodes : (s + 1) * nodes]
            from_row = chunk * per + r + s
            f_real = fields_ref[pl.ds(from_row, local, stride=rhs), :]
            f_imag = fields_ref[pl.ds(local * rhs + from_row, local, stride=rhs), :]
            held[pl.ds(r + s, local, stride=per), :] = f_real + z_real * real - z_imag * imag
            held[pl.ds(local * per + r + s, local, stride=per), :] = f_imag + z_real * imag + z_imag * real
    copy = pltpu.make_async_copy(
        held.reshape(rows, per, nodes), out_ref.at[:, pl.ds(chunk * per, per), :], sem
    )
    copy.start()
    if ahead:
        for r in range(0, per, 2):
            next_out[r // 2] = back_product(table_ref, next_refs, range(ahead), r)
    copy.wait()


PEER = [(i, i ^ 1) for i in range(4)]
ACROSS = [(i, i ^ 2) for i in range(4)]


def after(x, *earlier):
    return lax.optimization_barrier((x,) + earlier)[0]


def cost(flops, moved):
    return pl.CostEstimate(flops=flops, bytes_accessed=moved, transcendentals=0)


def on_device(parts, ring, fields, impedance, tile_data, tile_cols, tile_count):
    _, local, rhs, nodes = fields.shape
    per = rhs // CHUNKS
    slots, block = tile_data.shape[2], tile_data.shape[-1]
    rows = 2 * local
    paired = parts == 4
    order = (lambda a, j: a ^ j) if paired else (lambda a, j: j)
    tables = jnp.asarray(
        np.stack([dft_tables(parts, local, order, False), dft_tables(parts, local, order, True)], axis=1)
    )
    table_shape = jax.ShapeDtypeStruct(tables.shape[2:], jnp.bfloat16)
    flat_fields = fields.reshape(rows * rhs, nodes)
    cut_fields = fields.reshape(rows, rhs, nodes)
    flat_impedance = impedance.reshape(rows, nodes)
    flat_tiles = tile_data.reshape(local * slots, 2 * block, block)
    share = local * slots // SHARES
    tiles_shape = jax.ShapeDtypeStruct((share + 1, 2 * block, block), tile_data.dtype)
    params = pltpu.CompilerParams(vmem_limit_bytes=VMEM_LIMIT)
    pack_params = pltpu.CompilerParams(vmem_limit_bytes=PACK_VMEM_LIMIT)
    stage_params = pltpu.CompilerParams(vmem_limit_bytes=STAGE_VMEM_LIMIT)
    vmem, smem = pl.BlockSpec(memory_space=pltpu.VMEM), pl.BlockSpec(memory_space=pltpu.SMEM)
    hbm = pl.BlockSpec(memory_space=pltpu.HBM)
    move = 16 * fields.size
    multiply = 4 * rows * rows * parts * per * nodes
    chunk_shape = jax.ShapeDtypeStruct((per, rows, nodes), jnp.int16)

    az = lax.axis_index("az").astype(jnp.int32)[None]
    place = lax.axis_index("curve").astype(jnp.int32)[None]
    first, coded, forward_table, back_table = pl.pallas_call(
        functools.partial(pack_kernel, CHUNKS),
        out_shape=[chunk_shape, jax.ShapeDtypeStruct((rhs, rows, nodes), jnp.int16), table_shape, table_shape],
        in_specs=[smem, hbm, hbm],
        out_specs=[vmem] * 4,
        scratch_shapes=[
            pltpu.VMEM((CHUNKS, rows * per, nodes), jnp.float32),
            pltpu.SemaphoreType.DMA((CHUNKS + 2,)),
        ],
        cost_estimate=cost(0, move),
        compiler_params=pack_params,
        name="pack",
    )(az, cut_fields, tables)

    peer = lax.ppermute(coded, "az", PEER) if paired else None
    find = functools.partial(begin_find, ring)
    find_shapes = [tiles_shape, jax.ShapeDtypeStruct((slots * local,), jnp.int32)]
    find_operands = (after(place, coded), tile_cols[:, 0, :].T, tile_count.reshape(local), flat_tiles)
    if paired:
        near_part, far_part, head, slot = pl.pallas_call(
            functools.partial(split_kernel, per, find),
            out_shape=[jax.ShapeDtypeStruct((per, rows, nodes), jnp.float32), chunk_shape] + find_shapes,
            in_specs=[vmem] * 3 + [smem] * 3 + [hbm],
            out_specs=[vmem] * 3 + [smem],
            scratch_shapes=[pltpu.SemaphoreType.DMA],
            cost_estimate=cost(3 * multiply, move),
            compiler_params=stage_params,
            name="split",
        )(forward_table, coded, peer, *find_operands)
    else:
        head, slot = pl.pallas_call(
            functools.partial(find_kernel, find),
            out_shape=find_shapes,
            in_specs=[smem] * 3 + [hbm],
            out_specs=[vmem, smem],
            scratch_shapes=[pltpu.SemaphoreType.DMA],
            compiler_params=stage_params,
            name="find",
        )(*find_operands)
    tiles = [head]

    sides = [(i, i ^ 1) for i in range(ring)]
    onward = [(i, (i + 2 if i % 2 == 0 else i - 2) % ring) for i in range(ring)]
    modes_shape = jax.ShapeDtypeStruct((local, 2 * per, nodes), jnp.bfloat16)
    held_modes = pltpu.VMEM((per * rows, nodes), jnp.float32)
    owns, earlier = [], None
    for index in range(CHUNKS):
        if paired and index:
            across = after(lax.ppermute(after(far_part, earlier), "az", ACROSS), tiles[-1])
            own = pl.pallas_call(
                finish_kernel,
                out_shape=modes_shape,
                in_specs=[vmem] * 2,
                out_specs=vmem,
                scratch_shapes=[held_modes],
                cost_estimate=cost(0, move // 2),
                compiler_params=params,
                name="finish",
            )(near_part, across)
        else:
            if paired:
                across = after(lax.ppermute(first, "az", ACROSS), far_part)
                earlier = across
                sources = [coded, peer, across, lax.ppermute(across, "az", PEER)]
                firsts = (0,) * parts
            else:
                every = lax.all_gather(coded[index * per : (index + 1) * per], "az")
                sources, firsts = [every[j] for j in range(parts)], (0,) * parts
            own = pl.pallas_call(
                functools.partial(forward_kernel, firsts),
                out_shape=modes_shape,
                in_specs=[vmem] * (1 + parts),
                out_specs=vmem,
                scratch_shapes=[held_modes],
                cost_estimate=cost(3 * multiply, move),
                compiler_params=params,
                name="forward",
            )(forward_table, *sources)
        owns.append(own)
        if index == 0:
            for turn in range(1, SHARES):
                tail = pl.pallas_call(
                    functools.partial(stage_kernel, turn * share),
                    out_shape=tiles_shape,
                    in_specs=[hbm],
                    out_specs=vmem,
                    scratch_shapes=[pltpu.SemaphoreType.DMA],
                    cost_estimate=cost(0, 2 * tile_data.size // SHARES),
                    compiler_params=stage_params,
                    name="stage",
                )(after(flat_tiles, own))
                tiles.append(tail)

    side_in = [lax.ppermute(own, "curve", sides) for own in owns]
    side_in[0] = after(side_in[0], *owns[1:])
    far_in = [lax.ppermute(side, "curve", onward) for side in side_in]
    part_shape = jax.ShapeDtypeStruct((local * 2 * per, nodes), jnp.float32)
    parts_of = pl.pallas_call(
        functools.partial(inner_kernel, CHUNKS),
        out_shape=[part_shape] * CHUNKS,
        in_specs=[smem] + [vmem] * (SHARES + CHUNKS + 1),
        out_specs=[vmem] * CHUNKS,
        cost_estimate=cost(0, tile_data.size),
        compiler_params=params,
        name="inner",
    )(slot, *tiles, *owns, side_in[0])

    nears = []
    for index in range(CHUNKS):
        if index == 0:
            roles, values = (2,), [after(far_in[0], parts_of[0], *side_in[1:])]
        else:
            roles, values = (1, 2), [side_in[index], after(far_in[index], nears[0])]
        nears.append(
            pl.pallas_call(
                functools.partial(outer_kernel, roles),
                out_shape=jax.ShapeDtypeStruct((per, rows, nodes), jnp.bfloat16),
                in_specs=[smem] + [vmem] * (SHARES + len(roles) + 1),
                out_specs=vmem,
                scratch_shapes=[pltpu.VMEM((local * 2 * per, nodes), jnp.float32)],
                cost_estimate=cost(0, tile_data.size // 2),
                compiler_params=params,
                name="outer",
            )(slot, *tiles, *values, parts_of[index])
        )

    peers = [lax.ppermute(near, "az", PEER) for near in nears] if paired else []
    out, ready = None, None
    for index, near in enumerate(nears):
        starts, ahead = 0, 0
        if paired:
            across = lax.ppermute(near, "az", ACROSS)
            if index:
                starts = 2
                across, out, ready = lax.optimization_barrier((across, out, ready))
                given = [across, lax.ppermute(across, "az", PEER), ready, out]
            else:
                across = after(across, nears[-1])
                given = [near, peers[0], across, lax.ppermute(across, "az", PEER)]
            if index + 1 < CHUNKS:
                ahead = 2
                given[4 - starts : 4 - starts] = [nears[index + 1], peers[index + 1]]
        else:
            every = lax.all_gather(near, "az")
            given = [every[j] for j in range(parts)] + ([] if out is None else [out])
        operands = [back_table, flat_fields, flat_impedance] + given
        results = pl.pallas_call(
            functools.partial(back_kernel, parts - starts, ahead, index, starts),
            out_shape=[jax.ShapeDtypeStruct((rows, rhs, nodes), jnp.float32)]
            + [jax.ShapeDtypeStruct((per // 2, rows, 2 * nodes), jnp.float32)] * (ahead > 0),
            in_specs=[vmem] * (len(operands) - (out is not None)) + [hbm] * (out is not None),
            out_specs=[hbm] + [vmem] * (ahead > 0),
            scratch_shapes=[pltpu.VMEM((rows * per, nodes), jnp.float32), pltpu.SemaphoreType.DMA],
            input_output_aliases={} if out is None else {len(operands) - 1: 0},
            cost_estimate=cost(2 * multiply, move),
            compiler_params=params,
            name="back",
        )(*operands)
        out, ready = results[0], results[-1]
    return out.reshape(fields.shape)


def solution(mesh):
    placed = (
        P(None, "az", None, "curve"),
        P(None, "az", "curve"),
        P("az", "curve", None, None, None, None),
        P("az", "curve", None),
        P("az", "curve"),
    )
    return jax.shard_map(
        functools.partial(on_device, mesh.shape["az"], mesh.shape["curve"]),
        mesh=mesh,
        in_specs=placed,
        out_specs=P(None, "az", None, "curve"),
        check_vma=False,
    )
```

```python
import functools

import jax
import jax.numpy as jnp
import numpy as np
from jax import lax
from jax.experimental import pallas as pl
from jax.experimental.pallas import tpu as pltpu
from jax.sharding import PartitionSpec as P

CHUNKS = 2
SHARES = 2
FIELD_BOUND = 6.0
PARTIAL_BOUND = 4.25
CODE_TOP = 32767.0
VMEM_LIMIT = 24 * 1024 * 1024
STAGE_VMEM_LIMIT = 42 * 1024 * 1024
PACK_VMEM_LIMIT = 52 * 1024 * 1024


def dft_tables(parts, local, order, inverse):
    period = parts * local
    own = np.arange(local)
    tables = np.zeros((parts, 2 * local, parts * 2 * local), np.float64)
    for a in range(parts):
        rows = a * local + own
        for j in range(parts):
            cols = order(a, j) * local + own
            angle = 2.0 * np.pi / period * ((rows[:, None] * cols[None, :]) % period)
            cosine, sine = np.cos(angle), np.sin(angle)
            if inverse:
                block = np.block([[cosine, -sine], [sine, cosine]])
            else:
                block = np.block([[cosine, sine], [-sine, cosine]]) / period
            tables[a, :, j * 2 * local : (j + 1) * 2 * local] = block
    tables = tables.astype(np.float32)
    high = tables.astype(jnp.bfloat16)
    low = (tables - high.astype(np.float32)).astype(jnp.bfloat16)
    return np.stack([high, low], axis=1)


def encoded(x, bound):
    root = jnp.sqrt(jnp.sqrt(jnp.abs(x) * (1.0 / bound)))
    return jnp.round(jnp.where(x < 0, -root, root) * CODE_TOP).astype(jnp.int32).astype(jnp.int16)


def decoded(code, bound=FIELD_BOUND):
    t = code.astype(jnp.int32).astype(jnp.float32) * (bound**0.25 / CODE_TOP)
    return (t * jnp.abs(t)) * (t * t)


def pack_kernel(chunks, az_ref, fields_ref, tables_ref, first_ref, all_ref, forward_out, back_out, held, sems):
    rows, rhs, nodes = fields_ref.shape
    per = rhs // chunks
    copies = [
        pltpu.make_async_copy(
            fields_ref.at[:, pl.ds(index * per, per), :], held.at[index].reshape(rows, per, nodes), sems.at[index]
        )
        for index in range(chunks)
    ]
    tables = [
        pltpu.make_async_copy(tables_ref.at[az_ref[0], way], out, sems.at[chunks + way])
        for way, out in enumerate((forward_out, back_out))
    ]
    for copy in copies + tables:
        copy.start()
    for index in range(chunks):
        copies[index].wait()
        for r in range(per):
            code = encoded(held[index, pl.ds(r, rows, stride=per), :], FIELD_BOUND)
            all_ref[index * per + r] = code
            if index == 0:
                first_ref[r] = code
    for table in tables:
        table.wait()


def exact_product(table_ref, cols, x):
    high = x.astype(jnp.bfloat16)
    low = (x - high.astype(jnp.float32)).astype(jnp.bfloat16)
    table_high, table_low = table_ref[0, :, cols], table_ref[1, :, cols]
    total = jnp.dot(table_high, high, preferred_element_type=jnp.float32)
    total += jnp.dot(table_low, high, preferred_element_type=jnp.float32)
    return total + jnp.dot(table_high, low, preferred_element_type=jnp.float32)


def write_modes(held, modes_ref):
    local, both = modes_ref.shape[:2]
    rhs, rows = both // 2, 2 * local
    for k in range(local):
        real = held[pl.ds(k, rhs, stride=rows), :]
        imag = held[pl.ds(local + k, rhs, stride=rows), :]
        modes_ref[k] = jnp.concatenate([real, imag], axis=0).astype(jnp.bfloat16)


def split_kernel(first, sort, table_ref, own_ref, peer_ref, place_ref, cols_ref, count_ref, tiles_ref,
                 near_ref, far_ref, out_ref, live_ref, sem):
    copy = sort(place_ref, cols_ref, count_ref, tiles_ref, out_ref, live_ref, sem)
    per, rows, nodes = far_ref.shape
    odd = lax.rem(lax.broadcasted_iota(jnp.int32, (rows, 2 * nodes), 0), 2) == 1
    for r in range(0, per, 2):
        near = jnp.zeros((rows, 2 * nodes), jnp.float32)
        far = jnp.zeros((rows, 2 * nodes), jnp.float32)
        for j, ref in enumerate((own_ref, peer_ref)):
            x = jnp.concatenate([decoded(ref[first + r]), decoded(ref[first + r + 1])], axis=1)
            cols = slice(j * rows, (j + 1) * rows)
            near += exact_product(table_ref, cols, x)
            far += exact_product(table_ref, cols, jnp.where(odd, -x, x))
        code = encoded(far, PARTIAL_BOUND)
        for s in range(2):
            near_ref[r + s] = near[:, s * nodes : (s + 1) * nodes]
            far_ref[r + s] = code[:, s * nodes : (s + 1) * nodes]
    copy.wait()


def finish_kernel(near_ref, far_ref, modes_ref, held):
    per, rows = far_ref.shape[:2]
    for r in range(per):
        held[r * rows : (r + 1) * rows, :] = near_ref[r] + decoded(far_ref[r], PARTIAL_BOUND)
    write_modes(held, modes_ref)


def forward_kernel(firsts, table_ref, *refs):
    sources = len(firsts)
    coded_refs, modes_ref, held = refs[:sources], refs[sources], refs[sources + 1]
    rhs = modes_ref.shape[1] // 2
    rows, nodes = coded_refs[0].shape[1:]
    for r in range(0, rhs, 2):
        total = jnp.zeros((rows, 2 * nodes), jnp.float32)
        for j in range(sources):
            at = firsts[j] + r
            x = jnp.concatenate([decoded(coded_refs[j][at]), decoded(coded_refs[j][at + 1])], axis=1)
            total += exact_product(table_ref, slice(j * rows, (j + 1) * rows), x)
        held[r * rows : (r + 1) * rows, :] = total[:, :nodes]
        held[(r + 1) * rows : (r + 2) * rows, :] = total[:, nodes:]
    write_modes(held, modes_ref)


def begin_sort(first, place_ref, cols_ref, count_ref, tiles_ref, out_ref, live_ref, sem):
    slots, modes = cols_ref.shape
    share = out_ref.shape[1]
    place = place_ref[0]
    even = lax.rem(place, 2) == 0
    side = jnp.where(even, place + 1, place - 1)

    def begin(k, carry):
        mode = first + k
        for t in range(slots):
            block = cols_ref[t, mode]
            role = jnp.where(block == place, 0, jnp.where(block == side, 1, 2))
            pltpu.make_async_copy(tiles_ref.at[mode * slots + t], out_ref.at[role, k], sem).start()
            live_ref[role * share + k] = (t < count_ref[mode]).astype(jnp.int32)
        return carry

    lax.fori_loop(0, share, begin, 0)
    return pltpu.make_async_copy(out_ref, out_ref, sem)


def sort_kernel(sort, *refs):
    sort(*refs).wait()


def tile_product(tiles_ref, live_ref, k, roles, values):
    share = tiles_ref.shape[1]
    kept = []
    for role, value in zip(roles, values):
        kept.append(jnp.where(live_ref[role * share + k] == 0, jnp.zeros_like(value), value))
    return lax.dot_general(
        jnp.concatenate(kept, axis=1),
        jnp.concatenate([tiles_ref[role, k] for role in roles], axis=1),
        (((1,), (1,)), ((), ())),
        preferred_element_type=jnp.float32,
    )


def combined(product):
    rhs, block = product.shape[0] // 2, product.shape[1] // 2
    real = product[:rhs, :block] - product[rhs:, block:]
    imag = product[rhs:, :block] + product[:rhs, block:]
    return real, imag


def put(out_ref, k, both, real, imag):
    out_ref[k * both : k * both + both // 2, :] = real
    out_ref[k * both + both // 2 : (k + 1) * both, :] = imag


def inner_kernel(chunks, shares, *refs):
    live_refs, tile_refs, refs = refs[:shares], refs[shares : 2 * shares], refs[2 * shares :]
    own_refs, side_ref, part_refs = refs[:chunks], refs[chunks], refs[chunks + 1 :]
    modes, both = side_ref.shape[:2]
    for k in range(modes):
        turn, at = divmod(k, modes // shares)
        owns = jnp.concatenate([ref[k] for ref in own_refs], axis=0)
        product = tile_product(tile_refs[turn], live_refs[turn], at, (0,), [owns])
        side = tile_product(tile_refs[turn], live_refs[turn], at, (1,), [side_ref[k]])
        for index, part_ref in enumerate(part_refs):
            mine = product[index * both : (index + 1) * both]
            put(part_ref, k, both, *combined(mine + side if index == 0 else mine))


def outer_kernel(roles, shares, *refs):
    live_refs, tile_refs, refs = refs[:shares], refs[shares : 2 * shares], refs[2 * shares :]
    value_refs, (part_ref, near_ref, held) = refs[:-3], refs[-3:]
    modes, both = value_refs[0].shape[:2]
    rhs = both // 2
    for k in range(modes):
        turn, at = divmod(k, modes // shares)
        values = [ref[k] for ref in value_refs]
        real, imag = combined(tile_product(tile_refs[turn], live_refs[turn], at, roles, values))
        at_real, at_imag = slice(k * both, k * both + rhs), slice(k * both + rhs, (k + 1) * both)
        held[at_real, :] = real + part_ref[at_real, :]
        held[at_imag, :] = imag + part_ref[at_imag, :]
    for r in range(rhs):
        for part in range(2):
            rows = slice(part * modes, (part + 1) * modes)
            near_ref[r, rows, :] = held[pl.ds(part * rhs + r, modes, stride=both), :].astype(jnp.bfloat16)


def back_product(table_ref, near_refs, terms, r):
    rows = near_refs[0].shape[1]
    total = None
    for j, ref in zip(terms, near_refs):
        x = jnp.concatenate([ref[r], ref[r + 1]], axis=1)
        for way in range(2):
            product = jnp.dot(
                table_ref[way, :, j * rows : (j + 1) * rows], x, preferred_element_type=jnp.float32
            )
            total = product if total is None else total + product
    return total


def back_kernel(sources, ahead, chunk, starts, table_ref, fields_ref, impedance_ref, *refs):
    given, next_refs, refs = refs[:sources], refs[sources : sources + ahead], refs[sources + ahead :]
    if starts:
        ready_ref, refs = refs[0], refs[1:]
    if ahead:
        out_ref, next_out, held, sem = refs[-4:]
    else:
        out_ref, held, sem = refs[-3:]
    per, rows, nodes = given[0].shape
    rhs = fields_ref.shape[0] // rows
    local = rows // 2
    z_real, z_imag = impedance_ref[:local], impedance_ref[local:]
    for r in range(0, per, 2):
        total = back_product(table_ref, given, range(starts, starts + sources), r)
        if starts:
            total += ready_ref[r // 2]
        for s in range(2):
            real, imag = total[:local, s * nodes : (s + 1) * nodes], total[local:, s * nodes : (s + 1) * nodes]
            from_row = chunk * per + r + s
            f_real = fields_ref[pl.ds(from_row, local, stride=rhs), :]
            f_imag = fields_ref[pl.ds(local * rhs + from_row, local, stride=rhs), :]
            held[pl.ds(r + s, local, stride=per), :] = f_real + z_real * real - z_imag * imag
            held[pl.ds(local * per + r + s, local, stride=per), :] = f_imag + z_real * imag + z_imag * real
    copy = pltpu.make_async_copy(
        held.reshape(rows, per, nodes), out_ref.at[:, pl.ds(chunk * per, per), :], sem
    )
    copy.start()
    if ahead:
        for r in range(0, per, 2):
            next_out[r // 2] = back_product(table_ref, next_refs, range(ahead), r)
    copy.wait()


PEER = [(i, i ^ 1) for i in range(4)]
ACROSS = [(i, i ^ 2) for i in range(4)]


def after(x, *earlier):
    return lax.optimization_barrier((x,) + earlier)[0]


def cost(flops, moved):
    return pl.CostEstimate(flops=flops, bytes_accessed=moved, transcendentals=0)


def on_device(parts, ring, fields, impedance, tile_data, tile_cols, tile_count):
    _, local, rhs, nodes = fields.shape
    per = rhs // CHUNKS
    slots, block = tile_data.shape[2], tile_data.shape[-1]
    rows = 2 * local
    paired = parts == 4
    order = (lambda a, j: a ^ j) if paired else (lambda a, j: j)
    tables = jnp.asarray(
        np.stack([dft_tables(parts, local, order, False), dft_tables(parts, local, order, True)], axis=1)
    )
    table_shape = jax.ShapeDtypeStruct(tables.shape[2:], jnp.bfloat16)
    flat_fields = fields.reshape(rows * rhs, nodes)
    cut_fields = fields.reshape(rows, rhs, nodes)
    flat_impedance = impedance.reshape(rows, nodes)
    flat_tiles = tile_data.reshape(local * slots, 2 * block, block)
    share = local // SHARES
    sort_shapes = [
        jax.ShapeDtypeStruct((slots, share, 2 * block, block), tile_data.dtype),
        jax.ShapeDtypeStruct((slots * share,), jnp.int32),
    ]
    params = pltpu.CompilerParams(vmem_limit_bytes=VMEM_LIMIT)
    pack_params = pltpu.CompilerParams(vmem_limit_bytes=PACK_VMEM_LIMIT)
    stage_params = pltpu.CompilerParams(vmem_limit_bytes=STAGE_VMEM_LIMIT)
    vmem, smem = pl.BlockSpec(memory_space=pltpu.VMEM), pl.BlockSpec(memory_space=pltpu.SMEM)
    hbm = pl.BlockSpec(memory_space=pltpu.HBM)
    move = 16 * fields.size
    multiply = 4 * rows * rows * parts * per * nodes
    chunk_shape = jax.ShapeDtypeStruct((per, rows, nodes), jnp.int16)

    az = lax.axis_index("az").astype(jnp.int32)[None]
    place = lax.axis_index("curve").astype(jnp.int32)[None]
    first, coded, forward_table, back_table = pl.pallas_call(
        functools.partial(pack_kernel, CHUNKS),
        out_shape=[chunk_shape, jax.ShapeDtypeStruct((rhs, rows, nodes), jnp.int16), table_shape, table_shape],
        in_specs=[smem, hbm, hbm],
        out_specs=[vmem] * 4,
        scratch_shapes=[
            pltpu.VMEM((CHUNKS, rows * per, nodes), jnp.float32),
            pltpu.SemaphoreType.DMA((CHUNKS + 2,)),
        ],
        cost_estimate=cost(0, move),
        compiler_params=pack_params,
        name="pack",
    )(az, cut_fields, tables)

    peer = lax.ppermute(coded, "az", PEER) if paired else None
    pattern = (tile_cols[:, 0, :].T, tile_count.reshape(local))

    def sorting(turn, wait_for):
        return pl.pallas_call(
            functools.partial(sort_kernel, functools.partial(begin_sort, turn * share)),
            out_shape=sort_shapes,
            in_specs=[smem] * 3 + [hbm],
            out_specs=[vmem, smem],
            scratch_shapes=[pltpu.SemaphoreType.DMA],
            cost_estimate=cost(0, 2 * tile_data.size // SHARES),
            compiler_params=stage_params,
            name="sort",
        )(after(place, wait_for), *pattern, flat_tiles)

    if paired:
        near_part, far_part, head, live = pl.pallas_call(
            functools.partial(split_kernel, per, functools.partial(begin_sort, 0)),
            out_shape=[jax.ShapeDtypeStruct((per, rows, nodes), jnp.float32), chunk_shape] + sort_shapes,
            in_specs=[vmem] * 3 + [smem] * 3 + [hbm],
            out_specs=[vmem] * 3 + [smem],
            scratch_shapes=[pltpu.SemaphoreType.DMA],
            cost_estimate=cost(3 * multiply, move),
            compiler_params=stage_params,
            name="split",
        )(forward_table, coded, peer, after(place, coded), *pattern, flat_tiles)
    else:
        head, live = sorting(0, coded)
    tiles, lives = [head], [live]

    sides = [(i, i ^ 1) for i in range(ring)]
    onward = [(i, (i + 2 if i % 2 == 0 else i - 2) % ring) for i in range(ring)]
    modes_shape = jax.ShapeDtypeStruct((local, 2 * per, nodes), jnp.bfloat16)
    held_modes = pltpu.VMEM((per * rows, nodes), jnp.float32)
    owns, earlier = [], None
    for index in range(CHUNKS):
        if paired and index:
            across = after(lax.ppermute(after(far_part, earlier), "az", ACROSS), tiles[-1])
            own = pl.pallas_call(
                finish_kernel,
                out_shape=modes_shape,
                in_specs=[vmem] * 2,
                out_specs=vmem,
                scratch_shapes=[held_modes],
                cost_estimate=cost(0, move // 2),
                compiler_params=params,
                name="finish",
            )(near_part, across)
        else:
            if paired:
                across = after(lax.ppermute(first, "az", ACROSS), far_part)
                earlier = across
                sources = [coded, peer, across, lax.ppermute(across, "az", PEER)]
                firsts = (0,) * parts
            else:
                every = lax.all_gather(coded[index * per : (index + 1) * per], "az")
                sources, firsts = [every[j] for j in range(parts)], (0,) * parts
            own = pl.pallas_call(
                functools.partial(forward_kernel, firsts),
                out_shape=modes_shape,
                in_specs=[vmem] * (1 + parts),
                out_specs=vmem,
                scratch_shapes=[held_modes],
                cost_estimate=cost(3 * multiply, move),
                compiler_params=params,
                name="forward",
            )(forward_table, *sources)
        owns.append(own)
        if index == 0:
            for turn in range(1, SHARES):
                tail, live = sorting(turn, own)
                tiles.append(tail)
                lives.append(live)

    side_in = [lax.ppermute(own, "curve", sides) for own in owns]
    side_in[0] = after(side_in[0], *owns[1:])
    far_in = [lax.ppermute(side, "curve", onward) for side in side_in]
    part_shape = jax.ShapeDtypeStruct((local * 2 * per, nodes), jnp.float32)
    parts_of = pl.pallas_call(
        functools.partial(inner_kernel, CHUNKS, SHARES),
        out_shape=[part_shape] * CHUNKS,
        in_specs=[smem] * SHARES + [vmem] * (SHARES + CHUNKS + 1),
        out_specs=[vmem] * CHUNKS,
        cost_estimate=cost(0, tile_data.size),
        compiler_params=params,
        name="inner",
    )(*lives, *tiles, *owns, side_in[0])

    nears = []
    for index in range(CHUNKS):
        if index == 0:
            roles, values = (2,), [after(far_in[0], parts_of[0], *side_in[1:])]
        else:
            roles, values = (1, 2), [side_in[index], after(far_in[index], nears[0])]
        nears.append(
            pl.pallas_call(
                functools.partial(outer_kernel, roles, SHARES),
                out_shape=jax.ShapeDtypeStruct((per, rows, nodes), jnp.bfloat16),
                in_specs=[smem] * SHARES + [vmem] * (SHARES + len(roles) + 1),
                out_specs=vmem,
                scratch_shapes=[pltpu.VMEM((local * 2 * per, nodes), jnp.float32)],
                cost_estimate=cost(0, tile_data.size // 2),
                compiler_params=params,
                name="outer",
            )(*lives, *tiles, *values, parts_of[index])
        )

    peers = [lax.ppermute(near, "az", PEER) for near in nears] if paired else []
    out, ready = None, None
    for index, near in enumerate(nears):
        starts, ahead = 0, 0
        if paired:
            across = lax.ppermute(near, "az", ACROSS)
            if index:
                starts = 2
                across, out, ready = lax.optimization_barrier((across, out, ready))
                given = [across, lax.ppermute(across, "az", PEER), ready, out]
            else:
                across = after(across, nears[-1])
                given = [near, peers[0], across, lax.ppermute(across, "az", PEER)]
            if index + 1 < CHUNKS:
                ahead = 2
                given[4 - starts : 4 - starts] = [nears[index + 1], peers[index + 1]]
        else:
            every = lax.all_gather(near, "az")
            given = [every[j] for j in range(parts)] + ([] if out is None else [out])
        operands = [back_table, flat_fields, flat_impedance] + given
        results = pl.pallas_call(
            functools.partial(back_kernel, parts - starts, ahead, index, starts),
            out_shape=[jax.ShapeDtypeStruct((rows, rhs, nodes), jnp.float32)]
            + [jax.ShapeDtypeStruct((per // 2, rows, 2 * nodes), jnp.float32)] * (ahead > 0),
            in_specs=[vmem] * (len(operands) - (out is not None)) + [hbm] * (out is not None),
            out_specs=[hbm] + [vmem] * (ahead > 0),
            scratch_shapes=[pltpu.VMEM((rows * per, nodes), jnp.float32), pltpu.SemaphoreType.DMA],
            input_output_aliases={} if out is None else {len(operands) - 1: 0},
            cost_estimate=cost(2 * multiply, move),
            compiler_params=params,
            name="back",
        )(*operands)
        out, ready = results[0], results[-1]
    return out.reshape(fields.shape)


def solution(mesh):
    placed = (
        P(None, "az", None, "curve"),
        P(None, "az", "curve"),
        P("az", "curve", None, None, None, None),
        P("az", "curve", None),
        P("az", "curve"),
    )
    return jax.shard_map(
        functools.partial(on_device, mesh.shape["az"], mesh.shape["curve"]),
        mesh=mesh,
        in_specs=placed,
        out_specs=P(None, "az", None, "curve"),
        check_vma=False,
    )
```

```python
import functools

import jax
import jax.numpy as jnp
import numpy as np
from jax import lax
from jax.experimental import pallas as pl
from jax.experimental.pallas import tpu as pltpu
from jax.sharding import PartitionSpec as P

CHUNKS = 2
SHARES = 2
FIELD_BOUND = 6.0
PARTIAL_BOUND = 4.25
CODE_TOP = 32767.0
VMEM_LIMIT = 24 * 1024 * 1024
STAGE_VMEM_LIMIT = 42 * 1024 * 1024
PACK_VMEM_LIMIT = 52 * 1024 * 1024


def dft_tables(parts, local, order, inverse):
    period = parts * local
    own = np.arange(local)
    tables = np.zeros((parts, 2 * local, parts * 2 * local), np.float64)
    for a in range(parts):
        rows = a * local + own
        for j in range(parts):
            cols = order(a, j) * local + own
            angle = 2.0 * np.pi / period * ((rows[:, None] * cols[None, :]) % period)
            cosine, sine = np.cos(angle), np.sin(angle)
            if inverse:
                block = np.block([[cosine, -sine], [sine, cosine]])
            else:
                block = np.block([[cosine, sine], [-sine, cosine]]) / period
            tables[a, :, j * 2 * local : (j + 1) * 2 * local] = block
    tables = tables.astype(np.float32)
    high = tables.astype(jnp.bfloat16)
    low = (tables - high.astype(np.float32)).astype(jnp.bfloat16)
    return np.stack([high, low], axis=1)


def encoded(x, bound):
    root = jnp.sqrt(jnp.sqrt(jnp.abs(x) * (1.0 / bound)))
    return jnp.round(jnp.where(x < 0, -root, root) * CODE_TOP).astype(jnp.int32).astype(jnp.int16)


def decoded(code, bound=FIELD_BOUND):
    t = code.astype(jnp.int32).astype(jnp.float32) * (bound**0.25 / CODE_TOP)
    return (t * jnp.abs(t)) * (t * t)


def pack_kernel(chunks, az_ref, fields_ref, tables_ref, first_ref, all_ref, forward_out, back_out, held, sems):
    rows, rhs, nodes = fields_ref.shape
    per = rhs // chunks
    copies = [
        pltpu.make_async_copy(
            fields_ref.at[:, pl.ds(index * per, per), :], held.at[index].reshape(rows, per, nodes), sems.at[index]
        )
        for index in range(chunks)
    ]
    tables = [
        pltpu.make_async_copy(tables_ref.at[az_ref[0], way], out, sems.at[chunks + way])
        for way, out in enumerate((forward_out, back_out))
    ]
    for copy in copies + tables:
        copy.start()
    for index in range(chunks):
        copies[index].wait()
        for r in range(per):
            code = encoded(held[index, pl.ds(r, rows, stride=per), :], FIELD_BOUND)
            all_ref[index * per + r] = code
            if index == 0:
                first_ref[r] = code
    for table in tables:
        table.wait()


def exact_product(table_ref, cols, x):
    high = x.astype(jnp.bfloat16)
    low = (x - high.astype(jnp.float32)).astype(jnp.bfloat16)
    table_high, table_low = table_ref[0, :, cols], table_ref[1, :, cols]
    total = jnp.dot(table_high, high, preferred_element_type=jnp.float32)
    total += jnp.dot(table_low, high, preferred_element_type=jnp.float32)
    return total + jnp.dot(table_high, low, preferred_element_type=jnp.float32)


def write_modes(held, modes_ref):
    local, both = modes_ref.shape[:2]
    rhs, rows = both // 2, 2 * local
    for k in range(local):
        real = held[pl.ds(k, rhs, stride=rows), :]
        imag = held[pl.ds(local + k, rhs, stride=rows), :]
        modes_ref[k] = jnp.concatenate([real, imag], axis=0).astype(jnp.bfloat16)


def split_kernel(first, sort, table_ref, own_ref, peer_ref, place_ref, cols_ref, count_ref, tiles_ref,
                 near_ref, far_ref, out_ref, live_ref, sem):
    copy = sort(place_ref, cols_ref, count_ref, tiles_ref, out_ref, live_ref, sem)
    per, rows, nodes = far_ref.shape
    odd = lax.rem(lax.broadcasted_iota(jnp.int32, (rows, 2 * nodes), 0), 2) == 1
    for r in range(0, per, 2):
        near = jnp.zeros((rows, 2 * nodes), jnp.float32)
        far = jnp.zeros((rows, 2 * nodes), jnp.float32)
        for j, ref in enumerate((own_ref, peer_ref)):
            x = jnp.concatenate([decoded(ref[first + r]), decoded(ref[first + r + 1])], axis=1)
            cols = slice(j * rows, (j + 1) * rows)
            near += exact_product(table_ref, cols, x)
            far += exact_product(table_ref, cols, jnp.where(odd, -x, x))
        code = encoded(far, PARTIAL_BOUND)
        for s in range(2):
            near_ref[r + s] = near[:, s * nodes : (s + 1) * nodes]
            far_ref[r + s] = code[:, s * nodes : (s + 1) * nodes]
    copy.wait()


def finish_kernel(near_ref, far_ref, modes_ref, held):
    per, rows = far_ref.shape[:2]
    for r in range(per):
        held[r * rows : (r + 1) * rows, :] = near_ref[r] + decoded(far_ref[r], PARTIAL_BOUND)
    write_modes(held, modes_ref)


def forward_kernel(firsts, table_ref, *refs):
    sources = len(firsts)
    coded_refs, modes_ref, held = refs[:sources], refs[sources], refs[sources + 1]
    rhs = modes_ref.shape[1] // 2
    rows, nodes = coded_refs[0].shape[1:]
    for r in range(0, rhs, 2):
        total = jnp.zeros((rows, 2 * nodes), jnp.float32)
        for j in range(sources):
            at = firsts[j] + r
            x = jnp.concatenate([decoded(coded_refs[j][at]), decoded(coded_refs[j][at + 1])], axis=1)
            total += exact_product(table_ref, slice(j * rows, (j + 1) * rows), x)
        held[r * rows : (r + 1) * rows, :] = total[:, :nodes]
        held[(r + 1) * rows : (r + 2) * rows, :] = total[:, nodes:]
    write_modes(held, modes_ref)


def begin_sort(first, place_ref, cols_ref, count_ref, tiles_ref, out_ref, live_ref, sem):
    slots, modes = cols_ref.shape
    share = out_ref.shape[1]
    place = place_ref[0]
    even = lax.rem(place, 2) == 0
    side = jnp.where(even, place + 1, place - 1)

    def begin(k, carry):
        mode = first + k
        for t in range(slots):
            block = cols_ref[t, mode]
            role = jnp.where(block == place, 0, jnp.where(block == side, 1, 2))
            pltpu.make_async_copy(tiles_ref.at[mode * slots + t], out_ref.at[role, k], sem).start()
            used = jnp.where(t < count_ref[mode], 1.0, 0.0)
            live_ref[role, k] = jnp.full(live_ref.shape[2:], used, jnp.float32).astype(jnp.bfloat16)
        return carry

    lax.fori_loop(0, share, begin, 0)
    return pltpu.make_async_copy(out_ref, out_ref, sem)


def sort_kernel(sort, *refs):
    sort(*refs).wait()


def tile_product(tiles_ref, live_ref, k, roles, values):
    kept = []
    for role, value in zip(roles, values):
        live = live_ref[role, k]
        kept.append(value * jnp.concatenate([live] * (value.shape[0] // live.shape[0]), axis=0))
    return lax.dot_general(
        jnp.concatenate(kept, axis=1),
        jnp.concatenate([tiles_ref[role, k] for role in roles], axis=1),
        (((1,), (1,)), ((), ())),
        preferred_element_type=jnp.float32,
    )


def combined(product):
    rhs, block = product.shape[0] // 2, product.shape[1] // 2
    real = product[:rhs, :block] - product[rhs:, block:]
    imag = product[rhs:, :block] + product[:rhs, block:]
    return real, imag


def put(out_ref, k, both, real, imag):
    out_ref[k * both : k * both + both // 2, :] = real
    out_ref[k * both + both // 2 : (k + 1) * both, :] = imag


def inner_kernel(chunks, shares, *refs):
    live_refs, tile_refs, refs = refs[:shares], refs[shares : 2 * shares], refs[2 * shares :]
    own_refs, side_ref, part_refs = refs[:chunks], refs[chunks], refs[chunks + 1 :]
    modes, both = side_ref.shape[:2]
    for k in range(modes):
        turn, at = divmod(k, modes // shares)
        owns = jnp.concatenate([ref[k] for ref in own_refs], axis=0)
        product = tile_product(tile_refs[turn], live_refs[turn], at, (0,), [owns])
        side = tile_product(tile_refs[turn], live_refs[turn], at, (1,), [side_ref[k]])
        for index, part_ref in enumerate(part_refs):
            mine = product[index * both : (index + 1) * both]
            put(part_ref, k, both, *combined(mine + side if index == 0 else mine))


def outer_kernel(roles, shares, *refs):
    live_refs, tile_refs, refs = refs[:shares], refs[shares : 2 * shares], refs[2 * shares :]
    value_refs, (part_ref, near_ref, held) = refs[:-3], refs[-3:]
    modes, both = value_refs[0].shape[:2]
    rhs = both // 2
    for k in range(modes):
        turn, at = divmod(k, modes // shares)
        values = [ref[k] for ref in value_refs]
        real, imag = combined(tile_product(tile_refs[turn], live_refs[turn], at, roles, values))
        at_real, at_imag = slice(k * both, k * both + rhs), slice(k * both + rhs, (k + 1) * both)
        held[at_real, :] = real + part_ref[at_real, :]
        held[at_imag, :] = imag + part_ref[at_imag, :]
    for r in range(rhs):
        for part in range(2):
            rows = slice(part * modes, (part + 1) * modes)
            near_ref[r, rows, :] = held[pl.ds(part * rhs + r, modes, stride=both), :].astype(jnp.bfloat16)


def back_product(table_ref, near_refs, terms, r):
    rows = near_refs[0].shape[1]
    total = None
    for j, ref in zip(terms, near_refs):
        x = jnp.concatenate([ref[r], ref[r + 1]], axis=1)
        for way in range(2):
            product = jnp.dot(
                table_ref[way, :, j * rows : (j + 1) * rows], x, preferred_element_type=jnp.float32
            )
            total = product if total is None else total + product
    return total


def back_kernel(sources, ahead, chunk, starts, table_ref, fields_ref, impedance_ref, *refs):
    given, next_refs, refs = refs[:sources], refs[sources : sources + ahead], refs[sources + ahead :]
    if starts:
        ready_ref, refs = refs[0], refs[1:]
    if ahead:
        out_ref, next_out, held, sem = refs[-4:]
    else:
        out_ref, held, sem = refs[-3:]
    per, rows, nodes = given[0].shape
    rhs = fields_ref.shape[0] // rows
    local = rows // 2
    z_real, z_imag = impedance_ref[:local], impedance_ref[local:]
    for r in range(0, per, 2):
        total = back_product(table_ref, given, range(starts, starts + sources), r)
        if starts:
            total += ready_ref[r // 2]
        for s in range(2):
            real, imag = total[:local, s * nodes : (s + 1) * nodes], total[local:, s * nodes : (s + 1) * nodes]
            from_row = chunk * per + r + s
            f_real = fields_ref[pl.ds(from_row, local, stride=rhs), :]
            f_imag = fields_ref[pl.ds(local * rhs + from_row, local, stride=rhs), :]
            held[pl.ds(r + s, local, stride=per), :] = f_real + z_real * real - z_imag * imag
            held[pl.ds(local * per + r + s, local, stride=per), :] = f_imag + z_real * imag + z_imag * real
    copy = pltpu.make_async_copy(
        held.reshape(rows, per, nodes), out_ref.at[:, pl.ds(chunk * per, per), :], sem
    )
    copy.start()
    if ahead:
        for r in range(0, per, 2):
            next_out[r // 2] = back_product(table_ref, next_refs, range(ahead), r)
    copy.wait()


PEER = [(i, i ^ 1) for i in range(4)]
ACROSS = [(i, i ^ 2) for i in range(4)]


def after(x, *earlier):
    return lax.optimization_barrier((x,) + earlier)[0]


def cost(flops, moved):
    return pl.CostEstimate(flops=flops, bytes_accessed=moved, transcendentals=0)


def on_device(parts, ring, fields, impedance, tile_data, tile_cols, tile_count):
    _, local, rhs, nodes = fields.shape
    per = rhs // CHUNKS
    slots, block = tile_data.shape[2], tile_data.shape[-1]
    rows = 2 * local
    paired = parts == 4
    order = (lambda a, j: a ^ j) if paired else (lambda a, j: j)
    tables = jnp.asarray(
        np.stack([dft_tables(parts, local, order, False), dft_tables(parts, local, order, True)], axis=1)
    )
    table_shape = jax.ShapeDtypeStruct(tables.shape[2:], jnp.bfloat16)
    flat_fields = fields.reshape(rows * rhs, nodes)
    cut_fields = fields.reshape(rows, rhs, nodes)
    flat_impedance = impedance.reshape(rows, nodes)
    flat_tiles = tile_data.reshape(local * slots, 2 * block, block)
    share = local // SHARES
    sort_shapes = [
        jax.ShapeDtypeStruct((slots, share, 2 * block, block), tile_data.dtype),
        jax.ShapeDtypeStruct((slots, share, 2 * per, nodes), jnp.bfloat16),
    ]
    params = pltpu.CompilerParams(vmem_limit_bytes=VMEM_LIMIT)
    pack_params = pltpu.CompilerParams(vmem_limit_bytes=PACK_VMEM_LIMIT)
    stage_params = pltpu.CompilerParams(vmem_limit_bytes=STAGE_VMEM_LIMIT)
    vmem, smem = pl.BlockSpec(memory_space=pltpu.VMEM), pl.BlockSpec(memory_space=pltpu.SMEM)
    hbm = pl.BlockSpec(memory_space=pltpu.HBM)
    move = 16 * fields.size
    multiply = 4 * rows * rows * parts * per * nodes
    chunk_shape = jax.ShapeDtypeStruct((per, rows, nodes), jnp.int16)

    az = lax.axis_index("az").astype(jnp.int32)[None]
    place = lax.axis_index("curve").astype(jnp.int32)[None]
    first, coded, forward_table, back_table = pl.pallas_call(
        functools.partial(pack_kernel, CHUNKS),
        out_shape=[chunk_shape, jax.ShapeDtypeStruct((rhs, rows, nodes), jnp.int16), table_shape, table_shape],
        in_specs=[smem, hbm, hbm],
        out_specs=[vmem] * 4,
        scratch_shapes=[
            pltpu.VMEM((CHUNKS, rows * per, nodes), jnp.float32),
            pltpu.SemaphoreType.DMA((CHUNKS + 2,)),
        ],
        cost_estimate=cost(0, move),
        compiler_params=pack_params,
        name="pack",
    )(az, cut_fields, tables)

    peer = lax.ppermute(coded, "az", PEER) if paired else None
    pattern = (tile_cols[:, 0, :].T, tile_count.reshape(local))

    def sorting(turn, wait_for):
        return pl.pallas_call(
            functools.partial(sort_kernel, functools.partial(begin_sort, turn * share)),
            out_shape=sort_shapes,
            in_specs=[smem] * 3 + [hbm],
            out_specs=[vmem] * 2,
            scratch_shapes=[pltpu.SemaphoreType.DMA],
            cost_estimate=cost(0, 2 * tile_data.size // SHARES),
            compiler_params=stage_params,
            name="sort",
        )(after(place, wait_for), *pattern, flat_tiles)

    if paired:
        near_part, far_part, head, live = pl.pallas_call(
            functools.partial(split_kernel, per, functools.partial(begin_sort, 0)),
            out_shape=[jax.ShapeDtypeStruct((per, rows, nodes), jnp.float32), chunk_shape] + sort_shapes,
            in_specs=[vmem] * 3 + [smem] * 3 + [hbm],
            out_specs=[vmem] * 4,
            scratch_shapes=[pltpu.SemaphoreType.DMA],
            cost_estimate=cost(3 * multiply, move),
            compiler_params=stage_params,
            name="split",
        )(forward_table, coded, peer, after(place, coded), *pattern, flat_tiles)
    else:
        head, live = sorting(0, coded)
    tiles, lives = [head], [live]

    sides = [(i, i ^ 1) for i in range(ring)]
    onward = [(i, (i + 2 if i % 2 == 0 else i - 2) % ring) for i in range(ring)]
    modes_shape = jax.ShapeDtypeStruct((local, 2 * per, nodes), jnp.bfloat16)
    held_modes = pltpu.VMEM((per * rows, nodes), jnp.float32)
    owns, earlier = [], None
    for index in range(CHUNKS):
        if paired and index:
            across = after(lax.ppermute(after(far_part, earlier), "az", ACROSS), tiles[-1])
            own = pl.pallas_call(
                finish_kernel,
                out_shape=modes_shape,
                in_specs=[vmem] * 2,
                out_specs=vmem,
                scratch_shapes=[held_modes],
                cost_estimate=cost(0, move // 2),
                compiler_params=params,
                name="finish",
            )(near_part, across)
        else:
            if paired:
                across = after(lax.ppermute(first, "az", ACROSS), far_part)
                earlier = across
                sources = [coded, peer, across, lax.ppermute(across, "az", PEER)]
                firsts = (0,) * parts
            else:
                every = lax.all_gather(coded[index * per : (index + 1) * per], "az")
                sources, firsts = [every[j] for j in range(parts)], (0,) * parts
            own = pl.pallas_call(
                functools.partial(forward_kernel, firsts),
                out_shape=modes_shape,
                in_specs=[vmem] * (1 + parts),
                out_specs=vmem,
                scratch_shapes=[held_modes],
                cost_estimate=cost(3 * multiply, move),
                compiler_params=params,
                name="forward",
            )(forward_table, *sources)
        owns.append(own)
        if index == 0:
            for turn in range(1, SHARES):
                tail, live = sorting(turn, own)
                tiles.append(tail)
                lives.append(live)

    side_in = [lax.ppermute(own, "curve", sides) for own in owns]
    side_in[0] = after(side_in[0], *owns[1:])
    far_in = [lax.ppermute(side, "curve", onward) for side in side_in]
    part_shape = jax.ShapeDtypeStruct((local * 2 * per, nodes), jnp.float32)
    parts_of = pl.pallas_call(
        functools.partial(inner_kernel, CHUNKS, SHARES),
        out_shape=[part_shape] * CHUNKS,
        in_specs=[vmem] * (2 * SHARES + CHUNKS + 1),
        out_specs=[vmem] * CHUNKS,
        cost_estimate=cost(0, tile_data.size),
        compiler_params=params,
        name="inner",
    )(*lives, *tiles, *owns, side_in[0])

    nears = []
    for index in range(CHUNKS):
        if index == 0:
            roles, values = (2,), [after(far_in[0], parts_of[0], *side_in[1:])]
        else:
            roles, values = (1, 2), [side_in[index], after(far_in[index], nears[0])]
        nears.append(
            pl.pallas_call(
                functools.partial(outer_kernel, roles, SHARES),
                out_shape=jax.ShapeDtypeStruct((per, rows, nodes), jnp.bfloat16),
                in_specs=[vmem] * (2 * SHARES + len(roles) + 1),
                out_specs=vmem,
                scratch_shapes=[pltpu.VMEM((local * 2 * per, nodes), jnp.float32)],
                cost_estimate=cost(0, tile_data.size // 2),
                compiler_params=params,
                name="outer",
            )(*lives, *tiles, *values, parts_of[index])
        )

    peers = [lax.ppermute(near, "az", PEER) for near in nears] if paired else []
    out, ready = None, None
    for index, near in enumerate(nears):
        starts, ahead = 0, 0
        if paired:
            across = lax.ppermute(near, "az", ACROSS)
            if index:
                starts = 2
                across, out, ready = lax.optimization_barrier((across, out, ready))
                given = [across, lax.ppermute(across, "az", PEER), ready, out]
            else:
                across = after(across, nears[-1])
                given = [near, peers[0], across, lax.ppermute(across, "az", PEER)]
            if index + 1 < CHUNKS:
                ahead = 2
                given[4 - starts : 4 - starts] = [nears[index + 1], peers[index + 1]]
        else:
            every = lax.all_gather(near, "az")
            given = [every[j] for j in range(parts)] + ([] if out is None else [out])
        operands = [back_table, flat_fields, flat_impedance] + given
        results = pl.pallas_call(
            functools.partial(back_kernel, parts - starts, ahead, index, starts),
            out_shape=[jax.ShapeDtypeStruct((rows, rhs, nodes), jnp.float32)]
            + [jax.ShapeDtypeStruct((per // 2, rows, 2 * nodes), jnp.float32)] * (ahead > 0),
            in_specs=[vmem] * (len(operands) - (out is not None)) + [hbm] * (out is not None),
            out_specs=[hbm] + [vmem] * (ahead > 0),
            scratch_shapes=[pltpu.VMEM((rows * per, nodes), jnp.float32), pltpu.SemaphoreType.DMA],
            input_output_aliases={} if out is None else {len(operands) - 1: 0},
            cost_estimate=cost(2 * multiply, move),
            compiler_params=params,
            name="back",
        )(*operands)
        out, ready = results[0], results[-1]
    return out.reshape(fields.shape)


def solution(mesh):
    placed = (
        P(None, "az", None, "curve"),
        P(None, "az", "curve"),
        P("az", "curve", None, None, None, None),
        P("az", "curve", None),
        P("az", "curve"),
    )
    return jax.shard_map(
        functools.partial(on_device, mesh.shape["az"], mesh.shape["curve"]),
        mesh=mesh,
        in_specs=placed,
        out_specs=P(None, "az", None, "curve"),
        check_vma=False,
    )
```

```python
import functools

import jax
import jax.numpy as jnp
import numpy as np
from jax import lax
from jax.experimental import pallas as pl
from jax.experimental.pallas import tpu as pltpu
from jax.sharding import PartitionSpec as P

CHUNKS = 2
SHARES = 2
FIELD_BOUND = 6.0
PARTIAL_BOUND = 4.25
CODE_TOP = 32767.0
VMEM_LIMIT = 24 * 1024 * 1024
STAGE_VMEM_LIMIT = 42 * 1024 * 1024
PACK_VMEM_LIMIT = 52 * 1024 * 1024


def dft_tables(parts, local, order, inverse):
    period = parts * local
    own = np.arange(local)
    tables = np.zeros((parts, 2 * local, parts * 2 * local), np.float64)
    for a in range(parts):
        rows = a * local + own
        for j in range(parts):
            cols = order(a, j) * local + own
            angle = 2.0 * np.pi / period * ((rows[:, None] * cols[None, :]) % period)
            cosine, sine = np.cos(angle), np.sin(angle)
            if inverse:
                block = np.block([[cosine, -sine], [sine, cosine]])
            else:
                block = np.block([[cosine, sine], [-sine, cosine]]) / period
            tables[a, :, j * 2 * local : (j + 1) * 2 * local] = block
    tables = tables.astype(np.float32)
    high = tables.astype(jnp.bfloat16)
    low = (tables - high.astype(np.float32)).astype(jnp.bfloat16)
    return np.stack([high, low], axis=1)


def encoded(x, bound):
    root = jnp.sqrt(jnp.sqrt(jnp.abs(x) * (1.0 / bound)))
    return jnp.round(jnp.where(x < 0, -root, root) * CODE_TOP).astype(jnp.int32).astype(jnp.int16)


def decoded(code, bound=FIELD_BOUND):
    t = code.astype(jnp.int32).astype(jnp.float32) * (bound**0.25 / CODE_TOP)
    return (t * jnp.abs(t)) * (t * t)


def pack_kernel(chunks, fields_ref, tables_ref, first_ref, all_ref, forward_out, back_out, held, sems):
    rows, rhs, nodes = fields_ref.shape
    per = rhs // chunks
    copies = [
        pltpu.make_async_copy(
            fields_ref.at[:, pl.ds(index * per, per), :], held.at[index].reshape(rows, per, nodes), sems.at[index]
        )
        for index in range(chunks)
    ]
    tables = [
        pltpu.make_async_copy(tables_ref.at[lax.axis_index("az"), way], out, sems.at[chunks + way])
        for way, out in enumerate((forward_out, back_out))
    ]
    for copy in copies + tables:
        copy.start()
    for index in range(chunks):
        copies[index].wait()
        for r in range(per):
            code = encoded(held[index, pl.ds(r, rows, stride=per), :], FIELD_BOUND)
            all_ref[index * per + r] = code
            if index == 0:
                first_ref[r] = code
    for table in tables:
        table.wait()


def exact_product(table_ref, cols, x):
    high = x.astype(jnp.bfloat16)
    low = (x - high.astype(jnp.float32)).astype(jnp.bfloat16)
    table_high, table_low = table_ref[0, :, cols], table_ref[1, :, cols]
    total = jnp.dot(table_high, high, preferred_element_type=jnp.float32)
    total += jnp.dot(table_low, high, preferred_element_type=jnp.float32)
    return total + jnp.dot(table_high, low, preferred_element_type=jnp.float32)


def write_modes(held, modes_ref):
    local, both = modes_ref.shape[:2]
    rhs, rows = both // 2, 2 * local
    for k in range(local):
        real = held[pl.ds(k, rhs, stride=rows), :]
        imag = held[pl.ds(local + k, rhs, stride=rows), :]
        modes_ref[k] = jnp.concatenate([real, imag], axis=0).astype(jnp.bfloat16)


def split_kernel(first, sort, table_ref, own_ref, peer_ref, cols_ref, count_ref, tiles_ref,
                 near_ref, far_ref, out_ref, live_ref, sem):
    copy = sort(cols_ref, count_ref, tiles_ref, out_ref, live_ref, sem)
    per, rows, nodes = far_ref.shape
    odd = lax.rem(lax.broadcasted_iota(jnp.int32, (rows, 2 * nodes), 0), 2) == 1
    for r in range(0, per, 2):
        near = jnp.zeros((rows, 2 * nodes), jnp.float32)
        far = jnp.zeros((rows, 2 * nodes), jnp.float32)
        for j, ref in enumerate((own_ref, peer_ref)):
            x = jnp.concatenate([decoded(ref[first + r]), decoded(ref[first + r + 1])], axis=1)
            cols = slice(j * rows, (j + 1) * rows)
            near += exact_product(table_ref, cols, x)
            far += exact_product(table_ref, cols, jnp.where(odd, -x, x))
        code = encoded(far, PARTIAL_BOUND)
        for s in range(2):
            near_ref[r + s] = near[:, s * nodes : (s + 1) * nodes]
            far_ref[r + s] = code[:, s * nodes : (s + 1) * nodes]
    copy.wait()


def finish_kernel(near_ref, far_ref, modes_ref, held):
    per, rows = far_ref.shape[:2]
    for r in range(per):
        held[r * rows : (r + 1) * rows, :] = near_ref[r] + decoded(far_ref[r], PARTIAL_BOUND)
    write_modes(held, modes_ref)


def forward_kernel(firsts, table_ref, *refs):
    sources = len(firsts)
    coded_refs, modes_ref, held = refs[:sources], refs[sources], refs[sources + 1]
    rhs = modes_ref.shape[1] // 2
    rows, nodes = coded_refs[0].shape[1:]
    for r in range(0, rhs, 2):
        total = jnp.zeros((rows, 2 * nodes), jnp.float32)
        for j in range(sources):
            at = firsts[j] + r
            x = jnp.concatenate([decoded(coded_refs[j][at]), decoded(coded_refs[j][at + 1])], axis=1)
            total += exact_product(table_ref, slice(j * rows, (j + 1) * rows), x)
        held[r * rows : (r + 1) * rows, :] = total[:, :nodes]
        held[(r + 1) * rows : (r + 2) * rows, :] = total[:, nodes:]
    write_modes(held, modes_ref)


def begin_sort(first, cols_ref, count_ref, tiles_ref, out_ref, live_ref, sem):
    slots, modes = cols_ref.shape
    share = out_ref.shape[1]
    place = lax.axis_index("curve")
    even = lax.rem(place, 2) == 0
    side = jnp.where(even, place + 1, place - 1)

    def begin(k, carry):
        mode = first + k
        for t in range(slots):
            block = cols_ref[t, mode]
            role = jnp.where(block == place, 0, jnp.where(block == side, 1, 2))
            pltpu.make_async_copy(tiles_ref.at[mode * slots + t], out_ref.at[role, k], sem).start()
            used = jnp.where(t < count_ref[mode], 1.0, 0.0)
            live_ref[role, k] = jnp.full(live_ref.shape[2:], used, jnp.float32).astype(jnp.bfloat16)
        return carry

    lax.fori_loop(0, share, begin, 0)
    return pltpu.make_async_copy(out_ref, out_ref, sem)


def sort_kernel(sort, *refs):
    sort(*refs).wait()


def tile_product(tiles_ref, live_ref, k, roles, values):
    kept = []
    for role, value in zip(roles, values):
        live = live_ref[role, k]
        kept.append(value * jnp.concatenate([live] * (value.shape[0] // live.shape[0]), axis=0))
    return lax.dot_general(
        jnp.concatenate(kept, axis=1),
        jnp.concatenate([tiles_ref[role, k] for role in roles], axis=1),
        (((1,), (1,)), ((), ())),
        preferred_element_type=jnp.float32,
    )


def combined(product):
    rhs, block = product.shape[0] // 2, product.shape[1] // 2
    real = product[:rhs, :block] - product[rhs:, block:]
    imag = product[rhs:, :block] + product[:rhs, block:]
    return real, imag


def put(out_ref, k, both, real, imag):
    out_ref[k * both : k * both + both // 2, :] = real
    out_ref[k * both + both // 2 : (k + 1) * both, :] = imag


def inner_kernel(chunks, shares, *refs):
    live_refs, tile_refs, refs = refs[:shares], refs[shares : 2 * shares], refs[2 * shares :]
    own_refs, side_ref, part_refs = refs[:chunks], refs[chunks], refs[chunks + 1 :]
    modes, both = side_ref.shape[:2]
    for k in range(modes):
        turn, at = divmod(k, modes // shares)
        owns = jnp.concatenate([ref[k] for ref in own_refs], axis=0)
        product = tile_product(tile_refs[turn], live_refs[turn], at, (0,), [owns])
        side = tile_product(tile_refs[turn], live_refs[turn], at, (1,), [side_ref[k]])
        for index, part_ref in enumerate(part_refs):
            mine = product[index * both : (index + 1) * both]
            put(part_ref, k, both, *combined(mine + side if index == 0 else mine))


def outer_kernel(roles, shares, *refs):
    live_refs, tile_refs, refs = refs[:shares], refs[shares : 2 * shares], refs[2 * shares :]
    value_refs, (part_ref, near_ref, held) = refs[:-3], refs[-3:]
    modes, both = value_refs[0].shape[:2]
    rhs = both // 2
    for k in range(modes):
        turn, at = divmod(k, modes // shares)
        values = [ref[k] for ref in value_refs]
        real, imag = combined(tile_product(tile_refs[turn], live_refs[turn], at, roles, values))
        at_real, at_imag = slice(k * both, k * both + rhs), slice(k * both + rhs, (k + 1) * both)
        held[at_real, :] = real + part_ref[at_real, :]
        held[at_imag, :] = imag + part_ref[at_imag, :]
    for r in range(rhs):
        for part in range(2):
            rows = slice(part * modes, (part + 1) * modes)
            near_ref[r, rows, :] = held[pl.ds(part * rhs + r, modes, stride=both), :].astype(jnp.bfloat16)


def back_product(table_ref, near_refs, terms, r):
    rows = near_refs[0].shape[1]
    total = None
    for j, ref in zip(terms, near_refs):
        x = jnp.concatenate([ref[r], ref[r + 1]], axis=1)
        for way in range(2):
            product = jnp.dot(
                table_ref[way, :, j * rows : (j + 1) * rows], x, preferred_element_type=jnp.float32
            )
            total = product if total is None else total + product
    return total


def lead_kernel(counts, table_ref, *refs):
    near_refs, out_refs = refs[: -len(counts)], refs[-len(counts) :]
    for count, out_ref in zip(counts, out_refs):
        for r in range(0, near_refs[0].shape[0], 2):
            out_ref[r // 2] = back_product(table_ref, near_refs[:count], range(count), r)
        near_refs = near_refs[count:]


def back_kernel(sources, chunk, starts, table_ref, fields_ref, impedance_ref, *refs):
    given, (out_ref, held, sem) = refs[:sources], refs[-3:]
    per, rows, nodes = given[0].shape
    rhs = fields_ref.shape[0] // rows
    local = rows // 2
    z_real, z_imag = impedance_ref[:local], impedance_ref[local:]
    for r in range(0, per, 2):
        total = back_product(table_ref, given, range(starts, starts + sources), r)
        if starts:
            total += refs[sources][r // 2]
        for s in range(2):
            real, imag = total[:local, s * nodes : (s + 1) * nodes], total[local:, s * nodes : (s + 1) * nodes]
            from_row = chunk * per + r + s
            f_real = fields_ref[pl.ds(from_row, local, stride=rhs), :]
            f_imag = fields_ref[pl.ds(local * rhs + from_row, local, stride=rhs), :]
            held[pl.ds(r + s, local, stride=per), :] = f_real + z_real * real - z_imag * imag
            held[pl.ds(local * per + r + s, local, stride=per), :] = f_imag + z_real * imag + z_imag * real
    copy = pltpu.make_async_copy(
        held.reshape(rows, per, nodes), out_ref.at[:, pl.ds(chunk * per, per), :], sem
    )
    copy.start()
    copy.wait()


PEER = [(i, i ^ 1) for i in range(4)]
ACROSS = [(i, i ^ 2) for i in range(4)]


def after(x, *earlier):
    return lax.optimization_barrier((x,) + earlier)[0]


def cost(flops, moved):
    return pl.CostEstimate(flops=flops, bytes_accessed=moved, transcendentals=0)


def on_device(parts, ring, fields, impedance, tile_data, tile_cols, tile_count):
    _, local, rhs, nodes = fields.shape
    per = rhs // CHUNKS
    slots, block = tile_data.shape[2], tile_data.shape[-1]
    rows = 2 * local
    paired = parts == 4
    order = (lambda a, j: a ^ j) if paired else (lambda a, j: j)
    tables = jnp.asarray(
        np.stack([dft_tables(parts, local, order, False), dft_tables(parts, local, order, True)], axis=1)
    )
    table_shape = jax.ShapeDtypeStruct(tables.shape[2:], jnp.bfloat16)
    flat_fields = fields.reshape(rows * rhs, nodes)
    cut_fields = fields.reshape(rows, rhs, nodes)
    flat_impedance = impedance.reshape(rows, nodes)
    flat_tiles = tile_data.reshape(local * slots, 2 * block, block)
    share = local // SHARES
    sort_shapes = [
        jax.ShapeDtypeStruct((slots, share, 2 * block, block), tile_data.dtype),
        jax.ShapeDtypeStruct((slots, share, 2 * per, nodes), jnp.bfloat16),
    ]
    params = pltpu.CompilerParams(vmem_limit_bytes=VMEM_LIMIT)
    pack_params = pltpu.CompilerParams(vmem_limit_bytes=PACK_VMEM_LIMIT)
    stage_params = pltpu.CompilerParams(vmem_limit_bytes=STAGE_VMEM_LIMIT)
    vmem, smem = pl.BlockSpec(memory_space=pltpu.VMEM), pl.BlockSpec(memory_space=pltpu.SMEM)
    hbm = pl.BlockSpec(memory_space=pltpu.HBM)
    move = 16 * fields.size
    multiply = 4 * rows * rows * parts * per * nodes
    chunk_shape = jax.ShapeDtypeStruct((per, rows, nodes), jnp.int16)

    first, coded, forward_table, back_table = pl.pallas_call(
        functools.partial(pack_kernel, CHUNKS),
        out_shape=[chunk_shape, jax.ShapeDtypeStruct((rhs, rows, nodes), jnp.int16), table_shape, table_shape],
        in_specs=[hbm, hbm],
        out_specs=[vmem] * 4,
        scratch_shapes=[
            pltpu.VMEM((CHUNKS, rows * per, nodes), jnp.float32),
            pltpu.SemaphoreType.DMA((CHUNKS + 2,)),
        ],
        cost_estimate=cost(0, move),
        compiler_params=pack_params,
        name="pack",
    )(cut_fields, tables)

    peer = lax.ppermute(coded, "az", PEER) if paired else None
    pattern = (tile_cols[:, 0, :].T, tile_count.reshape(local))

    def sorting(turn, wait_for):
        return pl.pallas_call(
            functools.partial(sort_kernel, functools.partial(begin_sort, turn * share)),
            out_shape=sort_shapes,
            in_specs=[smem] * 2 + [hbm],
            out_specs=[vmem] * 2,
            scratch_shapes=[pltpu.SemaphoreType.DMA],
            cost_estimate=cost(0, 2 * tile_data.size // SHARES),
            compiler_params=stage_params,
            name="sort",
        )(*pattern, after(flat_tiles, wait_for))

    if paired:
        near_part, far_part, head, live = pl.pallas_call(
            functools.partial(split_kernel, per, functools.partial(begin_sort, 0)),
            out_shape=[jax.ShapeDtypeStruct((per, rows, nodes), jnp.float32), chunk_shape] + sort_shapes,
            in_specs=[vmem] * 3 + [smem] * 2 + [hbm],
            out_specs=[vmem] * 4,
            scratch_shapes=[pltpu.SemaphoreType.DMA],
            cost_estimate=cost(3 * multiply, move),
            compiler_params=stage_params,
            name="split",
        )(forward_table, coded, peer, *pattern, flat_tiles)
    else:
        head, live = sorting(0, coded)
    tiles, lives = [head], [live]

    sides = [(i, i ^ 1) for i in range(ring)]
    onward = [(i, (i + 2 if i % 2 == 0 else i - 2) % ring) for i in range(ring)]
    modes_shape = jax.ShapeDtypeStruct((local, 2 * per, nodes), jnp.bfloat16)
    held_modes = pltpu.VMEM((per * rows, nodes), jnp.float32)
    owns, earlier = [], None
    for index in range(CHUNKS):
        if paired and index:
            across = after(lax.ppermute(after(far_part, earlier), "az", ACROSS), tiles[-1])
            own = pl.pallas_call(
                finish_kernel,
                out_shape=modes_shape,
                in_specs=[vmem] * 2,
                out_specs=vmem,
                scratch_shapes=[held_modes],
                cost_estimate=cost(0, move // 2),
                compiler_params=params,
                name="finish",
            )(near_part, across)
        else:
            if paired:
                across = after(lax.ppermute(first, "az", ACROSS), far_part)
                earlier = across
                sources = [coded, peer, across, lax.ppermute(across, "az", PEER)]
                firsts = (0,) * parts
            else:
                every = lax.all_gather(coded[index * per : (index + 1) * per], "az")
                sources, firsts = [every[j] for j in range(parts)], (0,) * parts
            own = pl.pallas_call(
                functools.partial(forward_kernel, firsts),
                out_shape=modes_shape,
                in_specs=[vmem] * (1 + parts),
                out_specs=vmem,
                scratch_shapes=[held_modes],
                cost_estimate=cost(3 * multiply, move),
                compiler_params=params,
                name="forward",
            )(forward_table, *sources)
        owns.append(own)
        if index == 0:
            for turn in range(1, SHARES):
                tail, live = sorting(turn, own)
                tiles.append(tail)
                lives.append(live)

    side_in = [lax.ppermute(own, "curve", sides) for own in owns]
    side_in[0] = after(side_in[0], *owns[1:])
    part_shape = jax.ShapeDtypeStruct((local * 2 * per, nodes), jnp.float32)
    parts_of = pl.pallas_call(
        functools.partial(inner_kernel, CHUNKS, SHARES),
        out_shape=[part_shape] * CHUNKS,
        in_specs=[vmem] * (2 * SHARES + CHUNKS + 1),
        out_specs=[vmem] * CHUNKS,
        cost_estimate=cost(0, tile_data.size),
        compiler_params=params,
        name="inner",
    )(*lives, *tiles, *owns, side_in[0])

    side_in[1:] = [after(side, *parts_of) for side in side_in[1:]]
    far_in = [lax.ppermute(side, "curve", onward) for side in side_in]
    nears = []
    for index in range(CHUNKS):
        if index == 0:
            roles, values = (2,), [after(far_in[0], parts_of[0], *side_in[1:])]
        else:
            roles, values = (1, 2), [side_in[index], after(far_in[index], nears[0])]
        nears.append(
            pl.pallas_call(
                functools.partial(outer_kernel, roles, SHARES),
                out_shape=jax.ShapeDtypeStruct((per, rows, nodes), jnp.bfloat16),
                in_specs=[vmem] * (2 * SHARES + len(roles) + 1),
                out_specs=vmem,
                scratch_shapes=[pltpu.VMEM((local * 2 * per, nodes), jnp.float32)],
                cost_estimate=cost(0, tile_data.size // 2),
                compiler_params=params,
                name="outer",
            )(*lives, *tiles, *values, parts_of[index])
        )

    if paired:
        peers = [lax.ppermute(near, "az", PEER) for near in nears]
        across = [lax.ppermute(near, "az", ACROSS) for near in nears]
        counts = [2] * (CHUNKS - 1) + [1]
        led = [x for near, peer_near, count in zip(nears, peers, counts) for x in (near, peer_near)[:count]]
        ready = pl.pallas_call(
            functools.partial(lead_kernel, counts),
            out_shape=[jax.ShapeDtypeStruct((per // 2, rows, 2 * nodes), jnp.float32)] * CHUNKS,
            in_specs=[vmem] * (1 + len(led)),
            out_specs=[vmem] * CHUNKS,
            cost_estimate=cost(2 * multiply, move),
            compiler_params=params,
            name="lead",
        )(back_table, *led)
        across[:-1] = [after(x, nears[-1]) for x in across[:-1]]
        across[-1] = after(across[-1], *ready)
        crossed = [lax.ppermute(x, "az", PEER) for x in across]
        crossed[:-1] = [after(x, across[-1]) for x in crossed[:-1]]
    out = None
    for index, near in enumerate(nears):
        starts = 0
        if paired:
            starts = counts[index]
            given = [near, peers[index], across[index], crossed[index]][starts:] + [ready[index]]
        else:
            every = lax.all_gather(near, "az")
            given = [every[j] for j in range(parts)]
        operands = [back_table, flat_fields, flat_impedance] + given + ([] if out is None else [out])
        out = pl.pallas_call(
            functools.partial(back_kernel, parts - starts, index, starts),
            out_shape=jax.ShapeDtypeStruct((rows, rhs, nodes), jnp.float32),
            in_specs=[vmem] * (len(operands) - (out is not None)) + [hbm] * (out is not None),
            out_specs=hbm,
            scratch_shapes=[pltpu.VMEM((rows * per, nodes), jnp.float32), pltpu.SemaphoreType.DMA],
            input_output_aliases={} if out is None else {len(operands) - 1: 0},
            cost_estimate=cost(2 * multiply, move),
            compiler_params=params,
            name="back",
        )(*operands)
    return out.reshape(fields.shape)


def solution(mesh):
    placed = (
        P(None, "az", None, "curve"),
        P(None, "az", "curve"),
        P("az", "curve", None, None, None, None),
        P("az", "curve", None),
        P("az", "curve"),
    )
    return jax.shard_map(
        functools.partial(on_device, mesh.shape["az"], mesh.shape["curve"]),
        mesh=mesh,
        in_specs=placed,
        out_specs=P(None, "az", None, "curve"),
        check_vma=False,
    )
```

```python
import functools

import jax
import jax.numpy as jnp
import numpy as np
from jax import lax
from jax.experimental import pallas as pl
from jax.experimental.pallas import tpu as pltpu
from jax.sharding import PartitionSpec as P

CHUNKS = 2
SHARES = 2
FIELD_BOUND = 6.0
PARTIAL_BOUND = 4.25
CODE_TOP = 32767.0
VMEM_LIMIT = 24 * 1024 * 1024
STAGE_VMEM_LIMIT = 42 * 1024 * 1024
PACK_VMEM_LIMIT = 52 * 1024 * 1024


def dft_tables(parts, local, order, inverse):
    period = parts * local
    own = np.arange(local)
    tables = np.zeros((parts, 2 * local, parts * 2 * local), np.float64)
    for a in range(parts):
        rows = a * local + own
        for j in range(parts):
            cols = order(a, j) * local + own
            angle = 2.0 * np.pi / period * ((rows[:, None] * cols[None, :]) % period)
            cosine, sine = np.cos(angle), np.sin(angle)
            if inverse:
                block = np.block([[cosine, -sine], [sine, cosine]])
            else:
                block = np.block([[cosine, sine], [-sine, cosine]]) / period
            tables[a, :, j * 2 * local : (j + 1) * 2 * local] = block
    tables = tables.astype(np.float32)
    high = tables.astype(jnp.bfloat16)
    low = (tables - high.astype(np.float32)).astype(jnp.bfloat16)
    return np.stack([high, low], axis=1)


def encoded(x, bound):
    root = lax.rsqrt(lax.rsqrt(jnp.maximum(jnp.abs(x) * (1.0 / bound), 1e-30)))
    return jnp.round(jnp.where(x < 0, -root, root) * CODE_TOP).astype(jnp.int32).astype(jnp.int16)


def decoded(code, bound=FIELD_BOUND):
    t = code.astype(jnp.int32).astype(jnp.float32) * (bound**0.25 / CODE_TOP)
    return (t * jnp.abs(t)) * (t * t)


def pack_kernel(chunks, fields_ref, tables_ref, first_ref, all_ref, forward_out, back_out, held, sems):
    rows, rhs, nodes = fields_ref.shape
    per = rhs // chunks
    copies = [
        pltpu.make_async_copy(
            fields_ref.at[:, pl.ds(index * per, per), :], held.at[index].reshape(rows, per, nodes), sems.at[index]
        )
        for index in range(chunks)
    ]
    tables = [
        pltpu.make_async_copy(tables_ref.at[lax.axis_index("az"), way], out, sems.at[chunks + way])
        for way, out in enumerate((forward_out, back_out))
    ]
    for copy in copies + tables:
        copy.start()
    for index in range(chunks):
        copies[index].wait()
        for r in range(per):
            code = encoded(held[index, pl.ds(r, rows, stride=per), :], FIELD_BOUND)
            all_ref[index * per + r] = code
            if index == 0:
                first_ref[r] = code
    for table in tables:
        table.wait()


def exact_product(table_ref, cols, x):
    high = x.astype(jnp.bfloat16)
    low = (x - high.astype(jnp.float32)).astype(jnp.bfloat16)
    table_high, table_low = table_ref[0, :, cols], table_ref[1, :, cols]
    total = jnp.dot(table_high, high, preferred_element_type=jnp.float32)
    total += jnp.dot(table_low, high, preferred_element_type=jnp.float32)
    return total + jnp.dot(table_high, low, preferred_element_type=jnp.float32)


def write_modes(held, modes_ref):
    local, both = modes_ref.shape[:2]
    rhs, rows = both // 2, 2 * local
    for k in range(local):
        real = held[pl.ds(k, rhs, stride=rows), :]
        imag = held[pl.ds(local + k, rhs, stride=rows), :]
        modes_ref[k] = jnp.concatenate([real, imag], axis=0).astype(jnp.bfloat16)


def split_kernel(first, sort, table_ref, own_ref, peer_ref, cols_ref, count_ref, tiles_ref,
                 lead_ref, near_ref, far_ref, out_ref, live_ref, sem):
    copy = sort(cols_ref, count_ref, tiles_ref, out_ref, live_ref, sem)
    per, rows, nodes = far_ref.shape
    odd = lax.rem(lax.broadcasted_iota(jnp.int32, (rows, 2 * nodes), 0), 2) == 1
    for r in range(0, first, 2):
        lead = jnp.zeros((rows, 2 * nodes), jnp.float32)
        for j, ref in enumerate((own_ref, peer_ref)):
            x = jnp.concatenate([decoded(ref[r]), decoded(ref[r + 1])], axis=1)
            lead += exact_product(table_ref, slice(j * rows, (j + 1) * rows), x)
        for s in range(2):
            lead_ref[r + s] = lead[:, s * nodes : (s + 1) * nodes]
    for r in range(0, per, 2):
        near = jnp.zeros((rows, 2 * nodes), jnp.float32)
        far = jnp.zeros((rows, 2 * nodes), jnp.float32)
        for j, ref in enumerate((own_ref, peer_ref)):
            x = jnp.concatenate([decoded(ref[first + r]), decoded(ref[first + r + 1])], axis=1)
            cols = slice(j * rows, (j + 1) * rows)
            near += exact_product(table_ref, cols, x)
            far += exact_product(table_ref, cols, jnp.where(odd, -x, x))
        code = encoded(far, PARTIAL_BOUND)
        for s in range(2):
            near_ref[r + s] = near[:, s * nodes : (s + 1) * nodes]
            far_ref[r + s] = code[:, s * nodes : (s + 1) * nodes]
    copy.wait()


def finish_kernel(near_ref, far_ref, modes_ref, held):
    per, rows = far_ref.shape[:2]
    for r in range(per):
        held[r * rows : (r + 1) * rows, :] = near_ref[r] + decoded(far_ref[r], PARTIAL_BOUND)
    write_modes(held, modes_ref)


def forward_kernel(starts, table_ref, *refs):
    coded_refs, modes_ref, held = refs[:-2], refs[-2], refs[-1]
    if starts:
        ready_ref, coded_refs = coded_refs[0], coded_refs[1:]
    rhs = modes_ref.shape[1] // 2
    rows, nodes = coded_refs[0].shape[1:]
    for r in range(0, rhs, 2):
        total = jnp.zeros((rows, 2 * nodes), jnp.float32)
        for j, ref in enumerate(coded_refs, starts):
            x = jnp.concatenate([decoded(ref[r]), decoded(ref[r + 1])], axis=1)
            total += exact_product(table_ref, slice(j * rows, (j + 1) * rows), x)
        for s in range(2):
            part = total[:, s * nodes : (s + 1) * nodes]
            held[(r + s) * rows : (r + s + 1) * rows, :] = part + ready_ref[r + s] if starts else part
    write_modes(held, modes_ref)


def begin_sort(first, cols_ref, count_ref, tiles_ref, out_ref, live_ref, sem):
    slots, modes = cols_ref.shape
    share = out_ref.shape[1]
    place = lax.axis_index("curve")
    even = lax.rem(place, 2) == 0
    side = jnp.where(even, place + 1, place - 1)

    def begin(k, carry):
        mode = first + k
        for t in range(slots):
            block = cols_ref[t, mode]
            role = jnp.where(block == place, 0, jnp.where(block == side, 1, 2))
            pltpu.make_async_copy(tiles_ref.at[mode * slots + t], out_ref.at[role, k], sem).start()
            used = jnp.where(t < count_ref[mode], 1.0, 0.0)
            live_ref[role, k] = jnp.full(live_ref.shape[2:], used, jnp.float32).astype(jnp.bfloat16)
        return carry

    lax.fori_loop(0, share, begin, 0)
    return pltpu.make_async_copy(out_ref, out_ref, sem)


def sort_kernel(sort, *refs):
    sort(*refs).wait()


def tile_product(tiles_ref, live_ref, k, roles, values):
    kept = []
    for role, value in zip(roles, values):
        live = live_ref[role, k]
        kept.append(value * jnp.concatenate([live] * (value.shape[0] // live.shape[0]), axis=0))
    return lax.dot_general(
        jnp.concatenate(kept, axis=1),
        jnp.concatenate([tiles_ref[role, k] for role in roles], axis=1),
        (((1,), (1,)), ((), ())),
        preferred_element_type=jnp.float32,
    )


def combined(product):
    rhs, block = product.shape[0] // 2, product.shape[1] // 2
    real = product[:rhs, :block] - product[rhs:, block:]
    imag = product[rhs:, :block] + product[:rhs, block:]
    return real, imag


def put(out_ref, k, both, real, imag):
    out_ref[k * both : k * both + both // 2, :] = real
    out_ref[k * both + both // 2 : (k + 1) * both, :] = imag


def inner_kernel(chunks, shares, *refs):
    live_refs, tile_refs, refs = refs[:shares], refs[shares : 2 * shares], refs[2 * shares :]
    own_refs, side_ref, part_refs = refs[:chunks], refs[chunks], refs[chunks + 1 :]
    modes, both = side_ref.shape[:2]
    for k in range(modes):
        turn, at = divmod(k, modes // shares)
        owns = jnp.concatenate([ref[k] for ref in own_refs], axis=0)
        product = tile_product(tile_refs[turn], live_refs[turn], at, (0,), [owns])
        side = tile_product(tile_refs[turn], live_refs[turn], at, (1,), [side_ref[k]])
        for index, part_ref in enumerate(part_refs):
            mine = product[index * both : (index + 1) * both]
            put(part_ref, k, both, *combined(mine + side if index == 0 else mine))


def outer_kernel(roles, shares, *refs):
    live_refs, tile_refs, refs = refs[:shares], refs[shares : 2 * shares], refs[2 * shares :]
    value_refs, (part_ref, near_ref, held) = refs[:-3], refs[-3:]
    modes, both = value_refs[0].shape[:2]
    rhs = both // 2
    for k in range(modes):
        turn, at = divmod(k, modes // shares)
        values = [ref[k] for ref in value_refs]
        real, imag = combined(tile_product(tile_refs[turn], live_refs[turn], at, roles, values))
        at_real, at_imag = slice(k * both, k * both + rhs), slice(k * both + rhs, (k + 1) * both)
        held[at_real, :] = real + part_ref[at_real, :]
        held[at_imag, :] = imag + part_ref[at_imag, :]
    for r in range(rhs):
        for part in range(2):
            rows = slice(part * modes, (part + 1) * modes)
            near_ref[r, rows, :] = held[pl.ds(part * rhs + r, modes, stride=both), :].astype(jnp.bfloat16)


def back_product(table_ref, near_refs, terms, r):
    rows = near_refs[0].shape[1]
    total = None
    for j, ref in zip(terms, near_refs):
        x = jnp.concatenate([ref[r], ref[r + 1]], axis=1)
        for way in range(2):
            product = jnp.dot(
                table_ref[way, :, j * rows : (j + 1) * rows], x, preferred_element_type=jnp.float32
            )
            total = product if total is None else total + product
    return total


def lead_kernel(counts, table_ref, *refs):
    near_refs, out_refs = refs[: -len(counts)], refs[-len(counts) :]
    for count, out_ref in zip(counts, out_refs):
        for r in range(0, near_refs[0].shape[0], 2):
            out_ref[r // 2] = back_product(table_ref, near_refs[:count], range(count), r)
        near_refs = near_refs[count:]


def back_kernel(sources, chunk, starts, table_ref, fields_ref, impedance_ref, *refs):
    given, (out_ref, held, sem) = refs[:sources], refs[-3:]
    per, rows, nodes = given[0].shape
    rhs = fields_ref.shape[0] // rows
    local = rows // 2
    z_real, z_imag = impedance_ref[:local], impedance_ref[local:]
    for r in range(0, per, 2):
        total = back_product(table_ref, given, range(starts, starts + sources), r)
        if starts:
            total += refs[sources][r // 2]
        for s in range(2):
            real, imag = total[:local, s * nodes : (s + 1) * nodes], total[local:, s * nodes : (s + 1) * nodes]
            from_row = chunk * per + r + s
            f_real = fields_ref[pl.ds(from_row, local, stride=rhs), :]
            f_imag = fields_ref[pl.ds(local * rhs + from_row, local, stride=rhs), :]
            held[pl.ds(r + s, local, stride=per), :] = f_real + z_real * real - z_imag * imag
            held[pl.ds(local * per + r + s, local, stride=per), :] = f_imag + z_real * imag + z_imag * real
    copy = pltpu.make_async_copy(
        held.reshape(rows, per, nodes), out_ref.at[:, pl.ds(chunk * per, per), :], sem
    )
    copy.start()
    copy.wait()


PEER = [(i, i ^ 1) for i in range(4)]
ACROSS = [(i, i ^ 2) for i in range(4)]


def after(x, *earlier):
    return lax.optimization_barrier((x,) + earlier)[0]


def cost(flops, moved):
    return pl.CostEstimate(flops=flops, bytes_accessed=moved, transcendentals=0)


def on_device(parts, ring, fields, impedance, tile_data, tile_cols, tile_count):
    _, local, rhs, nodes = fields.shape
    per = rhs // CHUNKS
    slots, block = tile_data.shape[2], tile_data.shape[-1]
    rows = 2 * local
    paired = parts == 4
    order = (lambda a, j: a ^ j) if paired else (lambda a, j: j)
    tables = jnp.asarray(
        np.stack([dft_tables(parts, local, order, False), dft_tables(parts, local, order, True)], axis=1)
    )
    table_shape = jax.ShapeDtypeStruct(tables.shape[2:], jnp.bfloat16)
    flat_fields = fields.reshape(rows * rhs, nodes)
    cut_fields = fields.reshape(rows, rhs, nodes)
    flat_impedance = impedance.reshape(rows, nodes)
    flat_tiles = tile_data.reshape(local * slots, 2 * block, block)
    share = local // SHARES
    sort_shapes = [
        jax.ShapeDtypeStruct((slots, share, 2 * block, block), tile_data.dtype),
        jax.ShapeDtypeStruct((slots, share, 2 * per, nodes), jnp.bfloat16),
    ]
    params = pltpu.CompilerParams(vmem_limit_bytes=VMEM_LIMIT)
    pack_params = pltpu.CompilerParams(vmem_limit_bytes=PACK_VMEM_LIMIT)
    stage_params = pltpu.CompilerParams(vmem_limit_bytes=STAGE_VMEM_LIMIT)
    vmem, smem = pl.BlockSpec(memory_space=pltpu.VMEM), pl.BlockSpec(memory_space=pltpu.SMEM)
    hbm = pl.BlockSpec(memory_space=pltpu.HBM)
    move = 16 * fields.size
    multiply = 4 * rows * rows * parts * per * nodes
    chunk_shape = jax.ShapeDtypeStruct((per, rows, nodes), jnp.int16)

    first, coded, forward_table, back_table = pl.pallas_call(
        functools.partial(pack_kernel, CHUNKS),
        out_shape=[chunk_shape, jax.ShapeDtypeStruct((rhs, rows, nodes), jnp.int16), table_shape, table_shape],
        in_specs=[hbm, hbm],
        out_specs=[vmem] * 4,
        scratch_shapes=[
            pltpu.VMEM((CHUNKS, rows * per, nodes), jnp.float32),
            pltpu.SemaphoreType.DMA((CHUNKS + 2,)),
        ],
        cost_estimate=cost(0, move),
        compiler_params=pack_params,
        name="pack",
    )(cut_fields, tables)

    peer = lax.ppermute(coded, "az", PEER) if paired else None
    pattern = (tile_cols[:, 0, :].T, tile_count.reshape(local))

    def sorting(turn, wait_for):
        return pl.pallas_call(
            functools.partial(sort_kernel, functools.partial(begin_sort, turn * share)),
            out_shape=sort_shapes,
            in_specs=[smem] * 2 + [hbm],
            out_specs=[vmem] * 2,
            scratch_shapes=[pltpu.SemaphoreType.DMA],
            cost_estimate=cost(0, 2 * tile_data.size // SHARES),
            compiler_params=stage_params,
            name="sort",
        )(*pattern, after(flat_tiles, wait_for))

    if paired:
        lead_part, near_part, far_part, head, live = pl.pallas_call(
            functools.partial(split_kernel, per, functools.partial(begin_sort, 0)),
            out_shape=[jax.ShapeDtypeStruct((per, rows, nodes), jnp.float32)] * 2 + [chunk_shape] + sort_shapes,
            in_specs=[vmem] * 3 + [smem] * 2 + [hbm],
            out_specs=[vmem] * 5,
            scratch_shapes=[pltpu.SemaphoreType.DMA],
            cost_estimate=cost(3 * multiply, move),
            compiler_params=stage_params,
            name="split",
        )(forward_table, coded, peer, *pattern, flat_tiles)
    else:
        head, live = sorting(0, coded)
    tiles, lives = [head], [live]

    sides = [(i, i ^ 1) for i in range(ring)]
    onward = [(i, (i + 2 if i % 2 == 0 else i - 2) % ring) for i in range(ring)]
    modes_shape = jax.ShapeDtypeStruct((local, 2 * per, nodes), jnp.bfloat16)
    held_modes = pltpu.VMEM((per * rows, nodes), jnp.float32)
    owns, earlier = [], None
    for index in range(CHUNKS):
        if paired and index:
            across = after(lax.ppermute(after(far_part, earlier), "az", ACROSS), tiles[-1])
            own = pl.pallas_call(
                finish_kernel,
                out_shape=modes_shape,
                in_specs=[vmem] * 2,
                out_specs=vmem,
                scratch_shapes=[held_modes],
                cost_estimate=cost(0, move // 2),
                compiler_params=params,
                name="finish",
            )(near_part, across)
        else:
            if paired:
                across = after(lax.ppermute(first, "az", ACROSS), far_part)
                earlier = across
                starts, sources = 2, [lead_part, across, lax.ppermute(across, "az", PEER)]
            else:
                every = lax.all_gather(coded[index * per : (index + 1) * per], "az")
                starts, sources = 0, [every[j] for j in range(parts)]
            own = pl.pallas_call(
                functools.partial(forward_kernel, starts),
                out_shape=modes_shape,
                in_specs=[vmem] * (1 + len(sources)),
                out_specs=vmem,
                scratch_shapes=[held_modes],
                cost_estimate=cost(3 * multiply, move),
                compiler_params=params,
                name="forward",
            )(forward_table, *sources)
        owns.append(own)
        if index == 0:
            for turn in range(1, SHARES):
                tail, live = sorting(turn, own)
                tiles.append(tail)
                lives.append(live)

    side_in = [lax.ppermute(own, "curve", sides) for own in owns]
    side_in[0] = after(side_in[0], *owns[1:])
    part_shape = jax.ShapeDtypeStruct((local * 2 * per, nodes), jnp.float32)
    parts_of = pl.pallas_call(
        functools.partial(inner_kernel, CHUNKS, SHARES),
        out_shape=[part_shape] * CHUNKS,
        in_specs=[vmem] * (2 * SHARES + CHUNKS + 1),
        out_specs=[vmem] * CHUNKS,
        cost_estimate=cost(0, tile_data.size),
        compiler_params=params,
        name="inner",
    )(*lives, *tiles, *owns, side_in[0])

    side_in[1:] = [after(side, *parts_of) for side in side_in[1:]]
    far_in = [lax.ppermute(side, "curve", onward) for side in side_in]
    nears = []
    for index in range(CHUNKS):
        if index == 0:
            roles, values = (2,), [after(far_in[0], parts_of[0], *side_in[1:])]
        else:
            roles, values = (1, 2), [side_in[index], after(far_in[index], nears[0])]
        nears.append(
            pl.pallas_call(
                functools.partial(outer_kernel, roles, SHARES),
                out_shape=jax.ShapeDtypeStruct((per, rows, nodes), jnp.bfloat16),
                in_specs=[vmem] * (2 * SHARES + len(roles) + 1),
                out_specs=vmem,
                scratch_shapes=[pltpu.VMEM((local * 2 * per, nodes), jnp.float32)],
                cost_estimate=cost(0, tile_data.size // 2),
                compiler_params=params,
                name="outer",
            )(*lives, *tiles, *values, parts_of[index])
        )

    if paired:
        peers = [lax.ppermute(near, "az", PEER) for near in nears]
        across = [lax.ppermute(near, "az", ACROSS) for near in nears]
        counts = [2] * (CHUNKS - 1) + [1]
        led = [x for near, peer_near, count in zip(nears, peers, counts) for x in (near, peer_near)[:count]]
        ready = pl.pallas_call(
            functools.partial(lead_kernel, counts),
            out_shape=[jax.ShapeDtypeStruct((per // 2, rows, 2 * nodes), jnp.float32)] * CHUNKS,
            in_specs=[vmem] * (1 + len(led)),
            out_specs=[vmem] * CHUNKS,
            cost_estimate=cost(2 * multiply, move),
            compiler_params=params,
            name="lead",
        )(back_table, *led)
        across[:-1] = [after(x, nears[-1]) for x in across[:-1]]
        across[-1] = after(across[-1], *ready)
        crossed = [lax.ppermute(x, "az", PEER) for x in across]
        crossed[:-1] = [after(x, across[-1]) for x in crossed[:-1]]
    out = None
    for index, near in enumerate(nears):
        starts = 0
        if paired:
            starts = counts[index]
            given = [near, peers[index], across[index], crossed[index]][starts:] + [ready[index]]
        else:
            every = lax.all_gather(near, "az")
            given = [every[j] for j in range(parts)]
        operands = [back_table, flat_fields, flat_impedance] + given + ([] if out is None else [out])
        out = pl.pallas_call(
            functools.partial(back_kernel, parts - starts, index, starts),
            out_shape=jax.ShapeDtypeStruct((rows, rhs, nodes), jnp.float32),
            in_specs=[vmem] * (len(operands) - (out is not None)) + [hbm] * (out is not None),
            out_specs=hbm,
            scratch_shapes=[pltpu.VMEM((rows * per, nodes), jnp.float32), pltpu.SemaphoreType.DMA],
            input_output_aliases={} if out is None else {len(operands) - 1: 0},
            cost_estimate=cost(2 * multiply, move),
            compiler_params=params,
            name="back",
        )(*operands)
    return out.reshape(fields.shape)


def solution(mesh):
    placed = (
        P(None, "az", None, "curve"),
        P(None, "az", "curve"),
        P("az", "curve", None, None, None, None),
        P("az", "curve", None),
        P("az", "curve"),
    )
    return jax.shard_map(
        functools.partial(on_device, mesh.shape["az"], mesh.shape["curve"]),
        mesh=mesh,
        in_specs=placed,
        out_specs=P(None, "az", None, "curve"),
        check_vma=False,
    )
```

```python
import functools

import jax
import jax.numpy as jnp
import numpy as np
from jax import lax
from jax.experimental import pallas as pl
from jax.experimental.pallas import tpu as pltpu
from jax.sharding import PartitionSpec as P

CHUNKS = 2
SHARES = 2
FIELD_BOUND = 6.0
PARTIAL_BOUND = 4.25
CODE_TOP = 32767.0
VMEM_LIMIT = 24 * 1024 * 1024
STAGE_VMEM_LIMIT = 42 * 1024 * 1024
PACK_VMEM_LIMIT = 53 * 1024 * 1024


def dft_tables(parts, local, order, inverse):
    period = parts * local
    own = np.arange(local)
    tables = np.zeros((parts, 2 * local, parts * 2 * local), np.float64)
    for a in range(parts):
        rows = a * local + own
        for j in range(parts):
            cols = order(a, j) * local + own
            angle = 2.0 * np.pi / period * ((rows[:, None] * cols[None, :]) % period)
            cosine, sine = np.cos(angle), np.sin(angle)
            if inverse:
                block = np.block([[cosine, -sine], [sine, cosine]])
            else:
                block = np.block([[cosine, sine], [-sine, cosine]]) / period
            tables[a, :, j * 2 * local : (j + 1) * 2 * local] = block
    tables = tables.astype(np.float32)
    high = tables.astype(jnp.bfloat16)
    low = (tables - high.astype(np.float32)).astype(jnp.bfloat16)
    return np.stack([high, low], axis=1)


def encoded(x, bound):
    root = lax.rsqrt(lax.rsqrt(jnp.maximum(jnp.abs(x) * (1.0 / bound), 1e-30)))
    return jnp.round(jnp.where(x < 0, -root, root) * CODE_TOP).astype(jnp.int32).astype(jnp.int16)


def decoded(code, bound=FIELD_BOUND):
    t = code.astype(jnp.int32).astype(jnp.float32) * (bound**0.25 / CODE_TOP)
    return (t * jnp.abs(t)) * (t * t)


def pack_kernel(chunks, fields_ref, first_ref, all_ref, held, sems):
    rows, rhs, nodes = fields_ref.shape
    per = rhs // chunks
    copies = [
        pltpu.make_async_copy(
            fields_ref.at[:, pl.ds(index * per, per), :], held.at[index].reshape(rows, per, nodes), sems.at[index]
        )
        for index in range(chunks)
    ]
    for copy in copies:
        copy.start()
    for index in range(chunks):
        copies[index].wait()
        for r in range(per):
            code = encoded(held[index, pl.ds(r, rows, stride=per), :], FIELD_BOUND)
            all_ref[index * per + r] = code
            if index == 0:
                first_ref[r] = code


def begin_tables(tables_ref, forward_out, back_out, sems):
    copies = [
        pltpu.make_async_copy(tables_ref.at[lax.axis_index("az"), way], out, sems.at[way])
        for way, out in enumerate((forward_out, back_out))
    ]
    for copy in copies:
        copy.start()
    return copies


def table_kernel(*refs):
    for copy in begin_tables(*refs):
        copy.wait()


def exact_product(table_ref, cols, x):
    high = x.astype(jnp.bfloat16)
    low = (x - high.astype(jnp.float32)).astype(jnp.bfloat16)
    table_high, table_low = table_ref[0, :, cols], table_ref[1, :, cols]
    total = jnp.dot(table_high, high, preferred_element_type=jnp.float32)
    total += jnp.dot(table_low, high, preferred_element_type=jnp.float32)
    return total + jnp.dot(table_high, low, preferred_element_type=jnp.float32)


def write_modes(held, modes_ref):
    local, both = modes_ref.shape[:2]
    rhs, rows = both // 2, 2 * local
    for k in range(local):
        real = held[pl.ds(k, rhs, stride=rows), :]
        imag = held[pl.ds(local + k, rhs, stride=rows), :]
        modes_ref[k] = jnp.concatenate([real, imag], axis=0).astype(jnp.bfloat16)


def split_kernel(first, sort, own_ref, peer_ref, cols_ref, count_ref, tiles_ref, tables_ref,
                 table_ref, back_ref, lead_ref, near_ref, far_ref, out_ref, live_ref, sem, table_sems):
    tables = begin_tables(tables_ref, table_ref, back_ref, table_sems)
    copy = sort(cols_ref, count_ref, tiles_ref, out_ref, live_ref, sem)
    for table in tables:
        table.wait()
    per, rows, nodes = far_ref.shape
    odd = lax.rem(lax.broadcasted_iota(jnp.int32, (rows, 2 * nodes), 0), 2) == 1
    for r in range(0, first, 2):
        lead = jnp.zeros((rows, 2 * nodes), jnp.float32)
        for j, ref in enumerate((own_ref, peer_ref)):
            x = jnp.concatenate([decoded(ref[r]), decoded(ref[r + 1])], axis=1)
            lead += exact_product(table_ref, slice(j * rows, (j + 1) * rows), x)
        for s in range(2):
            lead_ref[r + s] = lead[:, s * nodes : (s + 1) * nodes]
    for r in range(0, per, 2):
        near = jnp.zeros((rows, 2 * nodes), jnp.float32)
        far = jnp.zeros((rows, 2 * nodes), jnp.float32)
        for j, ref in enumerate((own_ref, peer_ref)):
            x = jnp.concatenate([decoded(ref[first + r]), decoded(ref[first + r + 1])], axis=1)
            cols = slice(j * rows, (j + 1) * rows)
            near += exact_product(table_ref, cols, x)
            far += exact_product(table_ref, cols, jnp.where(odd, -x, x))
        code = encoded(far, PARTIAL_BOUND)
        for s in range(2):
            near_ref[r + s] = near[:, s * nodes : (s + 1) * nodes]
            far_ref[r + s] = code[:, s * nodes : (s + 1) * nodes]
    copy.wait()


def finish_kernel(near_ref, far_ref, modes_ref, held):
    per, rows = far_ref.shape[:2]
    for r in range(per):
        held[r * rows : (r + 1) * rows, :] = near_ref[r] + decoded(far_ref[r], PARTIAL_BOUND)
    write_modes(held, modes_ref)


def forward_kernel(starts, table_ref, *refs):
    coded_refs, modes_ref, held = refs[:-2], refs[-2], refs[-1]
    if starts:
        ready_ref, coded_refs = coded_refs[0], coded_refs[1:]
    rhs = modes_ref.shape[1] // 2
    rows, nodes = coded_refs[0].shape[1:]
    for r in range(0, rhs, 2):
        total = jnp.zeros((rows, 2 * nodes), jnp.float32)
        for j, ref in enumerate(coded_refs, starts):
            x = jnp.concatenate([decoded(ref[r]), decoded(ref[r + 1])], axis=1)
            total += exact_product(table_ref, slice(j * rows, (j + 1) * rows), x)
        for s in range(2):
            part = total[:, s * nodes : (s + 1) * nodes]
            held[(r + s) * rows : (r + s + 1) * rows, :] = part + ready_ref[r + s] if starts else part
    write_modes(held, modes_ref)


def begin_sort(first, cols_ref, count_ref, tiles_ref, out_ref, live_ref, sem):
    slots, modes = cols_ref.shape
    share = out_ref.shape[1]
    place = lax.axis_index("curve")
    even = lax.rem(place, 2) == 0
    side = jnp.where(even, place + 1, place - 1)

    def begin(k, carry):
        mode = first + k
        for t in range(slots):
            block = cols_ref[t, mode]
            role = jnp.where(block == place, 0, jnp.where(block == side, 1, 2))
            pltpu.make_async_copy(tiles_ref.at[mode * slots + t], out_ref.at[role, k], sem).start()
            used = jnp.where(t < count_ref[mode], 1.0, 0.0)
            live_ref[role, k] = jnp.full(live_ref.shape[2:], used, jnp.float32).astype(jnp.bfloat16)
        return carry

    lax.fori_loop(0, share, begin, 0)
    return pltpu.make_async_copy(out_ref, out_ref, sem)


def sort_kernel(sort, *refs):
    sort(*refs).wait()


def tile_product(tiles_ref, live_ref, k, roles, values):
    kept = []
    for role, value in zip(roles, values):
        live = live_ref[role, k]
        kept.append(value * jnp.concatenate([live] * (value.shape[0] // live.shape[0]), axis=0))
    return lax.dot_general(
        jnp.concatenate(kept, axis=1),
        jnp.concatenate([tiles_ref[role, k] for role in roles], axis=1),
        (((1,), (1,)), ((), ())),
        preferred_element_type=jnp.float32,
    )


def combined(product):
    rhs, block = product.shape[0] // 2, product.shape[1] // 2
    real = product[:rhs, :block] - product[rhs:, block:]
    imag = product[rhs:, :block] + product[:rhs, block:]
    return real, imag


def put(out_ref, k, both, real, imag):
    out_ref[k * both : k * both + both // 2, :] = real
    out_ref[k * both + both // 2 : (k + 1) * both, :] = imag


def inner_kernel(chunks, shares, *refs):
    live_refs, tile_refs, refs = refs[:shares], refs[shares : 2 * shares], refs[2 * shares :]
    own_refs, side_ref, part_refs = refs[:chunks], refs[chunks], refs[chunks + 1 :]
    modes, both = side_ref.shape[:2]
    for k in range(modes):
        turn, at = divmod(k, modes // shares)
        owns = jnp.concatenate([ref[k] for ref in own_refs], axis=0)
        product = tile_product(tile_refs[turn], live_refs[turn], at, (0,), [owns])
        side = tile_product(tile_refs[turn], live_refs[turn], at, (1,), [side_ref[k]])
        for index, part_ref in enumerate(part_refs):
            mine = product[index * both : (index + 1) * both]
            put(part_ref, k, both, *combined(mine + side if index == 0 else mine))


def outer_kernel(roles, shares, *refs):
    live_refs, tile_refs, refs = refs[:shares], refs[shares : 2 * shares], refs[2 * shares :]
    value_refs, (part_ref, near_ref, held) = refs[:-3], refs[-3:]
    modes, both = value_refs[0].shape[:2]
    rhs = both // 2
    for k in range(modes):
        turn, at = divmod(k, modes // shares)
        values = [ref[k] for ref in value_refs]
        real, imag = combined(tile_product(tile_refs[turn], live_refs[turn], at, roles, values))
        at_real, at_imag = slice(k * both, k * both + rhs), slice(k * both + rhs, (k + 1) * both)
        held[at_real, :] = real + part_ref[at_real, :]
        held[at_imag, :] = imag + part_ref[at_imag, :]
    for r in range(rhs):
        for part in range(2):
            rows = slice(part * modes, (part + 1) * modes)
            near_ref[r, rows, :] = held[pl.ds(part * rhs + r, modes, stride=both), :].astype(jnp.bfloat16)


def back_product(table_ref, near_refs, terms, r):
    rows = near_refs[0].shape[1]
    total = None
    for j, ref in zip(terms, near_refs):
        x = jnp.concatenate([ref[r], ref[r + 1]], axis=1)
        for way in range(2):
            product = jnp.dot(
                table_ref[way, :, j * rows : (j + 1) * rows], x, preferred_element_type=jnp.float32
            )
            total = product if total is None else total + product
    return total


def lead_kernel(counts, table_ref, *refs):
    near_refs, out_refs = refs[: -len(counts)], refs[-len(counts) :]
    for count, out_ref in zip(counts, out_refs):
        for r in range(0, near_refs[0].shape[0], 2):
            out_ref[r // 2] = back_product(table_ref, near_refs[:count], range(count), r)
        near_refs = near_refs[count:]


def back_kernel(sources, chunk, starts, table_ref, fields_ref, impedance_ref, *refs):
    given, (out_ref, held, sem) = refs[:sources], refs[-3:]
    per, rows, nodes = given[0].shape
    rhs = fields_ref.shape[0] // rows
    local = rows // 2
    z_real, z_imag = impedance_ref[:local], impedance_ref[local:]
    for r in range(0, per, 2):
        total = back_product(table_ref, given, range(starts, starts + sources), r)
        if starts:
            total += refs[sources][r // 2]
        for s in range(2):
            real, imag = total[:local, s * nodes : (s + 1) * nodes], total[local:, s * nodes : (s + 1) * nodes]
            from_row = chunk * per + r + s
            f_real = fields_ref[pl.ds(from_row, local, stride=rhs), :]
            f_imag = fields_ref[pl.ds(local * rhs + from_row, local, stride=rhs), :]
            held[pl.ds(r + s, local, stride=per), :] = f_real + z_real * real - z_imag * imag
            held[pl.ds(local * per + r + s, local, stride=per), :] = f_imag + z_real * imag + z_imag * real
    copy = pltpu.make_async_copy(
        held.reshape(rows, per, nodes), out_ref.at[:, pl.ds(chunk * per, per), :], sem
    )
    copy.start()
    copy.wait()


PEER = [(i, i ^ 1) for i in range(4)]
ACROSS = [(i, i ^ 2) for i in range(4)]


def after(x, *earlier):
    return lax.optimization_barrier((x,) + earlier)[0]


def cost(flops, moved):
    return pl.CostEstimate(flops=flops, bytes_accessed=moved, transcendentals=0)


def on_device(parts, ring, fields, impedance, tile_data, tile_cols, tile_count):
    _, local, rhs, nodes = fields.shape
    per = rhs // CHUNKS
    slots, block = tile_data.shape[2], tile_data.shape[-1]
    rows = 2 * local
    paired = parts == 4
    order = (lambda a, j: a ^ j) if paired else (lambda a, j: j)
    tables = jnp.asarray(
        np.stack([dft_tables(parts, local, order, False), dft_tables(parts, local, order, True)], axis=1)
    )
    table_shape = jax.ShapeDtypeStruct(tables.shape[2:], jnp.bfloat16)
    flat_fields = fields.reshape(rows * rhs, nodes)
    cut_fields = fields.reshape(rows, rhs, nodes)
    flat_impedance = impedance.reshape(rows, nodes)
    flat_tiles = tile_data.reshape(local * slots, 2 * block, block)
    share = local // SHARES
    sort_shapes = [
        jax.ShapeDtypeStruct((slots, share, 2 * block, block), tile_data.dtype),
        jax.ShapeDtypeStruct((slots, share, 2 * per, nodes), jnp.bfloat16),
    ]
    params = pltpu.CompilerParams(vmem_limit_bytes=VMEM_LIMIT)
    pack_params = pltpu.CompilerParams(vmem_limit_bytes=PACK_VMEM_LIMIT)
    stage_params = pltpu.CompilerParams(vmem_limit_bytes=STAGE_VMEM_LIMIT)
    vmem, smem = pl.BlockSpec(memory_space=pltpu.VMEM), pl.BlockSpec(memory_space=pltpu.SMEM)
    hbm = pl.BlockSpec(memory_space=pltpu.HBM)
    move = 16 * fields.size
    multiply = 4 * rows * rows * parts * per * nodes
    chunk_shape = jax.ShapeDtypeStruct((per, rows, nodes), jnp.int16)

    first, coded = pl.pallas_call(
        functools.partial(pack_kernel, CHUNKS),
        out_shape=[chunk_shape, jax.ShapeDtypeStruct((rhs, rows, nodes), jnp.int16)],
        in_specs=[hbm],
        out_specs=[vmem] * 2,
        scratch_shapes=[
            pltpu.VMEM((CHUNKS, rows * per, nodes), jnp.float32),
            pltpu.SemaphoreType.DMA((CHUNKS,)),
        ],
        cost_estimate=cost(0, move),
        compiler_params=pack_params,
        name="pack",
    )(cut_fields)

    peer = lax.ppermute(coded, "az", PEER) if paired else None
    pattern = (tile_cols[:, 0, :].T, tile_count.reshape(local))

    def sorting(turn, wait_for):
        return pl.pallas_call(
            functools.partial(sort_kernel, functools.partial(begin_sort, turn * share)),
            out_shape=sort_shapes,
            in_specs=[smem] * 2 + [hbm],
            out_specs=[vmem] * 2,
            scratch_shapes=[pltpu.SemaphoreType.DMA],
            cost_estimate=cost(0, 2 * tile_data.size // SHARES),
            compiler_params=stage_params,
            name="sort",
        )(*pattern, after(flat_tiles, wait_for))

    if paired:
        forward_table, back_table, lead_part, near_part, far_part, head, live = pl.pallas_call(
            functools.partial(split_kernel, per, functools.partial(begin_sort, 0)),
            out_shape=[table_shape] * 2
            + [jax.ShapeDtypeStruct((per, rows, nodes), jnp.float32)] * 2
            + [chunk_shape]
            + sort_shapes,
            in_specs=[vmem] * 2 + [smem] * 2 + [hbm] * 2,
            out_specs=[vmem] * 7,
            scratch_shapes=[pltpu.SemaphoreType.DMA, pltpu.SemaphoreType.DMA((2,))],
            cost_estimate=cost(3 * multiply, move),
            compiler_params=stage_params,
            name="split",
        )(coded, peer, *pattern, flat_tiles, tables)
    else:
        head, live = sorting(0, coded)
        forward_table, back_table = pl.pallas_call(
            table_kernel,
            out_shape=[table_shape] * 2,
            in_specs=[hbm],
            out_specs=[vmem] * 2,
            scratch_shapes=[pltpu.SemaphoreType.DMA((2,))],
            compiler_params=params,
            name="table",
        )(tables)
    tiles, lives = [head], [live]

    sides = [(i, i ^ 1) for i in range(ring)]
    onward = [(i, (i + 2 if i % 2 == 0 else i - 2) % ring) for i in range(ring)]
    modes_shape = jax.ShapeDtypeStruct((local, 2 * per, nodes), jnp.bfloat16)
    held_modes = pltpu.VMEM((per * rows, nodes), jnp.float32)
    owns, earlier = [], None
    for index in range(CHUNKS):
        if paired and index:
            across = after(lax.ppermute(after(far_part, earlier), "az", ACROSS), tiles[-1])
            own = pl.pallas_call(
                finish_kernel,
                out_shape=modes_shape,
                in_specs=[vmem] * 2,
                out_specs=vmem,
                scratch_shapes=[held_modes],
                cost_estimate=cost(0, move // 2),
                compiler_params=params,
                name="finish",
            )(near_part, across)
        else:
            if paired:
                across = after(lax.ppermute(first, "az", ACROSS), far_part)
                earlier = across
                starts, sources = 2, [lead_part, across, lax.ppermute(across, "az", PEER)]
            else:
                every = lax.all_gather(coded[index * per : (index + 1) * per], "az")
                starts, sources = 0, [every[j] for j in range(parts)]
            own = pl.pallas_call(
                functools.partial(forward_kernel, starts),
                out_shape=modes_shape,
                in_specs=[vmem] * (1 + len(sources)),
                out_specs=vmem,
                scratch_shapes=[held_modes],
                cost_estimate=cost(3 * multiply, move),
                compiler_params=params,
                name="forward",
            )(forward_table, *sources)
        owns.append(own)
        if index == 0:
            for turn in range(1, SHARES):
                tail, live = sorting(turn, own)
                tiles.append(tail)
                lives.append(live)

    side_in = [lax.ppermute(own, "curve", sides) for own in owns]
    side_in[0] = after(side_in[0], *owns[1:])
    part_shape = jax.ShapeDtypeStruct((local * 2 * per, nodes), jnp.float32)
    parts_of = pl.pallas_call(
        functools.partial(inner_kernel, CHUNKS, SHARES),
        out_shape=[part_shape] * CHUNKS,
        in_specs=[vmem] * (2 * SHARES + CHUNKS + 1),
        out_specs=[vmem] * CHUNKS,
        cost_estimate=cost(0, tile_data.size),
        compiler_params=params,
        name="inner",
    )(*lives, *tiles, *owns, side_in[0])

    side_in[1:] = [after(side, *parts_of) for side in side_in[1:]]
    far_in = [lax.ppermute(side, "curve", onward) for side in side_in]
    nears = []
    for index in range(CHUNKS):
        if index == 0:
            roles, values = (2,), [after(far_in[0], parts_of[0], *side_in[1:])]
        else:
            roles, values = (1, 2), [side_in[index], after(far_in[index], nears[0])]
        nears.append(
            pl.pallas_call(
                functools.partial(outer_kernel, roles, SHARES),
                out_shape=jax.ShapeDtypeStruct((per, rows, nodes), jnp.bfloat16),
                in_specs=[vmem] * (2 * SHARES + len(roles) + 1),
                out_specs=vmem,
                scratch_shapes=[pltpu.VMEM((local * 2 * per, nodes), jnp.float32)],
                cost_estimate=cost(0, tile_data.size // 2),
                compiler_params=params,
                name="outer",
            )(*lives, *tiles, *values, parts_of[index])
        )

    if paired:
        peers = [lax.ppermute(near, "az", PEER) for near in nears]
        across = [lax.ppermute(near, "az", ACROSS) for near in nears]
        counts = [2] * (CHUNKS - 1) + [1]
        led = [x for near, peer_near, count in zip(nears, peers, counts) for x in (near, peer_near)[:count]]
        ready = pl.pallas_call(
            functools.partial(lead_kernel, counts),
            out_shape=[jax.ShapeDtypeStruct((per // 2, rows, 2 * nodes), jnp.float32)] * CHUNKS,
            in_specs=[vmem] * (1 + len(led)),
            out_specs=[vmem] * CHUNKS,
            cost_estimate=cost(2 * multiply, move),
            compiler_params=params,
            name="lead",
        )(back_table, *led)
        across[:-1] = [after(x, nears[-1]) for x in across[:-1]]
        across[-1] = after(across[-1], *ready)
        crossed = [lax.ppermute(x, "az", PEER) for x in across]
        crossed[:-1] = [after(x, across[-1]) for x in crossed[:-1]]
    out = None
    for index, near in enumerate(nears):
        starts = 0
        if paired:
            starts = counts[index]
            given = [near, peers[index], across[index], crossed[index]][starts:] + [ready[index]]
        else:
            every = lax.all_gather(near, "az")
            given = [every[j] for j in range(parts)]
        operands = [back_table, flat_fields, flat_impedance] + given + ([] if out is None else [out])
        out = pl.pallas_call(
            functools.partial(back_kernel, parts - starts, index, starts),
            out_shape=jax.ShapeDtypeStruct((rows, rhs, nodes), jnp.float32),
            in_specs=[vmem] * (len(operands) - (out is not None)) + [hbm] * (out is not None),
            out_specs=hbm,
            scratch_shapes=[pltpu.VMEM((rows * per, nodes), jnp.float32), pltpu.SemaphoreType.DMA],
            input_output_aliases={} if out is None else {len(operands) - 1: 0},
            cost_estimate=cost(2 * multiply, move),
            compiler_params=params,
            name="back",
        )(*operands)
    return out.reshape(fields.shape)


def solution(mesh):
    placed = (
        P(None, "az", None, "curve"),
        P(None, "az", "curve"),
        P("az", "curve", None, None, None, None),
        P("az", "curve", None),
        P("az", "curve"),
    )
    return jax.shard_map(
        functools.partial(on_device, mesh.shape["az"], mesh.shape["curve"]),
        mesh=mesh,
        in_specs=placed,
        out_specs=P(None, "az", None, "curve"),
        check_vma=False,
    )
```
